128 devices in a mesh: expert: 16 (over z, y), tensor: 8 (over x, core).
Axes of the slice: x: 4, y: 4, z: 4, core: 2. Of those that a mesh axis runs over, the one named last changes fastest.
Arguments:
- tokens: bfloat16 [6144, 2048], P('expert'), may hold values from -6 to 6
- out_grad: bfloat16 [6144, 2048], P('expert'), may hold values from -6 to 6
- routes: int32 [6144, 6], P('expert'), may hold values from 0 to 63, all different within a row; in each aligned block of 384 rows (0 to 383, 384 to 767, ...) at most 48 rows name the same one
- segment: int32 [6144], replicated, may hold values from 0 to 2, as said below
- norm_gain: float32 [2048], replicated, may hold values from 0.5 to 1.5
- q_weight: bfloat16 [2048, 3072], P(None, 'tensor'), may hold values from -0.125 to 0.125
- kv_down: bfloat16 [2048, 576], replicated, may hold values from -0.125 to 0.125
- kv_gain: float32 [512], replicated, may hold values from 0.5 to 1.5
- kv_up: bfloat16 [512, 4096], P(None, 'tensor'), may hold values from -0.25 to 0.25
- out_weight: bfloat16 [2048, 2048], P('tensor'), may hold values from -1.5 to 1.5
- mix_gain: float32 [2048], replicated, may hold values from 0.5 to 1.5
- router: bfloat16 [2048, 64], replicated, may hold values from -0.0625 to 0.0625
- shared_gate: bfloat16 [2048, 2816], P(None, 'tensor'), may hold values from -0.125 to 0.125
- shared_up: bfloat16 [2048, 2816], P(None, 'tensor'), may hold values from -0.125 to 0.125
- shared_down: bfloat16 [2816, 2048], P('tensor'), may hold values from -0.15625 to 0.15625
- expert_gate: bfloat16 [64, 2048, 1408], P('expert', None, 'tensor'), may hold values from -0.125 to 0.125
- expert_up: bfloat16 [64, 2048, 1408], P('expert', None, 'tensor'), may hold values from -0.125 to 0.125
- expert_down: bfloat16 [64, 1408, 2048], P('expert', 'tensor'), may hold values from -6 to 6
- step_size: float32 [1], replicated, may hold values from 0.0001 to 0.001
- threshold: float32 [1], replicated, may hold values from 0.5 to 2
Outputs:
- layer_out: bfloat16 [6144, 2048], P('expert')
- tokens_grad: float32 [6144, 2048], P('expert')
- q_weight_grad: float32 [2048, 3072], P('expert', 'tensor')
- kv_down_grad: float32 [2048, 576], P('expert')
- kv_up_grad: float32 [512, 4096], P('expert', 'tensor')
- out_weight_grad: float32 [2048, 2048], P('tensor', 'expert')
- router_grad: float32 [2048, 64], P('expert')
- norm_gain_grad: float32 [2048], P('expert')
- kv_gain_grad: float32 [512], P('expert')
- mix_gain_grad: float32 [2048], P('expert')
- shared_gate_grad: float32 [2048, 2816], P('expert', 'tensor')
- shared_up_grad: float32 [2048, 2816], P('expert', 'tensor')
- shared_down_grad: float32 [2816, 2048], P('tensor', 'expert')
- expert_gate_grad: float32 [64, 2048, 1408], P('expert', None, 'tensor')
- expert_up_grad: float32 [64, 2048, 1408], P('expert', None, 'tensor')
- expert_down_grad: float32 [64, 1408, 2048], P('expert', 'tensor')
- q_weight_new: float32 [2048, 3072], P('expert', 'tensor')
- kv_up_new: float32 [512, 4096], P('expert', 'tensor')
The draws below stay inside these ranges and needn't reach their ends.
Inputs may be any that keep to these rules, and one draw needn't show every extreme that they name: `routes`: each row names 6 different experts. In the rows of one index of the expert axis (384 aligned rows) no expert is named by more than 48 rows, a bound that some block reaches. In each group continuations 1 to 2 come first in order, each 128 tokens or more, 512 tokens together; the last 1024 tokens have segment 0.
All inputs are finite; a program needn't handle non-finite values.
Results may differ from the reference program's by a relative error of at most 0.019.
Values may be sent and summed in bfloat16 or wider, within the bound.
No kernel may reach another device: no remote copies, remote signals or barrier semaphores. Data moves between devices by JAX's collectives and lax.ppermute only.
A program may use at most 384 MiB of HBM per device.

```python
import math
import jax
import jax.numpy as jnp
import numpy as np
from jax import lax

D = 2048
HEADS = 16
NOPE = 128
ROPE = 64
VDIM = 128
KVRANK = 512
FF = 1408
SHARED_FF = 2816
TOPK = 6
PROMPT = 1024
CLEN = 256
CONT = 2
EXPERTS = 64
GROUP = 1536
ROWS = 384
GROUPS = 4
TOKENS = 6144
CAP = 48
N_EXPERT = 16


def draw_segment(key, part):
    key = jax.random.fold_in(key, 7)
    shifts = jax.random.randint(key, (GROUPS, CONT // 2), -(CLEN // 2), CLEN // 2 + 1)
    lengths = jnp.stack([CLEN + shifts, CLEN - shifts], axis=-1).reshape(GROUPS, CONT)
    starts = jnp.cumsum(lengths, axis=1) - lengths
    position = jnp.arange(GROUP, dtype=jnp.int32)
    member = jnp.sum((position[None, :, None] >= starts[:, None, :]).astype(jnp.int32), axis=2)
    member = jnp.where(position[None, :] >= CONT * CLEN, 0, member)
    return member.reshape(TOKENS).astype(jnp.int32)


def steps_of(own_key, shape, split, low, high):
    def one(axis_at, blocks):
        heights = jax.random.uniform(jax.random.fold_in(jax.random.fold_in(own_key, 6), axis_at), (blocks,), jnp.float32, low / len(split), high / len(split))
        return jnp.repeat(jnp.exp(heights), shape[axis_at] // blocks).reshape((-1,) + (1,) * (len(shape) - axis_at - 1))

    gain = one(*split[0])
    for cut in split[1:]:
        gain = gain * one(*cut)
    return gain


def shared_out(stream_key, own, number, rows, number_of, top, bound, skew):
    sequence = jax.random.permutation(stream_key, number_of)
    packed, common = portions_of(number_of, rows * top, bound, skew, True), portions_of(number_of, rows * top, bound, skew, False)
    places = jnp.arange(number_of)

    def named(tallies, offset_by):
        used = int((tallies > 0).sum())
        fixed = max(1, used // 4)
        passed = fixed + (places - fixed + offset_by * (used - fixed)) % max(1, number_of - fixed)
        return jnp.zeros((number_of,), jnp.int32).at[sequence[jnp.where(places < fixed, places, passed)]].set(jnp.asarray(tallies, jnp.int32))

    tallies = jnp.where(number % 4 == 0, named(packed, number // 4), named(common, number - number // 4 - 1))
    mixed = jax.random.permutation(jax.random.fold_in(own, 3), number_of)
    source_of, receiver = mixed[0:number_of // 2 * 2:2], mixed[1:number_of // 2 * 2:2]
    room = jnp.minimum(tallies[source_of] - 1, bound - tallies[receiver]) // 2
    room = jnp.where((source_of == sequence[0]) | (receiver == sequence[0]) | (tallies[receiver] == 0), 0, jnp.maximum(room, 0))
    passed = jax.random.randint(jax.random.fold_in(own, 4), (number_of // 2,), 0, 1 << 20) % (room + 1)
    tallies = tallies.at[source_of].add(-passed).at[receiver].add(passed)
    labels = jnp.searchsorted(jnp.cumsum(tallies), jnp.arange(rows * top), side="right").astype(jnp.int32)
    table = labels.reshape(top, rows).T
    table = table[jax.random.permutation(jax.random.fold_in(own, 1), rows)]
    offset_by = jax.random.randint(jax.random.fold_in(own, 2), (rows, 1), 0, top)
    return jnp.take_along_axis(table, (jnp.arange(top)[None, :] + offset_by) % top, axis=1)


def portions_of(number_of, total, limit, skew, full):
    weights = [(1 << 20) // math.isqrt(standing ** skew) + 1 for standing in range(1, number_of + 1)]
    largest = limit if full else min(limit, max(-(-total // number_of), total * weights[0] // sum(weights)))
    least = 1 if total - largest >= number_of - 1 else 0
    counts, surplus = [largest] + [least] * (number_of - 1), total - largest - least * (number_of - 1)
    while surplus > 0:
        candidates = [i for i in range(1, number_of) if counts[i] < largest] or [i for i in range(1, number_of) if counts[i] < limit]
        whole, left = sum([weights[i] for i in candidates]), surplus
        for i in candidates:
            extra = min(limit - counts[i], max(1, left * weights[i] // whole), surplus)
            counts[i] = counts[i] + extra
            surplus = surplus - extra
    return np.array(counts)


def noise(own_key, dims, scale, most, cuts=(), held_as=jnp.bfloat16):
    entries = jax.random.normal(own_key, dims, jnp.float32) * scale
    if len(cuts) > 0:
        entries = steps_of(own_key, dims, cuts, -0.22, 0.18) * entries
    return jnp.clip(entries, min=-most, max=most).astype(held_as)


def setup_inputs(seed: int = 0) -> dict:
    key_list = jax.random.split(jax.random.key(seed), 21)
    tokens = noise(key_list[0], (TOKENS, D), 1.0, 6.0, ((0, 16),))
    out_grad = noise(key_list[1], (TOKENS, D), 1.0, 6.0, ((0, 16),))
    routes_keys = jax.random.split(jax.random.fold_in(key_list[2], 1), TOKENS // ROWS)
    routes_turns = jax.random.permutation(jax.random.fold_in(key_list[2], 3), TOKENS // ROWS)
    routes = jax.vmap(lambda own, number: shared_out(jax.random.fold_in(key_list[2], 2), own, number, ROWS, EXPERTS, TOPK, CAP, 1))(routes_keys, routes_turns).reshape((TOKENS, TOPK))
    segment = draw_segment(jax.random.fold_in(key_list[20], 71), 0)
    norm_gain = jnp.clip(1.0 + 0.1 * jax.random.normal(key_list[4], (D,), jnp.float32), 0.5, 1.5)
    q_weight = noise(key_list[5], (D, HEADS * (NOPE + ROPE)), D ** -0.5, 0.125, ((1, 8),))
    kv_down = noise(key_list[6], (D, KVRANK + ROPE), D ** -0.5, 0.125)
    kv_gain = jnp.clip(1.0 + 0.1 * jax.random.normal(key_list[7], (KVRANK,), jnp.float32), 0.5, 1.5)
    kv_up = noise(key_list[8], (KVRANK, HEADS * (NOPE + VDIM)), KVRANK ** -0.5, 0.25, ((1, 8),))
    out_weight = noise(key_list[9], (HEADS * VDIM, D), (HEADS * VDIM // 128) ** -0.5, 1.5, ((0, 8),))
    mix_gain = jnp.clip(1.0 + 0.1 * jax.random.normal(key_list[10], (D,), jnp.float32), 0.5, 1.5)
    router = noise(key_list[11], (D, EXPERTS), (4 * D) ** -0.5, 0.0625)
    shared_gate = noise(key_list[12], (D, SHARED_FF), D ** -0.5, 0.125, ((1, 8),))
    shared_up = noise(key_list[13], (D, SHARED_FF), D ** -0.5, 0.125, ((1, 8),))
    shared_down = noise(key_list[14], (SHARED_FF, D), (SHARED_FF // 2) ** -0.5, 0.15625, ((0, 8),))
    expert_gate = noise(key_list[15], (EXPERTS, D, FF), D ** -0.5, 0.125, ((0, 16), (2, 8)))
    expert_up = noise(key_list[16], (EXPERTS, D, FF), D ** -0.5, 0.125, ((0, 16), (2, 8)))
    expert_down = noise(key_list[17], (EXPERTS, FF, D), 1 ** -0.5, 6.0, ((0, 16), (1, 8)))
    step_size = jnp.clip(jnp.exp(jax.random.uniform(key_list[18], (1,), jnp.float32, math.log(0.0001), math.log(0.001))), 0.0001, 0.001)
    threshold = jnp.clip(jax.random.uniform(key_list[19], (1,), jnp.float32, 0.5, 2.0), 0.5, 2.0)
    return {"tokens": tokens, "out_grad": out_grad, "routes": routes, "segment": segment, "norm_gain": norm_gain, "q_weight": q_weight, "kv_down": kv_down, "kv_gain": kv_gain, "kv_up": kv_up, "out_weight": out_weight, "mix_gain": mix_gain, "router": router, "shared_gate": shared_gate, "shared_up": shared_up, "shared_down": shared_down, "expert_gate": expert_gate, "expert_up": expert_up, "expert_down": expert_down, "step_size": step_size, "threshold": threshold}


@jax.custom_vjp
def low(v):
    return lax.optimization_barrier(v.astype(jnp.bfloat16)).astype(jnp.float32)

@jax.custom_vjp
def low_back(v):
    return v

def low_keep(v):
    return (low(v), None)

def low_pass(kept, grad):
    return (grad,)

def back_keep(v):
    return (v, None)

def back_low(kept, grad):
    return (low(grad),)
low.defvjp(low_keep, low_pass)
low_back.defvjp(back_keep, back_low)
EPSILON = 1e-06
HIGHEST = lax.Precision.HIGHEST

def product(left, right):
    return jnp.dot(left, right, precision=HIGHEST)

def rms_norm(inputs, gain_vec):
    return inputs * lax.rsqrt(lax.optimization_barrier(jnp.mean(inputs * inputs, axis=-1, keepdims=True)) + EPSILON) * gain_vec

def rotate(inputs, cosine, sine):
    half_size = inputs.shape[-1] // 2
    first_half = inputs[..., :half_size]
    second_half = inputs[..., half_size:]
    return jnp.concatenate([first_half * cosine - second_half * sine, second_half * cosine + first_half * sine], axis=-1)

def place_index(segment_ids):
    count_all = segment_ids.shape[0]
    marking = (segment_ids[:, None] == jnp.arange(CONT + 1, dtype=jnp.int32)[None, :]).astype(jnp.int32)
    position = jnp.arange(count_all, dtype=jnp.int32)
    first_seen = lax.optimization_barrier(jnp.min(jnp.where(marking > 0, position[:, None], count_all), axis=0)).astype(jnp.int32)
    first_pos = lax.optimization_barrier(jnp.sum(marking * first_seen[None, :], axis=1))
    return (position - first_pos + jnp.where(segment_ids > 0, PROMPT, 0)).astype(jnp.int32)

def group_attention(pieces):
    query_rows, key_rows, value_rows, segment_ids = pieces
    position = jnp.arange(GROUP, dtype=jnp.int32)
    same_seq = (segment_ids[None, :] == segment_ids[:, None]) & (position[None, :] <= position[:, None])
    to_prompt = (segment_ids[None, :] == 0) & (segment_ids[:, None] > 0)
    allowed = same_seq | to_prompt
    raw_scores = jnp.einsum('ihd,jhd->hij', query_rows, key_rows, precision=HIGHEST) * (1.0 / math.sqrt(NOPE + ROPE))
    scores = jnp.where(allowed[None], low_back(raw_scores), -1e+30)
    head_peak = lax.optimization_barrier(jnp.max(scores, axis=(1, 2)))
    weights = low(jax.nn.softmax(scores, axis=-1))
    attended = jnp.einsum('hij,jhd->ihd', weights, value_rows, precision=HIGHEST)
    return (attended, head_peak)

def reference(tokens, out_grad, routes, segment, norm_gain, q_weight, kv_down, kv_gain, kv_up, out_weight, mix_gain, router, shared_gate, shared_up, shared_down, expert_gate, expert_up, expert_down, step_size, threshold):
    place = jax.vmap(place_index)(segment.reshape(GROUPS, GROUP)).reshape(TOKENS)
    half_size = ROPE // 2
    frequency = jnp.power(10000.0, -2.0 * jnp.arange(half_size, dtype=jnp.float32) / ROPE)
    angle = place.astype(jnp.float32)[:, None] * frequency[None, :]
    cosine = jnp.cos(angle)
    sine = jnp.sin(angle)
    flat_routes = routes.reshape(-1)
    most_rows = N_EXPERT * CAP

    def pick_rows(expert_id):
        return jnp.nonzero(flat_routes == expert_id, size=most_rows, fill_value=TOKENS * TOPK)[0].astype(jnp.int32)
    picked = jax.vmap(pick_rows)(jnp.arange(EXPERTS, dtype=jnp.int32))
    valid = (picked < TOKENS * TOPK).astype(jnp.float32)
    safe_pick = jnp.minimum(picked, TOKENS * TOPK - 1)
    token_lookup = (safe_pick // TOPK).astype(jnp.int32)
    column_of = (safe_pick % TOPK).astype(jnp.int32)

    def forward_pass(layer_input, first_norm_scale, query_weight, latent_down_weight, latent_norm_scale, latent_up_weight, output_weight, second_norm_scale, router_weight, common_gate_weight, common_up_weight, common_down_weight, routed_gate_weight, routed_up_weight, routed_down_weight):
        normed = low(rms_norm(layer_input, first_norm_scale))
        query_lin = low_back(product(normed, query_weight)).reshape(TOKENS, HEADS, NOPE + ROPE)
        query_rot = rotate(query_lin[..., NOPE:], cosine[:, None, :], sine[:, None, :])
        query = low(jnp.concatenate([query_lin[..., :NOPE], query_rot], axis=-1))
        latent = low(low_back(product(normed, latent_down_weight)))
        compressed = low(rms_norm(latent[:, :KVRANK], latent_norm_scale))
        kv_lin = low_back(product(compressed, latent_up_weight)).reshape(TOKENS, HEADS, NOPE + VDIM)
        key_rot = rotate(latent[:, KVRANK:], cosine, sine)
        keys = low(jnp.concatenate([kv_lin[..., :NOPE], jnp.broadcast_to(key_rot[:, None, :], (TOKENS, HEADS, ROPE))], axis=-1))
        values = low(kv_lin[..., NOPE:])
        attended, peaks = lax.map(jax.checkpoint(group_attention), (query.reshape(GROUPS, GROUP, HEADS, NOPE + ROPE), keys.reshape(GROUPS, GROUP, HEADS, NOPE + ROPE), values.reshape(GROUPS, GROUP, HEADS, VDIM), segment.reshape(GROUPS, GROUP)))
        attended_b = low_back(low(attended.reshape(TOKENS, HEADS * VDIM)))
        residual_mid = layer_input + low_back(product(attended_b, output_weight))
        mixed_in = low(rms_norm(residual_mid, second_norm_scale))
        logits = low_back(product(mixed_in, router_weight))
        gate_probs = jax.nn.softmax(logits, axis=-1)
        gates = jnp.take_along_axis(gate_probs, routes, axis=1)

        def single_expert(pieces):
            gate_w, up_w, down_w, token_ids = pieces
            rows_in = mixed_in[token_ids]
            gate_lin = low_back(product(rows_in, gate_w))
            up_lin = low_back(product(rows_in, up_w))
            act = low(jax.nn.silu(gate_lin) * up_lin)
            return low_back(product(act, down_w))
        built_params = lax.map(jax.checkpoint(single_expert), (routed_gate_weight, routed_up_weight, routed_down_weight, token_lookup))
        route_weight = gates[token_lookup, column_of] * valid
        routed = jnp.zeros((TOKENS, D), jnp.float32).at[token_lookup.reshape(-1)].add((route_weight[..., None] * built_params).reshape(-1, D))
        shared_gate_lin = low_back(product(mixed_in, common_gate_weight))
        shared_up_lin = low_back(product(mixed_in, common_up_weight))
        shared_act = low(jax.nn.silu(shared_gate_lin) * shared_up_lin)
        layer = residual_mid + routed + product(shared_act, common_down_weight)
        return (layer, lax.optimization_barrier(jnp.max(peaks, axis=0)))
    floats = [tokens.astype(jnp.float32), norm_gain.astype(jnp.float32), q_weight.astype(jnp.float32), kv_down.astype(jnp.float32), kv_gain.astype(jnp.float32), kv_up.astype(jnp.float32), out_weight.astype(jnp.float32), mix_gain.astype(jnp.float32), router.astype(jnp.float32), shared_gate.astype(jnp.float32), shared_up.astype(jnp.float32), shared_down.astype(jnp.float32), expert_gate.astype(jnp.float32), expert_up.astype(jnp.float32), expert_down.astype(jnp.float32)]
    layer, pullback, head_peak = jax.vjp(forward_pass, *floats, has_aux=True)
    grads = pullback(out_grad.astype(jnp.float32))
    factor = jnp.minimum(1.0, threshold[0] / jnp.maximum(head_peak, 1.0))
    root_factor = jnp.sqrt(factor)
    query_step = (floats[2] - step_size[0] * grads[2]).reshape(D, HEADS, NOPE + ROPE)
    q_weight_new = jnp.concatenate([query_step[..., :NOPE] * root_factor[None, :, None], query_step[..., NOPE:] * factor[None, :, None]], axis=-1).reshape(D, HEADS * (NOPE + ROPE))
    up_step = (floats[5] - step_size[0] * grads[5]).reshape(KVRANK, HEADS, NOPE + VDIM)
    kv_up_new = jnp.concatenate([up_step[..., :NOPE] * root_factor[None, :, None], up_step[..., NOPE:]], axis=-1).reshape(KVRANK, HEADS * (NOPE + VDIM))
    return (layer.astype(jnp.bfloat16), grads[0], grads[2], grads[3], grads[5], grads[6], grads[8], grads[1], grads[4], grads[7], grads[9], grads[10], grads[11], grads[12], grads[13], grads[14], q_weight_new, kv_up_new)
```

```python
import math

import jax
import jax.numpy as jnp
from jax import lax
from jax.sharding import Mesh
from jax.sharding import PartitionSpec as P

D = 2048
HALF = D // 2
NOPE = 128
ROPE = 64
VDIM = 128
KVRANK = 512
TOPK = 6
PROMPT = 1024
CONT = 2
EXPERTS = 64
CAP = 48
SPAN = 4
RING = 4
OWN = 48
EPSILON = 1e-06

BF = jnp.bfloat16
F32 = jnp.float32
EXPERT = ("z", "y")
TENSOR = ("x", "c")


def dot(left, right, contract=((1,), (0,))):
    return lax.dot_general(left, right, (contract, ((), ())), preferred_element_type=F32)


def swap(block):
    return lax.ppermute(block, "c", [(0, 1), (1, 0)])


def shift(block, axis, step):
    return lax.ppermute(block, axis, [(i, (i + step) % RING) for i in range(RING)])


def spread(block):
    return lax.all_to_all(block, EXPERT, split_axis=0, concat_axis=0, tiled=True)


def pick_index(blocks, index, axis=0):
    return lax.dynamic_index_in_dim(blocks, index, axis, keepdims=False)


def sum_ring(blocks, axis, index):
    total = pick_index(blocks, index)
    for step in (1, 2, 3):
        sent = pick_index(blocks, (index + step) % RING).astype(BF)
        total = total + shift(sent, axis, step).astype(F32)
    return total


def gather_ring(block, axis, index):
    blocks = jnp.zeros((RING,) + block.shape, block.dtype)
    blocks = lax.dynamic_update_index_in_dim(blocks, block, index, 0)
    for step in (1, 2, 3):
        blocks = lax.dynamic_update_index_in_dim(
            blocks, shift(block, axis, step), (index - step) % RING, 0
        )
    return blocks


def gather_pair(block, core):
    blocks = jnp.zeros((2,) + block.shape, block.dtype)
    blocks = lax.dynamic_update_index_in_dim(blocks, block, core, 0)
    return lax.dynamic_update_index_in_dim(blocks, swap(block), 1 - core, 0)


def sum_pair(halves, core):
    return pick_index(halves, core) + swap(pick_index(halves, 1 - core).astype(BF)).astype(F32)


def sum_rows(part, x, c):
    width = part.shape[1]
    half = sum_pair(part.reshape(2, RING * OWN, width), c)
    return sum_ring(half.reshape(RING, OWN, width), "x", x)


def gather_rows(block, x, c):
    width = block.shape[1]
    half = gather_ring(block, "x", x).reshape(RING * OWN, width)
    return gather_pair(half, c).reshape(2 * RING * OWN, width)


def split_two(value):
    high = lax.reduce_precision(value, 8, 7)
    return high.astype(BF), (value - high).astype(BF)


def norm_rows(inputs, gain_vec):
    inverse = lax.rsqrt(jnp.mean(inputs * inputs, axis=-1, keepdims=True) + EPSILON)
    return (inputs * inverse * gain_vec, inverse)


def norm_back(inputs, inverse, gain_vec, gradient):
    weighted = gradient * gain_vec
    inner = jnp.mean(weighted * inputs, axis=-1, keepdims=True)
    d_inputs = inverse * weighted - inputs * (inverse * inverse * inverse) * inner
    return (d_inputs, jnp.sum(gradient * inputs * inverse, axis=0))


def rotate(inputs, cosine, sine):
    half_size = inputs.shape[-1] // 2
    first_half = inputs[..., :half_size]
    second_half = inputs[..., half_size:]
    return jnp.concatenate(
        [first_half * cosine - second_half * sine, second_half * cosine + first_half * sine],
        axis=-1,
    )


def unrotate(gradient, cosine, sine):
    return rotate(gradient, cosine, -sine)


def place_index(segment_ids):
    count_all = segment_ids.shape[0]
    marking = (segment_ids[:, None] == jnp.arange(CONT + 1, dtype=jnp.int32)[None, :]).astype(
        jnp.int32
    )
    position = jnp.arange(count_all, dtype=jnp.int32)
    first_seen = jnp.min(jnp.where(marking > 0, position[:, None], count_all), axis=0)
    first_pos = jnp.sum(marking * first_seen[None, :], axis=1)
    return position - first_pos + jnp.where(segment_ids > 0, PROMPT, 0)


def silu_parts(linear):
    sigmoid = jax.nn.sigmoid(linear)
    return (linear * sigmoid, sigmoid * (1.0 + linear * (1.0 - sigmoid)))


def shards(
    tokens,
    out_grad,
    routes,
    segment,
    norm_gain,
    q_weight,
    kv_down,
    kv_gain,
    kv_up,
    out_weight,
    mix_gain,
    router,
    shared_gate,
    shared_up,
    shared_down,
    expert_gate,
    expert_up,
    expert_down,
    step_size,
    threshold,
):
    rows = tokens.shape[0]
    columns = expert_down.shape[1]
    x = lax.axis_index("x")
    c = lax.axis_index("c")
    y = lax.axis_index("y")
    z = lax.axis_index("z")
    j = z * RING + y
    t = x * 2 + c
    heads = q_weight.shape[1] // (NOPE + ROPE)
    group_len = rows * SPAN
    count = expert_down.shape[0] * 4
    score_scale = 1.0 / math.sqrt(NOPE + ROPE)
    own_start = c * (RING * OWN) + x * OWN

    def own_rows(array):
        return lax.dynamic_slice_in_dim(array, own_start, OWN, 0)

    routes_t = routes.T
    chosen = 4 * jnp.arange(count, dtype=jnp.int32) + x
    hot = jnp.any(routes_t[None, :, :] == chosen[:, None, None], axis=1)
    number = jnp.arange(rows, dtype=jnp.int32)
    earlier = (number[:, None] < number[None, :]).astype(BF)
    slot = dot(hot.astype(BF), earlier)
    pick = hot[:, None, :] & (slot[:, None, :] == jnp.arange(CAP, dtype=F32)[None, :, None])
    pick_b = pick.astype(BF).reshape(count * CAP, rows)

    def own_columns(array):
        axis = array.ndim - 1
        return jnp.concatenate(
            [
                lax.dynamic_slice_in_dim(array, c * HALF, HALF, axis),
                lax.dynamic_slice_in_dim(array, (1 - c) * HALF, HALF, axis),
            ],
            axis=axis,
        )

    def collect(weight):
        moved = lax.all_to_all(own_columns(weight), "x", split_axis=0, concat_axis=0, tiled=True)
        return moved.reshape(RING * columns, D)

    def dispatch(source, extra=None):
        half = lax.dynamic_slice_in_dim(source, c * HALF, HALF, 1)
        sent = dot(pick_b, half).astype(BF)
        if extra is not None:
            sent = jnp.concatenate([sent, extra], axis=1)
        width = sent.shape[1]
        arrived = spread(sent.reshape(count, CAP, width)).reshape(count * CAP, width)
        mine = arrived[:, :HALF]
        return jnp.concatenate([mine, swap(mine)], axis=1), arrived[:, HALF:]

    down_w = collect(expert_down)
    grad_rows, _ = dispatch(out_grad)
    gate_w = collect(jnp.swapaxes(expert_gate, 1, 2))
    up_w = collect(jnp.swapaxes(expert_up, 1, 2))
    act_grad_raw = dot(grad_rows, down_w, ((1,), (1,)))

    group_ids = lax.dynamic_slice_in_dim(segment, z * group_len, group_len)
    key_place = place_index(group_ids)
    row_start = y * rows
    row_ids = lax.dynamic_slice_in_dim(group_ids, row_start, rows)
    half_size = ROPE // 2
    frequency = jnp.power(10000.0, -2.0 * jnp.arange(half_size, dtype=F32) / ROPE)
    key_angle = key_place.astype(F32)[:, None] * frequency[None, :]
    key_cos = jnp.cos(key_angle)
    key_sin = jnp.sin(key_angle)
    row_cos = lax.dynamic_slice_in_dim(key_cos, row_start, rows)
    row_sin = lax.dynamic_slice_in_dim(key_sin, row_start, rows)
    key_number = jnp.arange(group_len, dtype=jnp.int32)
    row_number = row_start + number
    same_seq = (group_ids[None, :] == row_ids[:, None]) & (
        key_number[None, :] <= row_number[:, None]
    )
    to_prompt = (group_ids[None, :] == 0) & (row_ids[:, None] > 0)
    allowed = same_seq | to_prompt

    x_input = tokens.astype(F32)
    normed_f, _ = norm_rows(x_input, norm_gain)
    normed = normed_f.astype(BF)
    latent = dot(normed, kv_down).astype(BF)
    half_latent = lax.dynamic_slice_in_dim(latent, c * (rows // 2), rows // 2, 0)
    gathered = gather_pair(gather_ring(half_latent, "y", y), c)
    gathered = jnp.swapaxes(gathered, 0, 1).reshape(group_len, KVRANK + ROPE)
    query_lin = dot(normed, q_weight).reshape(rows, heads, NOPE + ROPE)
    query_rot = rotate(query_lin[..., NOPE:], row_cos[:, None, :], row_sin[:, None, :])
    query_rows = jnp.concatenate([query_lin[..., :NOPE], query_rot], axis=-1).astype(BF)
    comp_norm, _ = norm_rows(gathered[:, :KVRANK].astype(F32), kv_gain)
    compressed = comp_norm.astype(BF)
    kv_lin = dot(compressed, kv_up).reshape(group_len, heads, NOPE + VDIM)
    key_rot = rotate(gathered[:, KVRANK:].astype(F32), key_cos, key_sin)
    key_rows = jnp.concatenate(
        [kv_lin[..., :NOPE], jnp.broadcast_to(key_rot[:, None, :], (group_len, heads, ROPE))],
        axis=-1,
    ).astype(BF)
    value_rows = kv_lin[..., NOPE:].astype(BF)
    scores = jnp.where(
        allowed[None],
        jnp.einsum("ihd,jhd->hij", query_rows, key_rows, preferred_element_type=F32) * score_scale,
        -1e30,
    )
    row_peak = jnp.max(scores, axis=-1, keepdims=True)
    row_total = jnp.sum(jnp.exp(scores - row_peak), axis=-1, keepdims=True)
    log_total = row_peak + jnp.log(row_total)
    head_peak = jnp.max(row_peak[..., 0], axis=1)
    probs = jnp.exp(scores - log_total)
    weights = probs.astype(BF)
    attended = jnp.einsum("hij,jhd->ihd", weights, value_rows, preferred_element_type=F32)
    attended_b = attended.reshape(rows, heads * VDIM).astype(BF)
    attn_part = dot(attended_b, out_weight)

    residual = own_rows(tokens).astype(F32) + sum_rows(attn_part, x, c)
    mixed_f, inverse_two = norm_rows(residual, mix_gain)
    mixed_own = mixed_f.astype(BF)
    mixed_in = gather_rows(mixed_own, x, c)
    logits = dot(mixed_in, router)
    gate_probs = jax.nn.softmax(logits, axis=-1)

    gate_plane = pick_index(gate_probs.reshape(rows, count, 4), x, 2).T
    slot_gate = jnp.sum(jnp.where(pick, gate_plane[:, None, :], 0.0), axis=-1)
    gate_high, gate_low = split_two(slot_gate.reshape(count * CAP, 1))
    lane = jnp.arange(128, dtype=jnp.int32)[None, :]
    gate_cols = jnp.where(lane == 0, gate_high, jnp.where(lane == 1, gate_low, 0)).astype(BF)
    mixed_rows, gate_cols = dispatch(mixed_in, gate_cols)
    gate = gate_cols[:, 0:1].astype(F32) + gate_cols[:, 1:2].astype(F32)

    gate_lin = dot(mixed_rows, gate_w, ((1,), (1,)))
    up_lin = dot(mixed_rows, up_w, ((1,), (1,)))
    gate_silu, gate_slope = silu_parts(gate_lin)
    act_f = gate_silu * up_lin
    expert_act = act_f.astype(BF)
    act_grad = gate * act_grad_raw
    gate_lin_grad = (act_grad * up_lin * gate_slope).astype(BF)
    up_lin_grad = (act_grad * gate_silu).astype(BF)
    slot_grad = jnp.sum(expert_act.astype(F32) * act_grad_raw, axis=1, keepdims=True)
    grad_high, grad_low = split_two(slot_grad)
    expert_id = 4 * j + x
    slot_cols = jnp.where(
        lane == expert_id, grad_high, jnp.where(lane == EXPERTS + expert_id, grad_low, 0)
    ).astype(BF)
    rows_grad = dot(gate_lin_grad, gate_w) + dot(up_lin_grad, up_w)

    def give_back(value, extra=None):
        half = (value[:, :HALF] + swap(value[:, HALF:].astype(BF)).astype(F32)).astype(BF)
        if extra is not None:
            half = jnp.concatenate([half, extra], axis=1)
        width = half.shape[1]
        returned = spread(half.reshape(count, CAP, width)).reshape(count * CAP, width)
        return dot(pick_b, returned, ((0,), (0,)))

    def widen(half):
        zero = jnp.zeros_like(half)
        return jnp.concatenate(
            [jnp.where(c == 0, half, zero), jnp.where(c == 0, zero, half)], axis=1
        )

    shared_gate_lin = dot(mixed_in, shared_gate)
    shared_up_lin = dot(mixed_in, shared_up)
    shared_silu, shared_slope = silu_parts(shared_gate_lin)
    shared_act = (shared_silu * shared_up_lin).astype(BF)
    shared_part = dot(shared_act, shared_down)
    shared_act_grad = dot(out_grad, shared_down, ((1,), (1,)))
    shared_gate_lin_grad = (shared_act_grad * shared_up_lin * shared_slope).astype(BF)
    shared_up_lin_grad = (shared_act_grad * shared_silu).astype(BF)
    shared_mixed_grad = dot(shared_gate_lin_grad, shared_gate, ((1,), (1,))) + dot(
        shared_up_lin_grad, shared_up, ((1,), (1,))
    )

    returned_grad = give_back(rows_grad, slot_cols)
    mixed_part = jnp.concatenate(
        [shared_mixed_grad + widen(returned_grad[:, :HALF]), returned_grad[:, HALF:]], axis=1
    )
    mixed_total = sum_rows(mixed_part, x, c)
    prob_grad = mixed_total[:, D : D + EXPERTS] + mixed_total[:, D + EXPERTS :]
    own_probs = own_rows(gate_probs)
    logit_grad = (
        own_probs * (prob_grad - jnp.sum(own_probs * prob_grad, axis=-1, keepdims=True))
    ).astype(BF)
    mixed_grad = mixed_total[:, :D] + dot(logit_grad, router, ((1,), (1,)))
    mid_norm_grad, mix_gain_grad = norm_back(residual, inverse_two, mix_gain, mixed_grad)
    mid_grad = own_rows(out_grad).astype(F32) + mid_norm_grad
    branch_own = jnp.concatenate(
        [mid_grad.astype(BF), logit_grad, jnp.zeros((OWN, 128 - EXPERTS), BF)], axis=1
    )
    branch_all = gather_rows(branch_own, x, c)
    branch_grad = branch_all[:, :D]
    logit_grad_all = branch_all[:, D : D + EXPERTS]

    attended_grad = (
        dot(branch_grad, out_weight, ((1,), (1,))).astype(BF).reshape(rows, heads, VDIM)
    )
    value_grad = jnp.einsum("hij,ihd->jhd", weights, attended_grad, preferred_element_type=F32)
    prob_att_grad = jnp.einsum(
        "ihd,jhd->hij", attended_grad, value_rows, preferred_element_type=F32
    )
    score_grad = (
        probs * (prob_att_grad - jnp.sum(probs * prob_att_grad, axis=-1, keepdims=True))
    ).astype(BF)
    key_grad = (
        jnp.einsum("hij,ihd->jhd", score_grad, query_rows, preferred_element_type=F32) * score_scale
    )
    kv_grad = (
        jnp.concatenate([key_grad[..., :NOPE], value_grad], axis=-1)
        .reshape(group_len, heads * (NOPE + VDIM))
        .astype(BF)
    )
    comp_grad = dot(kv_grad, kv_up, ((1,), (1,)))
    key_rot_grad = unrotate(jnp.sum(key_grad[..., NOPE:], axis=1), key_cos, key_sin)
    latent_part = jnp.concatenate([comp_grad, key_rot_grad], axis=-1)
    halves = jnp.swapaxes(latent_part.reshape(SPAN, 2, rows // 2, KVRANK + ROPE), 0, 1)
    latent_half = sum_ring(sum_pair(halves, c), "y", y)
    latent_total = sum_ring(latent_half.reshape(RING, OWN, KVRANK + ROPE), "x", x)

    query_grad = (
        jnp.einsum("hij,jhd->ihd", score_grad, key_rows, preferred_element_type=F32) * score_scale
    )
    query_lin_grad = jnp.concatenate(
        [
            query_grad[..., :NOPE],
            unrotate(query_grad[..., NOPE:], row_cos[:, None, :], row_sin[:, None, :]),
        ],
        axis=-1,
    )
    query_lin_grad = query_lin_grad.reshape(rows, heads * (NOPE + ROPE)).astype(BF)
    normed_total = sum_rows(dot(query_lin_grad, q_weight, ((1,), (1,))), x, c)

    own_comp = own_rows(latent)[:, :KVRANK].astype(F32)
    _, own_inverse = norm_rows(own_comp, kv_gain)
    comp_own_grad, kv_gain_grad = norm_back(
        own_comp, own_inverse, kv_gain, latent_total[:, :KVRANK]
    )
    latent_grad = jnp.concatenate([comp_own_grad, latent_total[:, KVRANK:]], axis=-1).astype(BF)
    latent_grad_all = gather_rows(latent_grad, x, c)
    normed_grad = normed_total + dot(latent_grad, kv_down, ((1,), (1,)))
    own_input = own_rows(tokens).astype(F32)
    _, inverse_one = norm_rows(own_input, norm_gain)
    input_norm_grad, norm_gain_grad = norm_back(own_input, inverse_one, norm_gain, normed_grad)
    tokens_grad = gather_rows((mid_grad + input_norm_grad).astype(BF), x, c).astype(F32)

    produced = give_back(dot(expert_act, down_w) * gate)
    layer_total = residual + sum_rows(shared_part + widen(produced), x, c)
    layer_out = gather_rows(layer_total.astype(BF), x, c)

    def hand_back(gradient):
        moved = lax.all_to_all(
            gradient.astype(BF).reshape(RING, columns, D),
            "x",
            split_axis=0,
            concat_axis=0,
            tiled=True,
        )
        return own_columns(moved).astype(F32)

    expert_gate_grad = jnp.swapaxes(hand_back(dot(gate_lin_grad, mixed_rows, ((0,), (0,)))), 1, 2)
    expert_up_grad = jnp.swapaxes(hand_back(dot(up_lin_grad, mixed_rows, ((0,), (0,)))), 1, 2)
    expert_down_grad = hand_back(
        dot((expert_act.astype(F32) * gate).astype(BF), grad_rows, ((0,), (0,)))
    )

    shared_width = shared_down.shape[0]
    shared_grads = jnp.concatenate(
        [
            dot(
                mixed_in,
                jnp.concatenate([shared_gate_lin_grad, shared_up_lin_grad], axis=1),
                ((0,), (0,)),
            ),
            dot(out_grad, shared_act, ((0,), (0,))),
        ],
        axis=1,
    ).astype(BF)
    shared_grads = lax.psum_scatter(
        shared_grads, EXPERT, scatter_dimension=0, tiled=True
    ).astype(F32)
    shared_gate_grad = shared_grads[:, :shared_width]
    shared_up_grad = shared_grads[:, shared_width : 2 * shared_width]
    shared_down_grad = shared_grads[:, 2 * shared_width :].T
    out_weight_grad = dot(branch_grad, attended_b, ((0,), (0,))).astype(BF)
    out_weight_grad = (
        lax.psum_scatter(out_weight_grad, EXPERT, scatter_dimension=0, tiled=True).astype(F32).T
    )

    q_part = dot(normed, query_lin_grad, ((0,), (0,))).astype(BF).reshape(count, 128, -1)
    up_rows = KVRANK // count
    up_part = dot(compressed, kv_grad, ((0,), (0,))).astype(BF)
    up_part = jnp.swapaxes(up_part.reshape(count, up_rows, 4, 128), 1, 2).reshape(count, 128, 128)
    big = spread(jnp.concatenate([q_part, up_part], axis=2))
    big = jnp.sum(big.astype(F32), axis=0)
    q_width = q_weight.shape[1]
    q_weight_grad = big[:, :q_width]
    kv_up_grad = jnp.swapaxes(big[:, q_width:].reshape(4, up_rows, 128), 0, 1).reshape(
        up_rows, 4 * 128
    )

    kd_width = (KVRANK + ROPE) // 8
    rt_width = EXPERTS // 8
    kd_lhs = lax.dynamic_slice_in_dim(latent_grad_all, t * kd_width, kd_width, 1)
    rt_lhs = lax.dynamic_slice_in_dim(logit_grad_all, t * rt_width, rt_width, 1)
    kd_part = dot(kd_lhs, normed, ((0,), (0,))).astype(BF)
    rt_part = dot(rt_lhs, mixed_in, ((0,), (0,))).astype(BF)

    def vector_rows(vector):
        block = vector.reshape(count, 1, vector.shape[0] // count)
        block = jnp.pad(block, ((0, 0), (0, 0), (0, 128 - block.shape[2])))
        return jnp.concatenate(split_two(block), axis=1)

    peak_one = lax.reduce_precision(head_peak, 8, 7)
    peak_two = lax.reduce_precision(head_peak - peak_one, 8, 7)
    peak_three = head_peak - peak_one - peak_two
    peak_rows = jnp.pad(
        jnp.stack([peak_one, peak_two, peak_three]), ((0, 0), (0, 128 - heads))
    ).astype(BF)
    small = jnp.concatenate(
        [
            jnp.swapaxes(jnp.concatenate([kd_part, rt_part], axis=0).reshape(-1, count, 128), 0, 1),
            vector_rows(norm_gain_grad),
            vector_rows(mix_gain_grad),
            vector_rows(kv_gain_grad),
            jnp.broadcast_to(peak_rows[None], (count, 3, 128)),
            jnp.zeros((count, 7, 128), BF),
        ],
        axis=1,
    )
    small = spread(small).astype(F32)
    wide = kd_width + rt_width
    small_sum = jnp.sum(small[:, : wide + 6], axis=0)
    peaks = small[:, wide + 6 : wide + 9, :heads]
    top_peak = jnp.max(peaks[:, 0] + peaks[:, 1] + peaks[:, 2], axis=0)
    vectors = small_sum[wide : wide + 6].reshape(3, 2, 128).sum(axis=1)
    vector_high, vector_low = split_two(vectors)
    shared_small = jnp.concatenate(
        [small_sum[:wide].astype(BF), vector_high, vector_low, jnp.zeros((10, 128), BF)], axis=0
    )
    all_small = gather_pair(gather_ring(shared_small, "x", x), c)
    all_small = jnp.swapaxes(all_small, 0, 1).reshape(8, wide + 16, 128)
    kv_down_grad = all_small[:, :kd_width].reshape(8 * kd_width, 128).T.astype(F32)
    router_grad = all_small[:, kd_width:wide].reshape(8 * rt_width, 128).T.astype(F32)
    vectors = jnp.sum(all_small[:, wide : wide + 6].astype(F32), axis=0).reshape(2, 3, 128).sum(axis=0)
    norm_gain_grad = vectors[0]
    mix_gain_grad = vectors[1]
    kv_gain_grad = vectors[2, : KVRANK // count]

    factor = jnp.minimum(1.0, threshold[0] / jnp.maximum(top_peak, 1.0))
    root_factor = jnp.sqrt(factor)
    q_rows = q_weight.shape[0] // count
    own_query = lax.dynamic_slice_in_dim(q_weight, j * q_rows, q_rows, 0).astype(F32)
    query_step = (own_query - step_size[0] * q_weight_grad).reshape(q_rows, heads, NOPE + ROPE)
    q_weight_new = jnp.concatenate(
        [
            query_step[..., :NOPE] * root_factor[None, :, None],
            query_step[..., NOPE:] * factor[None, :, None],
        ],
        axis=-1,
    ).reshape(q_rows, heads * (NOPE + ROPE))
    own_up = lax.dynamic_slice_in_dim(kv_up, j * up_rows, up_rows, 0).astype(F32)
    up_step = (own_up - step_size[0] * kv_up_grad).reshape(up_rows, heads, NOPE + VDIM)
    kv_up_new = jnp.concatenate(
        [up_step[..., :NOPE] * root_factor[None, :, None], up_step[..., NOPE:]], axis=-1
    ).reshape(up_rows, heads * (NOPE + VDIM))
    return (
        layer_out,
        tokens_grad,
        q_weight_grad,
        kv_down_grad,
        kv_up_grad,
        out_weight_grad,
        router_grad,
        norm_gain_grad,
        kv_gain_grad,
        mix_gain_grad,
        shared_gate_grad,
        shared_up_grad,
        shared_down_grad,
        expert_gate_grad,
        expert_up_grad,
        expert_down_grad,
        q_weight_new,
        kv_up_new,
    )


def solution(mesh):
    fine = Mesh(mesh.devices.reshape(4, 4, 4, 2), ("z", "y", "x", "c"))
    return jax.shard_map(
        shards,
        mesh=fine,
        in_specs=(
            P(EXPERT, None),
            P(EXPERT, None),
            P(EXPERT, None),
            P(),
            P(),
            P(None, TENSOR),
            P(),
            P(),
            P(None, TENSOR),
            P(TENSOR, None),
            P(),
            P(),
            P(None, TENSOR),
            P(None, TENSOR),
            P(TENSOR, None),
            P(EXPERT, None, TENSOR),
            P(EXPERT, None, TENSOR),
            P(EXPERT, TENSOR, None),
            P(),
            P(),
        ),
        out_specs=(
            P(EXPERT, None),
            P(EXPERT, None),
            P(EXPERT, TENSOR),
            P(EXPERT, None),
            P(EXPERT, TENSOR),
            P(TENSOR, EXPERT),
            P(EXPERT, None),
            P(EXPERT),
            P(EXPERT),
            P(EXPERT),
            P(EXPERT, TENSOR),
            P(EXPERT, TENSOR),
            P(TENSOR, EXPERT),
            P(EXPERT, None, TENSOR),
            P(EXPERT, None, TENSOR),
            P(EXPERT, TENSOR, None),
            P(EXPERT, TENSOR),
            P(EXPERT, TENSOR),
        ),
        check_vma=False,
    )
```

```python
import functools
import math

import jax
import jax.numpy as jnp
from jax import lax
from jax.experimental import pallas as pl
from jax.experimental.pallas import tpu as pltpu
from jax.sharding import Mesh
from jax.sharding import PartitionSpec as P

D = 2048
HALF = D // 2
NOPE = 128
ROPE = 64
VDIM = 128
KVRANK = 512
TOPK = 6
PROMPT = 1024
CONT = 2
EXPERTS = 64
CAP = 48
SPAN = 4
RING = 4
OWN = 48
EPSILON = 1e-06

BF = jnp.bfloat16
F32 = jnp.float32
EXPERT = ("z", "y")
TENSOR = ("x", "c")


def dot(left, right, contract=((1,), (0,))):
    return lax.dot_general(left, right, (contract, ((), ())), preferred_element_type=F32)


def swap(block):
    return lax.ppermute(block, "c", [(0, 1), (1, 0)])


def shift(block, axis, step):
    return lax.ppermute(block, axis, [(i, (i + step) % RING) for i in range(RING)])


def spread(block):
    return lax.all_to_all(block, EXPERT, split_axis=0, concat_axis=0, tiled=True)


def pick_index(blocks, index, axis=0):
    return lax.dynamic_index_in_dim(blocks, index, axis, keepdims=False)


def sum_ring(blocks, axis, index):
    return sum_sent(*ring_parts(blocks, index), axis)


def ring_parts(blocks, index):
    own = pick_index(blocks, index)
    return own, [pick_index(blocks, (index + step) % RING).astype(BF) for step in (1, 2, 3)]


def sum_sent(own, parts, axis):
    for step in (1, 2, 3):
        own = own + shift(parts[step - 1], axis, step).astype(F32)
    return own


def gather_ring(block, axis, index):
    blocks = jnp.zeros((RING,) + block.shape, block.dtype)
    blocks = lax.dynamic_update_index_in_dim(blocks, block, index, 0)
    for step in (1, 2, 3):
        blocks = lax.dynamic_update_index_in_dim(
            blocks, shift(block, axis, step), (index - step) % RING, 0
        )
    return blocks


def gather_pair(block, core):
    blocks = jnp.zeros((2,) + block.shape, block.dtype)
    blocks = lax.dynamic_update_index_in_dim(blocks, block, core, 0)
    return lax.dynamic_update_index_in_dim(blocks, swap(block), 1 - core, 0)


def gather_rows(block):
    return lax.all_gather(block, TENSOR, axis=0, tiled=True)


def after(value, *others):
    return lax.optimization_barrier((value, *others))[0]


PIECE = 176
HIDDEN = RING * PIECE
SLOTS = 16 * CAP
TILE = 256
EXTRA = 128
NT = ((1,), (1,))
TN = ((0,), (0,))
VMEM_LIMIT = 56 << 20
HINT = 64


def whole(*shape):
    return pl.BlockSpec(shape, lambda *_: (0,) * len(shape))


def anywhere():
    return pl.BlockSpec(memory_space=pl.ANY)


def copy_all(pairs, sems):
    copies = [pltpu.make_async_copy(a, b, sems.at[i]) for i, (a, b) in enumerate(pairs)]
    for one in copies:
        one.start()
    for one in copies:
        one.wait()


def cost(flops, bytes_accessed, exps=0):
    return pl.CostEstimate(
        flops=int(flops) // HINT, bytes_accessed=int(bytes_accessed) // HINT, transcendentals=0
    )


OUTWARD = (192, 336)
HOMEWARD = (112, 96, 112, 208)


def spans(parts):
    found, start = [], 0
    for part, size in enumerate(parts):
        at = start
        while at < start + size:
            weight, inside = divmod(at, PIECE)
            length = min(PIECE - inside, start + size - at)
            found.append((part, at - start, weight, inside, length))
            at += length
        start += size
    return found


def pack_kernel(x_ref, *refs):
    for step in range(3):
        for part, at, weight, inside, length in spans(OUTWARD):
            out = refs[9 + step * len(OUTWARD) + part]
            out[at : at + length, :] = refs[3 * step + weight][0, inside : inside + length, :]


def pack(x, gate, up, down):
    block = 512

    def source(step):
        return pl.BlockSpec((1, PIECE, block), lambda i, x: (lax.rem(x[0] + step, RING), 0, i))

    outs = pl.pallas_call(
        pack_kernel,
        grid_spec=pltpu.PrefetchScalarGridSpec(
            num_scalar_prefetch=1,
            grid=(D // block,),
            in_specs=[source(step) for step in (1, 2, 3) for _ in range(3)],
            out_specs=[pl.BlockSpec((size, block), lambda i, _: (0, i)) for size in OUTWARD] * 3,
        ),
        out_shape=[jax.ShapeDtypeStruct((size, D), BF) for size in OUTWARD] * 3,
        compiler_params=pltpu.CompilerParams(vmem_limit_bytes=VMEM_LIMIT),
        cost_estimate=cost(0, 13 << 20),
        name="pack_weights",
    )(x.reshape(1), *((gate, up, down) * 3))
    return [outs[part :: len(OUTWARD)] for part in range(len(OUTWARD))]


def unpack_kernel(x_ref, *refs):
    outs = refs[len(HOMEWARD) * RING :]
    for step in range(RING):
        index = lax.rem(x_ref[0] + step, RING)
        for part, at, weight, inside, length in spans(HOMEWARD):
            piece = refs[part * RING + step]
            outs[weight][index, inside : inside + length, :] = piece[at : at + length, :].astype(F32)


def unpack(x, parts):
    block = 512
    return pl.pallas_call(
        unpack_kernel,
        grid_spec=pltpu.PrefetchScalarGridSpec(
            num_scalar_prefetch=1,
            grid=(D // block,),
            in_specs=[
                pl.BlockSpec((size, block), lambda i, _: (0, i))
                for size in HOMEWARD
                for _ in range(RING)
            ],
            out_specs=[pl.BlockSpec((RING, PIECE, block), lambda i, _: (0, 0, i))] * 3,
        ),
        out_shape=[jax.ShapeDtypeStruct((RING, PIECE, D), F32)] * 3,
        compiler_params=pltpu.CompilerParams(vmem_limit_bytes=VMEM_LIMIT),
        cost_estimate=cost(0, 26 << 20),
        name="unpack_gradients",
    )(x.reshape(1), *[piece for part in parts for piece in part])


def load_weight(which, index, own_ref, parts, weight):
    pairs = [(own_ref.at[index], weight.at[pl.ds(0, PIECE)])]
    for part, at, kind, inside, length in spans(OUTWARD):
        if kind == which:
            for step, piece in enumerate(parts[part]):
                start = (step + 1) * PIECE + inside
                pairs.append((piece.at[pl.ds(at, length)], weight.at[pl.ds(start, length)]))
    return pairs


def halves_of(place_ref):
    core = place_ref[1]
    return (
        pl.ds(pl.multiple_of(core * HALF, HALF), HALF),
        pl.ds(pl.multiple_of((1 - core) * HALF, HALF), HALF),
    )


def raw_kernel(place_ref, mine_ref, other_ref, own_down, p1, p2, p3, out_ref, down, sems):
    @pl.when(pl.program_id(0) == 0)
    def _():
        copy_all(load_weight(2, place_ref[0], own_down, {1: (p1, p2, p3)}, down), sems)

    first, second = halves_of(place_ref)
    out_ref[...] = dot(mine_ref[...], down[:, first], NT) + dot(other_ref[...], down[:, second], NT)


def raw_act_grad(place, mine, other, down, packed):
    return pl.pallas_call(
        raw_kernel,
        grid_spec=pltpu.PrefetchScalarGridSpec(
            num_scalar_prefetch=1,
            grid=(SLOTS // TILE,),
            in_specs=[pl.BlockSpec((TILE, HALF), lambda i, _: (i, 0))] * 2 + [anywhere()] * 4,
            out_specs=pl.BlockSpec((TILE, HIDDEN), lambda i, _: (i, 0)),
            scratch_shapes=[pltpu.VMEM((HIDDEN, D), BF), pltpu.SemaphoreType.DMA((4,))],
        ),
        out_shape=jax.ShapeDtypeStruct((SLOTS, HIDDEN), F32),
        compiler_params=pltpu.CompilerParams(vmem_limit_bytes=VMEM_LIMIT),
        cost_estimate=cost(2 * SLOTS * D * HIDDEN, 8 << 20),
        name="raw_act_grad",
    )(place, mine, other, down, *packed[1])


def expert_kernel(
    place_ref,
    mine_ref,
    other_ref,
    raw_ref,
    own_gate,
    own_up,
    p1,
    p2,
    p3,
    q1,
    q2,
    q3,
    act_ref,
    scaled_ref,
    gate_grad_ref,
    up_grad_ref,
    keep_ref,
    give_ref,
    columns_ref,
    gate_w,
    up_w,
    sems,
):
    @pl.when(pl.program_id(0) == 0)
    def _():
        index = place_ref[0]
        parts = {0: (p1, p2, p3), 1: (q1, q2, q3)}
        copy_all(
            load_weight(0, index, own_gate, parts, gate_w)
            + load_weight(1, index, own_up, parts, up_w),
            sems,
        )

    first, second = halves_of(place_ref)
    mine, other = mine_ref[:, :HALF], other_ref[:, :HALF]
    extra = mine_ref[:, HALF:].astype(F32)
    gate = extra[:, 0:1] + extra[:, 1:2]
    gate_lin = dot(mine, gate_w[:, first], NT) + dot(other, gate_w[:, second], NT)
    up_lin = dot(mine, up_w[:, first], NT) + dot(other, up_w[:, second], NT)
    raw = raw_ref[...]
    sigmoid = jax.nn.sigmoid(gate_lin)
    silu = gate_lin * sigmoid
    act = (silu * up_lin).astype(BF)
    act_ref[...] = act
    act = act.astype(F32)
    scaled_ref[...] = (act * gate).astype(BF)
    act_grad = raw * gate
    gate_grad = (act_grad * up_lin * (sigmoid * (1.0 + gate_lin * (1.0 - sigmoid)))).astype(BF)
    up_grad = (act_grad * silu).astype(BF)
    gate_grad_ref[...] = gate_grad
    up_grad_ref[...] = up_grad
    keep_ref[...] = dot(gate_grad, gate_w[:, first]) + dot(up_grad, up_w[:, first])
    give_ref[...] = (dot(gate_grad, gate_w[:, second]) + dot(up_grad, up_w[:, second])).astype(BF)
    slot_grad = jnp.sum(act * raw, axis=1, keepdims=True)
    high = slot_grad.astype(BF).astype(F32)
    lane = lax.broadcasted_iota(jnp.int32, (TILE, EXTRA), 1)
    expert_id = place_ref[2]
    columns_ref[...] = jnp.where(
        lane == expert_id, high, jnp.where(lane == EXPERTS + expert_id, slot_grad - high, 0.0)
    ).astype(BF)


def expert_pass(place, mine, other, raw, gate, up, packed):
    rows = lambda width: pl.BlockSpec((TILE, width), lambda i, _: (i, 0))
    shape = lambda width, dtype: jax.ShapeDtypeStruct((SLOTS, width), dtype)
    return pl.pallas_call(
        expert_kernel,
        grid_spec=pltpu.PrefetchScalarGridSpec(
            num_scalar_prefetch=1,
            grid=(SLOTS // TILE,),
            in_specs=[rows(HALF + EXTRA), rows(HALF + EXTRA), rows(HIDDEN)] + [anywhere()] * 8,
            out_specs=[rows(HIDDEN)] * 4 + [rows(HALF)] * 2 + [rows(EXTRA)],
            scratch_shapes=[pltpu.VMEM((HIDDEN, D), BF)] * 2 + [pltpu.SemaphoreType.DMA((11,))],
        ),
        out_shape=[shape(HIDDEN, BF)] * 4
        + [shape(HALF, F32), shape(HALF, BF), shape(EXTRA, BF)],
        compiler_params=pltpu.CompilerParams(vmem_limit_bytes=VMEM_LIMIT),
        cost_estimate=cost(8 * SLOTS * D * HIDDEN, 24 << 20, SLOTS * HIDDEN),
        name="expert_pass",
    )(place, mine, other, raw, gate, up, *packed[0], *packed[1])


def produce_kernel(place_ref, act_ref, mine_ref, own_down, p1, p2, p3, keep_ref, give_ref, down, sems):
    @pl.when(pl.program_id(0) == 0)
    def _():
        copy_all(load_weight(2, place_ref[0], own_down, {1: (p1, p2, p3)}, down), sems)

    first, second = halves_of(place_ref)
    extra = mine_ref[...].astype(F32)
    gate = extra[:, 0:1] + extra[:, 1:2]
    keep_ref[...] = dot(act_ref[...], down[:, first]) * gate
    give_ref[...] = (dot(act_ref[...], down[:, second]) * gate).astype(BF)


def produce(place, act, mine, down, packed):
    rows = lambda width: pl.BlockSpec((TILE, width), lambda i, _: (i, 0))
    return pl.pallas_call(
        produce_kernel,
        grid_spec=pltpu.PrefetchScalarGridSpec(
            num_scalar_prefetch=1,
            grid=(SLOTS // TILE,),
            in_specs=[
                rows(HIDDEN),
                pl.BlockSpec((TILE, EXTRA), lambda i, _: (i, HALF // EXTRA)),
            ]
            + [anywhere()] * 4,
            out_specs=[rows(HALF)] * 2,
            scratch_shapes=[pltpu.VMEM((HIDDEN, D), BF), pltpu.SemaphoreType.DMA((4,))],
        ),
        out_shape=[
            jax.ShapeDtypeStruct((SLOTS, HALF), F32),
            jax.ShapeDtypeStruct((SLOTS, HALF), BF),
        ],
        compiler_params=pltpu.CompilerParams(vmem_limit_bytes=VMEM_LIMIT),
        cost_estimate=cost(2 * SLOTS * D * HIDDEN, 9 << 20),
        name="produce",
    )(place, act, mine, down, *packed[1])


def weight_grad_kernel(place_ref, *refs, weights, parts):
    lefts = refs[: len(weights)]
    rights, outs = refs[len(weights) : -len(parts) * RING], refs[-len(parts) * RING :]
    own = pl.program_id(0) < 2
    rights = [jnp.where(own, rights[i][...], rights[i + 1][...]) for i in range(0, len(rights), 2)]
    for left, weight in zip(lefts, weights):
        right = rights[1] if weight == 2 and len(rights) > 1 else rights[0]
        product = dot(left[...], right, TN).astype(BF)
        for step in range(RING):
            for part, at, kind, inside, length in spans(HOMEWARD):
                if kind == weight:
                    start = step * PIECE + inside
                    out = outs[parts.index(part) * RING + step]
                    out[at : at + length, :] = product[start : start + length, :]


def weight_grads(place, weights, parts, lefts, rights):
    block = HALF // 2
    mine = pl.BlockSpec((SLOTS, block), lambda i, _: (0, jnp.minimum(i, 1)))
    other = pl.BlockSpec((SLOTS, block), lambda i, _: (0, jnp.maximum(i - 2, 0)))
    sizes = [HOMEWARD[part] for part in parts for _ in range(RING)]
    outs = pl.pallas_call(
        functools.partial(weight_grad_kernel, weights=weights, parts=parts),
        grid_spec=pltpu.PrefetchScalarGridSpec(
            num_scalar_prefetch=1,
            grid=(4,),
            in_specs=[whole(SLOTS, HIDDEN)] * len(lefts) + [mine, other] * len(rights),
            out_specs=[
                pl.BlockSpec((size, block), lambda i, place: (0, lax.rem(2 * place[1] + i, 4)))
                for size in sizes
            ],
        ),
        out_shape=[jax.ShapeDtypeStruct((size, D), BF) for size in sizes],
        compiler_params=pltpu.CompilerParams(vmem_limit_bytes=VMEM_LIMIT),
        cost_estimate=cost(2 * len(lefts) * SLOTS * D * HIDDEN, 18 << 20),
        name="weight_grads",
    )(place, *lefts, *[half for right in rights for half in right])
    return [outs[i * RING : (i + 1) * RING] for i in range(len(parts))]


SHARED = 352
WIDE = 384
ATT = 2 * VDIM


def shared_kernel(mixed, out_grad, gate_w, up_w, down_w, part, mixed_grad, grads):
    gate_lin = dot(mixed[...], gate_w[...], NT)
    up_lin = dot(mixed[...], up_w[...], NT)
    sigmoid = jax.nn.sigmoid(gate_lin)
    silu = gate_lin * sigmoid
    act = (silu * up_lin).astype(BF)
    act_grad = dot(out_grad[...], down_w[...], NT)
    gate_grad = (act_grad * up_lin * (sigmoid * (1.0 + gate_lin * (1.0 - sigmoid)))).astype(BF)
    up_grad = (act_grad * silu).astype(BF)
    for start in range(0, D, 512):
        at = slice(start, start + 512)
        part[:, at] = dot(act, down_w[:, at])
        mixed_grad[:, at] = dot(gate_grad, gate_w[:, at]) + dot(up_grad, up_w[:, at])
        zeros = jnp.zeros((512, WIDE - SHARED), BF)
        for i, (left, right) in enumerate(((mixed, gate_grad), (mixed, up_grad), (out_grad, act))):
            start = i * WIDE
            grads[at, start : start + SHARED] = dot(left[:, at], right, TN).astype(BF)
            grads[at, start + SHARED : start + WIDE] = zeros


def shared_experts(mixed, out_grad, gate_w, up_w, down_w):
    args = (mixed, out_grad, gate_w, up_w, down_w)
    rows = mixed.shape[0]
    outs = [
        jax.ShapeDtypeStruct((rows, D), F32),
        jax.ShapeDtypeStruct((rows, D), F32),
        jax.ShapeDtypeStruct((D, 3 * WIDE), BF),
    ]
    return pl.pallas_call(
        shared_kernel,
        grid=(1,),
        in_specs=[whole(*arg.shape) for arg in args],
        out_specs=[whole(*out.shape) for out in outs],
        out_shape=outs,
        compiler_params=pltpu.CompilerParams(vmem_limit_bytes=VMEM_LIMIT),
        cost_estimate=cost(18 * rows * D * SHARED, 18 << 20, rows * SHARED),
        name="shared_experts",
    )(*args)


GROUP = 1536
ROWS = 384
LATENT = KVRANK + ROPE
HEADS = 2
HEAD = NOPE + ROPE
SCALE = 1.0 / math.sqrt(HEAD)


def turn(block, cosine, sine):
    half = ROPE // 2
    return block * cosine + jnp.concatenate([block[:, half:], block[:, :half]], axis=1) * sine


def mask_bias(seg_keys, seg_rows, row_start):
    key = lax.broadcasted_iota(jnp.int32, (GROUP, ROWS), 0)
    row = lax.broadcasted_iota(jnp.int32, (GROUP, ROWS), 1) + row_start
    same = (seg_keys == seg_rows) & (key <= row)
    return jnp.where(same | ((seg_keys == 0) & (seg_rows > 0)), 0.0, -1e30)


def wide_tables(cos, sin):
    return jnp.concatenate([cos, cos], axis=1), jnp.concatenate([-sin, sin], axis=1)


def row_tables(cos_ref, sin_ref, row_start):
    at = pl.ds(pl.multiple_of(row_start, ROWS), ROWS)
    return wide_tables(cos_ref[at, :], sin_ref[at, :])


def head_queries(query, row_cos, row_sin, head):
    start = head * HEAD
    plain = query[:, start : start + NOPE].astype(BF)
    return plain, turn(query[:, start + NOPE : start + HEAD], row_cos, row_sin).astype(BF)


def attention_kernel(
    place_ref,
    mine_ref,
    other_ref,
    query_ref,
    gain_ref,
    kv_up_ref,
    out_weight_ref,
    cos_ref,
    sin_ref,
    seg_keys_ref,
    seg_rows_ref,
    give_ref,
    keep_ref,
    attended_ref,
    compressed_ref,
    kv_ref,
    key_rot_ref,
    log_total_ref,
    peak_ref,
    latent,
    attended,
):
    core = place_ref[1]
    half = ROWS // 2
    for block in range(SPAN):
        start = pl.multiple_of(block * ROWS + core * half, half)
        latent[pl.ds(start, half), :] = mine_ref[block]
        start = pl.multiple_of(block * ROWS + (1 - core) * half, half)
        latent[pl.ds(start, half), :] = other_ref[block]
    inputs = latent[:, :KVRANK].astype(F32)
    inverse = lax.rsqrt(jnp.mean(inputs * inputs, axis=1, keepdims=True) + EPSILON)
    compressed_ref[...] = (inputs * inverse * gain_ref[...]).astype(BF)
    kv_ref[...] = dot(compressed_ref[...], kv_up_ref[...]).astype(BF)
    cosine, sine = wide_tables(cos_ref[...], sin_ref[...])
    key_rot_ref[...] = turn(latent[:, KVRANK:].astype(F32), cosine, sine).astype(BF)
    seg_rows = seg_rows_ref[:, pl.ds(pl.multiple_of(place_ref[3], ROWS), ROWS)]
    bias = mask_bias(seg_keys_ref[...], seg_rows, place_ref[3])
    row_cos, row_sin = row_tables(cos_ref, sin_ref, place_ref[3])
    for head in range(HEADS):
        plain, turned = head_queries(query_ref, row_cos, row_sin, head)
        start = head * (NOPE + VDIM)
        scores = dot(kv_ref[:, start : start + NOPE], plain, NT)
        scores = (scores + dot(key_rot_ref[...], turned, NT)) * SCALE + bias
        peak = jnp.max(scores, axis=0, keepdims=True)
        powers = jnp.exp(scores - peak)
        total = jnp.sum(powers, axis=0, keepdims=True)
        log_total_ref[head : head + 1, :] = peak + jnp.log(total)
        peak_ref[head : head + 1, :] = peak
        weights = (powers * (1.0 / total)).astype(BF)
        values = kv_ref[:, start + NOPE : start + NOPE + VDIM]
        attended[:, head * VDIM : (head + 1) * VDIM] = dot(values, weights, TN).T
    attended_ref[...] = attended[...].astype(BF)
    for block in range(RING):
        for out, which in ((give_ref, 1 - core), (keep_ref, core)):
            start = pl.multiple_of(block * 2 * OWN + which * OWN, OWN)
            out[block] = dot(
                attended[pl.ds(start, OWN), :].astype(BF), out_weight_ref[...]
            ).astype(out.dtype)


def attention(place, mine, other, query, gain, kv_up, out_weight, tables, segs):
    shape = jax.ShapeDtypeStruct
    args = (mine, other, query, gain.reshape(1, KVRANK), kv_up, out_weight, *tables, *segs)
    outs = [
        shape((RING, OWN, D), BF),
        shape((RING, OWN, D), F32),
        shape((ROWS, HEADS * VDIM), BF),
        shape((GROUP, KVRANK), BF),
        shape((GROUP, HEADS * (NOPE + VDIM)), BF),
        shape((GROUP, ROPE), BF),
        shape((HEADS, ROWS), F32),
        shape((HEADS, ROWS), F32),
    ]
    return pl.pallas_call(
        attention_kernel,
        grid_spec=pltpu.PrefetchScalarGridSpec(
            num_scalar_prefetch=1,
            grid=(1,),
            in_specs=[whole(*arg.shape) for arg in args],
            out_specs=[whole(*out.shape) for out in outs],
            scratch_shapes=[
                pltpu.VMEM((GROUP, LATENT), BF),
                pltpu.VMEM((ROWS, HEADS * VDIM), F32),
            ],
        ),
        out_shape=outs,
        compiler_params=pltpu.CompilerParams(vmem_limit_bytes=VMEM_LIMIT),
        cost_estimate=cost(3e9, 14 << 20, 2 * GROUP * ROWS),
        name="attention_forward",
    )(place, *args)


def attention_back_kernel(
    place_ref,
    mine_ref,
    other_ref,
    query_ref,
    compressed_ref,
    kv_ref,
    key_rot_ref,
    log_total_ref,
    kv_up_ref,
    out_weight_ref,
    cos_ref,
    sin_ref,
    seg_keys_ref,
    seg_rows_ref,
    give_ref,
    keep_ref,
    kv_grad_ref,
    query_grad_ref,
    branch_ref,
    comp_grad,
    rot_grad,
):
    core = place_ref[1]
    interleave(core, mine_ref, other_ref, branch_ref, D + EXTRA)
    attended_grad = dot(branch_ref[:, :D], out_weight_ref[...], NT).astype(BF)
    seg_rows = seg_rows_ref[:, pl.ds(pl.multiple_of(place_ref[3], ROWS), ROWS)]
    bias = mask_bias(seg_keys_ref[...], seg_rows, place_ref[3])
    row_cos, row_sin = row_tables(cos_ref, sin_ref, place_ref[3])
    turned_sum = 0.0
    query_grads = []
    for head in range(HEADS):
        plain, turned = head_queries(query_ref, row_cos, row_sin, head)
        start = head * (NOPE + VDIM)
        keys = kv_ref[:, start : start + NOPE]
        values = kv_ref[:, start + NOPE : start + NOPE + VDIM]
        key_rot = key_rot_ref[...]
        scores = (dot(keys, plain, NT) + dot(key_rot, turned, NT)) * SCALE + bias
        probs = jnp.exp(scores - log_total_ref[head : head + 1, :])
        grad = attended_grad[:, head * VDIM : (head + 1) * VDIM]
        value_grad = dot(probs.astype(BF), grad)
        prob_grad = dot(values, grad, NT)
        inner = jnp.sum(probs * prob_grad, axis=0, keepdims=True)
        score_grad = (probs * (prob_grad - inner)).astype(BF)
        kv_grad_ref[:, start : start + NOPE] = (dot(score_grad, plain) * SCALE).astype(BF)
        kv_grad_ref[:, start + NOPE : start + NOPE + VDIM] = value_grad.astype(BF)
        turned_sum = turned_sum + dot(score_grad, turned) * SCALE
        query_grads.append((dot(keys, score_grad, TN) * SCALE).T)
        turned_grad = (dot(key_rot, score_grad, TN) * SCALE).T
        query_grads.append(turn(turned_grad, row_cos, -row_sin))
    comp_grad[...] = dot(kv_grad_ref[...], kv_up_ref[...], NT)
    cosine, sine = wide_tables(cos_ref[...], sin_ref[...])
    rot_grad[...] = turn(turned_sum, cosine, -sine)
    for block in range(SPAN):
        for inner in range(RING):
            for out, which in ((give_ref, 1 - core), (keep_ref, core)):
                start = pl.multiple_of(block * ROWS + inner * 2 * OWN + which * OWN, OWN)
                out[block, inner, :, :KVRANK] = comp_grad[pl.ds(start, OWN), :].astype(out.dtype)
                out[block, inner, :, KVRANK:] = rot_grad[pl.ds(start, OWN), :].astype(out.dtype)
    query_grad_ref[...] = jnp.concatenate(query_grads, axis=1).astype(BF)


def attention_back(
    place, mine, other, query, compressed, kv, key_rot, log_total, kv_up, out_weight, tables, segs
):
    shape = jax.ShapeDtypeStruct
    args = (
        mine, other, query, compressed, kv, key_rot, log_total, kv_up, out_weight, *tables, *segs
    )
    outs = [
        shape((SPAN, RING, OWN, LATENT), BF),
        shape((SPAN, RING, OWN, LATENT), F32),
        shape((GROUP, HEADS * (NOPE + VDIM)), BF),
        shape((ROWS, HEADS * HEAD), BF),
        shape((ROWS, D + EXTRA), BF),
    ]
    return pl.pallas_call(
        attention_back_kernel,
        grid_spec=pltpu.PrefetchScalarGridSpec(
            num_scalar_prefetch=1,
            grid=(1,),
            in_specs=[whole(*arg.shape) for arg in args],
            out_specs=[whole(*out.shape) for out in outs],
            scratch_shapes=[pltpu.VMEM((GROUP, KVRANK), F32), pltpu.VMEM((GROUP, ROPE), F32)],
        ),
        out_shape=outs,
        compiler_params=pltpu.CompilerParams(vmem_limit_bytes=VMEM_LIMIT),
        cost_estimate=cost(4e9, 16 << 20, 2 * GROUP * ROWS),
        name="attention_backward",
    )(place, *args)


def normed_kernel(place_ref, query_grad_ref, q_weight_ref, give_ref, keep_ref):
    core = place_ref[1]
    for block in range(RING):
        for out, which in ((give_ref, 1 - core), (keep_ref, core)):
            start = pl.multiple_of(block * 2 * OWN + which * OWN, OWN)
            part = query_grad_ref[pl.ds(start, OWN), :]
            out[block] = dot(part, q_weight_ref[...], NT).astype(out.dtype)


def normed_grad_part(place, query_grad, q_weight):
    args = (query_grad, q_weight)
    outs = [
        jax.ShapeDtypeStruct((RING, OWN, D), BF),
        jax.ShapeDtypeStruct((RING, OWN, D), F32),
    ]
    return pl.pallas_call(
        normed_kernel,
        grid_spec=pltpu.PrefetchScalarGridSpec(
            num_scalar_prefetch=1,
            grid=(1,),
            in_specs=[whole(*arg.shape) for arg in args],
            out_specs=[whole(*out.shape) for out in outs],
        ),
        out_shape=outs,
        compiler_params=pltpu.CompilerParams(vmem_limit_bytes=VMEM_LIMIT),
        cost_estimate=cost(6e8, 5 << 20),
        name="normed_grad_part",
    )(place, *args)


UP_ROWS = KVRANK // 16
BIG = HEADS * HEAD + ATT + 128


def projection_grad_kernel(
    normed, branch, compressed, query_grad, attended, kv_grad, out
):
    width = HEADS * HEAD
    out[:, :width] = dot(normed[...], query_grad[...], TN).astype(BF)
    out[:, width : width + ATT] = dot(branch[...], attended[...], TN).astype(BF)
    up = dot(compressed[...], kv_grad[...], TN)
    for index in range(4):
        for part in range(4):
            start = index * 128 + part * UP_ROWS
            out[start : start + UP_ROWS, width + ATT :] = up[
                index * UP_ROWS : (index + 1) * UP_ROWS, part * 128 : (part + 1) * 128
            ].astype(BF)


def projection_grads(normed, branch, compressed, query_grad, attended, kv_grad):
    block = 512
    return pl.pallas_call(
        projection_grad_kernel,
        grid=(D // block,),
        in_specs=[
            pl.BlockSpec((ROWS, block), lambda i: (0, i)),
            pl.BlockSpec((ROWS, block), lambda i: (0, i)),
            pl.BlockSpec((GROUP, 128), lambda i: (0, i)),
            whole(ROWS, HEADS * HEAD),
            whole(ROWS, ATT),
            whole(GROUP, HEADS * (NOPE + VDIM)),
        ],
        out_specs=pl.BlockSpec((block, BIG), lambda i: (i, 0)),
        out_shape=jax.ShapeDtypeStruct((D, BIG), BF),
        compiler_params=pltpu.CompilerParams(vmem_limit_bytes=VMEM_LIMIT),
        cost_estimate=cost(2e9, 10 << 20),
        name="projection_grads",
    )(normed, branch, compressed, query_grad, attended, kv_grad)


def combine_kernel(place_ref, pick_ref, returned_ref, shared_ref, give_ref, keep_ref, total):
    core = place_ref[1]
    rows = dot(pick_ref[...], returned_ref[...], TN)
    total[:, :D] = shared_ref[...]
    mine = pl.ds(pl.multiple_of(core * HALF, HALF), HALF)
    total[:, mine] = total[:, mine] + rows[:, :HALF]
    if returned_ref.shape[1] > HALF:
        total[:, D:] = rows[:, HALF:]
    for block in range(RING):
        for out, which in ((give_ref, 1 - core), (keep_ref, core)):
            start = pl.multiple_of(block * 2 * OWN + which * OWN, OWN)
            out[block] = total[pl.ds(start, OWN), :].astype(out.dtype)


def combine_rows(place, pick, returned, shared):
    width = D + returned.shape[1] - HALF
    args = (pick, returned, shared)
    outs = [
        jax.ShapeDtypeStruct((RING, OWN, width), BF),
        jax.ShapeDtypeStruct((RING, OWN, width), F32),
    ]
    return pl.pallas_call(
        combine_kernel,
        grid_spec=pltpu.PrefetchScalarGridSpec(
            num_scalar_prefetch=1,
            grid=(1,),
            in_specs=[whole(*arg.shape) for arg in args],
            out_specs=[whole(*out.shape) for out in outs],
            scratch_shapes=[pltpu.VMEM((ROWS, width), F32)],
        ),
        out_shape=outs,
        compiler_params=pltpu.CompilerParams(vmem_limit_bytes=VMEM_LIMIT),
        cost_estimate=cost(7e8, 8 << 20),
        name="combine_rows",
    )(place, *args)


def order_kernel(x_ref, *refs):
    for step in range(RING):
        refs[RING][lax.rem(x_ref[0] + RING - step, RING)] = refs[step][...]


def order_ring(x, blocks):
    rows, width = blocks[0].shape
    return pl.pallas_call(
        order_kernel,
        grid_spec=pltpu.PrefetchScalarGridSpec(
            num_scalar_prefetch=1,
            grid=(1,),
            in_specs=[whole(rows, width)] * RING,
            out_specs=whole(RING, rows, width),
        ),
        out_shape=jax.ShapeDtypeStruct((RING, rows, width), blocks[0].dtype),
        cost_estimate=cost(0, 2 << 20),
        name="order_ring",
    )(x.reshape(1), *blocks)


def interleave(core, mine_ref, other_ref, out, width):
    for block in range(RING):
        for ref, which in ((mine_ref, core), (other_ref, 1 - core)):
            start = pl.multiple_of(block * 2 * OWN + which * OWN, OWN)
            out[pl.ds(start, OWN), :] = ref[block, :, :width]


def gating_kernel(place_ref, mine_ref, other_ref, router_ref, pick_ref, mixed_ref, probs_ref, sent_ref):
    core = place_ref[1]
    interleave(core, mine_ref, other_ref, mixed_ref, D)
    logits = dot(mixed_ref[...], router_ref[...])
    powers = jnp.exp(logits - jnp.max(logits, axis=1, keepdims=True))
    probs = powers / jnp.sum(powers, axis=1, keepdims=True)
    probs_ref[...] = probs
    pick = pick_ref[...]
    high = probs.astype(BF)
    rest = probs - high.astype(F32)
    middle = rest.astype(BF)
    low = (rest - middle.astype(F32)).astype(BF)
    gates = dot(pick, high) + dot(pick, middle) + dot(pick, low)
    slot = lax.broadcasted_iota(jnp.int32, (SLOTS, EXPERTS), 0)
    lane = lax.broadcasted_iota(jnp.int32, (SLOTS, EXPERTS), 1)
    first = (lane - place_ref[0]) * (CAP // 4)
    inside = (slot >= first) & (slot < first + CAP) & (lax.rem(lane, 4) == place_ref[0])
    gate = jnp.sum(jnp.where(inside, gates, 0.0), axis=1, keepdims=True)
    high = gate.astype(BF).astype(F32)
    lane = lax.broadcasted_iota(jnp.int32, (SLOTS, EXTRA), 1)
    sent_ref[:, HALF:] = jnp.where(
        lane == 0, high, jnp.where(lane == 1, gate - high, 0.0)
    ).astype(BF)
    mine = pl.ds(pl.multiple_of(core * HALF, HALF), HALF)
    sent_ref[:, :HALF] = dot(pick, mixed_ref[:, mine]).astype(BF)


def gating(place, mine, other, router, pick):
    args = (mine, other, router, pick)
    outs = [
        jax.ShapeDtypeStruct((ROWS, D), BF),
        jax.ShapeDtypeStruct((ROWS, EXPERTS), F32),
        jax.ShapeDtypeStruct((SLOTS, HALF + EXTRA), BF),
    ]
    return pl.pallas_call(
        gating_kernel,
        grid_spec=pltpu.PrefetchScalarGridSpec(
            num_scalar_prefetch=1,
            grid=(1,),
            in_specs=[whole(*arg.shape) for arg in args],
            out_specs=[whole(*out.shape) for out in outs],
        ),
        out_shape=outs,
        compiler_params=pltpu.CompilerParams(vmem_limit_bytes=VMEM_LIMIT),
        cost_estimate=cost(8e8, 6 << 20),
        name="gating",
    )(place, *args)


KD_COLUMNS = LATENT // 8
ROUTER_COLUMNS = EXPERTS // 8
SHARE = KD_COLUMNS + ROUTER_COLUMNS
SMALL = SHARE + 16


def small_kernel(latent, logit, normed, mixed, norm_gain, mix_gain, kv_gain, peak_ref, out):
    kv_down = dot(latent[...], normed[...], TN)
    router = dot(logit[...], mixed[...], TN)
    lane = lax.broadcasted_iota(jnp.int32, (1, 128), 1)
    peak = 0.0
    for head in range(HEADS):
        highest = jnp.max(peak_ref[head : head + 1, :], axis=1, keepdims=True)
        peak = jnp.where(lane == head, highest, peak)

    def parts(row, number):
        found = []
        for _ in range(number):
            found.append(row.astype(BF).astype(F32))
            row = row - found[-1]
        return found

    peaks = parts(peak, 3)
    zeros = jnp.zeros((7, 128), F32)
    for index in range(16):
        at = slice(index * 128, (index + 1) * 128)
        gain = kv_gain[:, index * UP_ROWS : (index + 1) * UP_ROWS]
        gain = jnp.concatenate([gain, jnp.zeros((1, 128 - UP_ROWS), F32)], axis=1)
        rows = parts(norm_gain[:, at], 2) + parts(mix_gain[:, at], 2) + parts(gain, 2)
        rows = [kv_down[:, at], router[:, at]] + rows + peaks + [zeros]
        out[index] = jnp.concatenate(rows, axis=0).astype(BF)


def small_grads(latent, logit, normed, mixed, norm_gain, mix_gain, kv_gain, peak):
    args = (
        latent,
        logit,
        normed,
        mixed,
        norm_gain.reshape(1, D),
        mix_gain.reshape(1, D),
        kv_gain.reshape(1, KVRANK),
        peak,
    )
    return pl.pallas_call(
        small_kernel,
        grid=(1,),
        in_specs=[whole(*arg.shape) for arg in args],
        out_specs=whole(16, SMALL, 128),
        out_shape=jax.ShapeDtypeStruct((16, SMALL, 128), BF),
        compiler_params=pltpu.CompilerParams(vmem_limit_bytes=VMEM_LIMIT),
        cost_estimate=cost(2e8, 4 << 20),
        name="small_grads",
    )(*args)


def split_two(value):
    high = lax.reduce_precision(value, 8, 7)
    return high.astype(BF), (value - high).astype(BF)


def norm_rows(inputs, gain_vec):
    inverse = lax.rsqrt(jnp.mean(inputs * inputs, axis=-1, keepdims=True) + EPSILON)
    return (inputs * inverse * gain_vec, inverse)


def norm_back(inputs, inverse, gain_vec, gradient):
    weighted = gradient * gain_vec
    inner = jnp.mean(weighted * inputs, axis=-1, keepdims=True)
    d_inputs = inverse * weighted - inputs * (inverse * inverse * inverse) * inner
    return (d_inputs, jnp.sum(gradient * inputs * inverse, axis=0))


def rotate(inputs, cosine, sine):
    half_size = inputs.shape[-1] // 2
    first_half = inputs[..., :half_size]
    second_half = inputs[..., half_size:]
    return jnp.concatenate(
        [first_half * cosine - second_half * sine, second_half * cosine + first_half * sine],
        axis=-1,
    )


def unrotate(gradient, cosine, sine):
    return rotate(gradient, cosine, -sine)


def shards(
    tokens,
    out_grad,
    routes,
    segment,
    norm_gain,
    q_weight,
    kv_down,
    kv_gain,
    kv_up,
    out_weight,
    mix_gain,
    router,
    shared_gate,
    shared_up,
    shared_down,
    expert_gate,
    expert_up,
    expert_down,
    step_size,
    threshold,
):
    rows = tokens.shape[0]
    x = lax.axis_index("x")
    c = lax.axis_index("c")
    y = lax.axis_index("y")
    z = lax.axis_index("z")
    j = z * RING + y
    t = x * 2 + c
    heads = q_weight.shape[1] // (NOPE + ROPE)
    group_len = rows * SPAN
    count = expert_down.shape[0] * 4
    score_scale = 1.0 / math.sqrt(NOPE + ROPE)
    own_start = t * OWN

    def gather_few(block):
        ring = gather_ring(block, "x", x)
        return jnp.swapaxes(gather_pair(ring, c), 0, 1).reshape(-1, block.shape[1])

    def own_rows(array):
        return lax.dynamic_slice_in_dim(array, own_start, OWN, 0)

    routes_t = routes.T
    chosen = 4 * jnp.arange(count, dtype=jnp.int32) + x
    hot = jnp.any(routes_t[None, :, :] == chosen[:, None, None], axis=1)
    number = jnp.arange(rows, dtype=jnp.int32)
    earlier = (number[:, None] < number[None, :]).astype(BF)
    slot = dot(hot.astype(BF), earlier)
    pick = hot[:, None, :] & (slot[:, None, :] == jnp.arange(CAP, dtype=F32)[None, :, None])
    pick_b = pick.astype(BF).reshape(count * CAP, rows)

    place = jnp.stack([x, c, 4 * j + x, y * rows]).astype(jnp.int32)

    def pick_rows(source, extra=None):
        half = lax.dynamic_slice_in_dim(source, c * HALF, HALF, 1)
        sent = dot(pick_b, half).astype(BF)
        if extra is not None:
            sent = jnp.concatenate([sent, extra], axis=1)
        return sent

    def send_rows(sent):
        width = sent.shape[1]
        return spread(sent.reshape(count, CAP, width)).reshape(count * CAP, width)

    gate_t = jnp.swapaxes(expert_gate, 1, 2)
    up_t = jnp.swapaxes(expert_up, 1, 2)
    first_part, second_part = pack(x, gate_t, up_t, expert_down)
    first_part = [shift(first_part[step - 1], "x", step) for step in (1, 2, 3)]

    group_ids = lax.dynamic_slice_in_dim(segment, z * group_len, group_len)
    key_number = jnp.arange(group_len, dtype=jnp.int32)
    first_length = jnp.sum((group_ids == 1).astype(jnp.int32))
    key_place = jnp.where(
        group_ids == 0,
        key_number - (group_len - PROMPT),
        key_number + PROMPT - jnp.where(group_ids == 1, 0, first_length),
    )
    frequency = jnp.power(10000.0, -2.0 * jnp.arange(ROPE // 2, dtype=F32) / ROPE)
    key_angle = key_place.astype(F32)[:, None] * frequency[None, :]
    tables = (jnp.cos(key_angle), jnp.sin(key_angle))
    segs = (group_ids.reshape(group_len, 1), group_ids.reshape(1, group_len))

    x_input = tokens.astype(F32)
    normed_f, _ = norm_rows(x_input, norm_gain)
    normed = normed_f.astype(BF)
    latent = dot(normed, kv_down).astype(BF)
    half_latent = lax.dynamic_slice_in_dim(latent, c * (rows // 2), rows // 2, 0)
    gathered = after(gather_ring(half_latent, "y", y), *second_part)
    query_lin = dot(normed, q_weight)
    attn_give, attn_keep, attended_b, compressed, kv_rows, key_rot, log_total, row_peak = attention(
        place, gathered, swap(gathered), query_lin, kv_gain, kv_up, out_weight, tables, segs
    )

    attn_got = swap(after(attn_give, *first_part))
    grad_rows = send_rows(pick_rows(after(out_grad, attn_got)))
    grad_rows = (grad_rows, swap(grad_rows))
    residual = own_rows(tokens).astype(F32) + sum_ring(attn_keep + attn_got.astype(F32), "x", x)
    mixed_f, inverse_two = norm_rows(residual, mix_gain)
    mixed_own = mixed_f.astype(BF)
    mixed_ring = [mixed_own] + [shift(mixed_own, "x", step) for step in (1, 2, 3)]
    mixed_mine = order_ring(x, mixed_ring)
    second_part = [after(piece, mixed_mine) for piece in second_part]
    second_part = [shift(second_part[step - 1], "x", step) for step in (1, 2, 3)]
    packed = (first_part, second_part)
    mixed_other = after(swap(mixed_mine), grad_rows[1])

    mixed_in, gate_probs, mixed_sent = gating(place, mixed_mine, mixed_other, router, pick_b)
    mixed_rows = send_rows(mixed_sent)
    shared_part, shared_mixed_grad, shared_grads = shared_experts(
        after(mixed_in, mixed_sent), out_grad, shared_gate.T, shared_up.T, shared_down
    )
    raw = raw_act_grad(place, after(grad_rows[0], shared_part), grad_rows[1], expert_down, packed)
    mixed_rows = after(mixed_rows, raw)
    mixed_rows = (mixed_rows, swap(mixed_rows))
    expert_act, scaled_act, gate_lin_grad, up_lin_grad, grad_keep, grad_give, slot_cols = (
        expert_pass(place, *mixed_rows, raw, gate_t, up_t, packed)
    )

    grad_half = (grad_keep + swap(grad_give).astype(F32)).astype(BF)
    sent_grad = jnp.concatenate([grad_half, slot_cols], axis=1)
    returned_grad = send_rows(sent_grad)
    parts = weight_grads(
        place,
        (0, 1, 2),
        (0, 1, 2, 3),
        (gate_lin_grad, up_lin_grad, after(scaled_act, sent_grad)),
        (mixed_rows, grad_rows),
    )

    def send_home(part):
        return [part[0]] + [shift(part[step], "x", RING - step) for step in (1, 2, 3)]

    home = [send_home(parts[0])]
    produced_keep, produced_give = produce(
        place, after(expert_act, parts[0][0]), mixed_rows[0], expert_down, packed
    )
    mixed_give, mixed_keep = combine_rows(
        place, pick_b, after(returned_grad, parts[0][0], produced_give), shared_mixed_grad
    )
    mixed_half = mixed_keep + swap(after(mixed_give, *home[0])).astype(F32)
    mixed_half, mixed_sent = ring_parts(mixed_half, x)
    shared_grads = lax.psum_scatter(
        after(shared_grads, returned_grad), EXPERT, scatter_dimension=0, tiled=True
    )
    produced_half = (produced_keep + swap(produced_give).astype(F32)).astype(BF)
    produced = send_rows(after(produced_half, *mixed_sent))
    mixed_total = sum_sent(mixed_half, mixed_sent, "x")
    prob_grad = mixed_total[:, D : D + EXPERTS] + mixed_total[:, D + EXPERTS :]
    own_probs = own_rows(gate_probs)
    logit_grad = (
        own_probs * (prob_grad - jnp.sum(own_probs * prob_grad, axis=-1, keepdims=True))
    ).astype(BF)
    mixed_grad = mixed_total[:, :D] + dot(logit_grad, router, ((1,), (1,)))
    mid_norm_grad, mix_gain_grad = norm_back(residual, inverse_two, mix_gain, mixed_grad)
    mid_grad = own_rows(out_grad).astype(F32) + mid_norm_grad
    branch_own = jnp.concatenate(
        [mid_grad.astype(BF), logit_grad, jnp.zeros((OWN, 128 - EXPERTS), BF)], axis=1
    )
    branch_ring = [branch_own] + [shift(branch_own, "x", step) for step in (1, 2, 3)]
    branch_mine = order_ring(x, branch_ring)
    home.append(send_home([after(piece, branch_mine) for piece in parts[1]]))
    branch_mine = after(branch_mine, produced)
    latent_give, latent_keep, kv_grad, query_lin_grad, branch_all = attention_back(
        place, branch_mine, swap(branch_mine), query_lin, compressed, kv_rows, key_rot, log_total, kv_up, out_weight,
        tables, segs,
    )
    latent_give = after(latent_give, *home[1])
    latent_own, latent_sent = ring_parts(latent_keep + swap(latent_give).astype(F32), y)
    home.append(send_home([after(piece, latent_give) for piece in parts[2]]))
    normed_give, normed_keep = normed_grad_part(
        place, after(query_lin_grad, *latent_sent), q_weight
    )
    latent_half = sum_sent(latent_own, latent_sent, "y")
    latent_own, latent_sent = ring_parts(after(latent_half, normed_give, *home[2]), x)
    normed_half = normed_keep + swap(normed_give).astype(F32)
    normed_own, normed_sent = ring_parts(after(normed_half, *latent_sent), x)
    big = projection_grads(
        normed, branch_all, compressed, query_lin_grad, attended_b, after(kv_grad, *normed_sent)
    )
    latent_total = after(sum_sent(latent_own, latent_sent, "x"), big)
    normed_total = sum_sent(normed_own, normed_sent, "x")

    logit_grad_all = branch_all[:, D : D + EXPERTS]
    own_comp = own_rows(latent)[:, :KVRANK].astype(F32)
    _, own_inverse = norm_rows(own_comp, kv_gain)
    comp_own_grad, kv_gain_grad = norm_back(
        own_comp, own_inverse, kv_gain, latent_total[:, :KVRANK]
    )
    latent_grad = jnp.concatenate([comp_own_grad, latent_total[:, KVRANK:]], axis=-1).astype(BF)
    latent_ring = [latent_grad] + [shift(latent_grad, "x", step) for step in (1, 2, 3)]
    latent_grad_all = gather_pair(order_ring(x, latent_ring), c)
    latent_grad_all = jnp.swapaxes(latent_grad_all, 0, 1).reshape(rows, LATENT)
    normed_grad = normed_total + dot(latent_grad, kv_down, ((1,), (1,)))
    own_input = own_rows(tokens).astype(F32)
    _, inverse_one = norm_rows(own_input, norm_gain)
    input_norm_grad, norm_gain_grad = norm_back(own_input, inverse_one, norm_gain, normed_grad)

    shared_sum = after(shared_grads, latent_grad_all).astype(F32)
    shared_gate_grad = shared_sum[:, :SHARED]
    shared_up_grad = shared_sum[:, WIDE : WIDE + SHARED]
    shared_down_grad = shared_sum[:, 2 * WIDE : 2 * WIDE + SHARED].T

    up_rows = UP_ROWS
    big = spread(after(big, produced).reshape(count, 128, BIG))
    big = jnp.sum(big.astype(F32), axis=0)
    q_width = q_weight.shape[1]
    q_weight_grad = big[:, :q_width]
    out_weight_grad = big[:, q_width : q_width + ATT].T
    kv_up_grad = jnp.swapaxes(big[:, q_width + ATT :].reshape(4, up_rows, 128), 0, 1).reshape(
        up_rows, 4 * 128
    )

    kd_width = KD_COLUMNS
    rt_width = ROUTER_COLUMNS
    small = small_grads(
        lax.dynamic_slice_in_dim(latent_grad_all, t * kd_width, kd_width, 1),
        lax.dynamic_slice_in_dim(logit_grad_all, t * rt_width, rt_width, 1),
        normed,
        mixed_in,
        norm_gain_grad,
        mix_gain_grad,
        kv_gain_grad,
        row_peak,
    )
    small_sent = small
    small = spread(after(small, big))

    home.append(send_home([after(piece, *latent_ring) for piece in parts[3]]))
    layer_give, layer_keep = combine_rows(
        place, pick_b, after(produced, small_sent), shared_part
    )
    layer_half = layer_keep + swap(layer_give).astype(F32)
    layer_total = residual + sum_ring(after(layer_half, *home[3]), "x", x)
    tokens_own = (mid_grad + input_norm_grad).astype(BF)
    rows_out = gather_rows(jnp.concatenate([layer_total.astype(BF), tokens_own], axis=1))
    layer_out = rows_out[:, :D]
    tokens_grad = rows_out[:, D:].astype(F32)
    expert_gate_grad, expert_up_grad, expert_down_grad = unpack(
        x, [after(home[0], small, layer_total), *home[1:]]
    )
    expert_gate_grad = jnp.swapaxes(expert_gate_grad, 1, 2)
    expert_up_grad = jnp.swapaxes(expert_up_grad, 1, 2)

    small = small.astype(F32)
    wide = kd_width + rt_width
    small_sum = jnp.sum(small[:, : wide + 6], axis=0)
    peaks = small[:, wide + 6 : wide + 9, :heads]
    top_peak = jnp.max(peaks[:, 0] + peaks[:, 1] + peaks[:, 2], axis=0)
    vectors = small_sum[wide : wide + 6].reshape(3, 2, 128).sum(axis=1)
    vector_high, vector_low = split_two(vectors)
    shared_small = jnp.concatenate(
        [small_sum[:wide].astype(BF), vector_high, vector_low, jnp.zeros((10, 128), BF)], axis=0
    )
    all_small = gather_few(shared_small).reshape(8, wide + 16, 128)
    kv_down_grad = all_small[:, :kd_width].reshape(8 * kd_width, 128).T.astype(F32)
    router_grad = all_small[:, kd_width:wide].reshape(8 * rt_width, 128).T.astype(F32)
    vectors = jnp.sum(all_small[:, wide : wide + 6].astype(F32), axis=0).reshape(2, 3, 128).sum(axis=0)
    norm_gain_grad = vectors[0]
    mix_gain_grad = vectors[1]
    kv_gain_grad = vectors[2, : KVRANK // count]

    factor = jnp.minimum(1.0, threshold[0] / jnp.maximum(top_peak, 1.0))
    root_factor = jnp.sqrt(factor)
    q_rows = q_weight.shape[0] // count
    own_query = lax.dynamic_slice_in_dim(q_weight, j * q_rows, q_rows, 0).astype(F32)
    query_step = (own_query - step_size[0] * q_weight_grad).reshape(q_rows, heads, NOPE + ROPE)
    q_weight_new = jnp.concatenate(
        [
            query_step[..., :NOPE] * root_factor[None, :, None],
            query_step[..., NOPE:] * factor[None, :, None],
        ],
        axis=-1,
    ).reshape(q_rows, heads * (NOPE + ROPE))
    own_up = lax.dynamic_slice_in_dim(kv_up, j * up_rows, up_rows, 0).astype(F32)
    up_step = (own_up - step_size[0] * kv_up_grad).reshape(up_rows, heads, NOPE + VDIM)
    kv_up_new = jnp.concatenate(
        [up_step[..., :NOPE] * root_factor[None, :, None], up_step[..., NOPE:]], axis=-1
    ).reshape(up_rows, heads * (NOPE + VDIM))
    return (
        layer_out,
        tokens_grad,
        q_weight_grad,
        kv_down_grad,
        kv_up_grad,
        out_weight_grad,
        router_grad,
        norm_gain_grad,
        kv_gain_grad,
        mix_gain_grad,
        shared_gate_grad,
        shared_up_grad,
        shared_down_grad,
        expert_gate_grad,
        expert_up_grad,
        expert_down_grad,
        q_weight_new,
        kv_up_new,
    )


def solution(mesh):
    fine = Mesh(mesh.devices.reshape(4, 4, 4, 2), ("z", "y", "x", "c"))
    return jax.shard_map(
        shards,
        mesh=fine,
        in_specs=(
            P(EXPERT, None),
            P(EXPERT, None),
            P(EXPERT, None),
            P(),
            P(),
            P(None, TENSOR),
            P(),
            P(),
            P(None, TENSOR),
            P(TENSOR, None),
            P(),
            P(),
            P(None, TENSOR),
            P(None, TENSOR),
            P(TENSOR, None),
            P(EXPERT, None, TENSOR),
            P(EXPERT, None, TENSOR),
            P(EXPERT, TENSOR, None),
            P(),
            P(),
        ),
        out_specs=(
            P(EXPERT, None),
            P(EXPERT, None),
            P(EXPERT, TENSOR),
            P(EXPERT, None),
            P(EXPERT, TENSOR),
            P(TENSOR, EXPERT),
            P(EXPERT, None),
            P(EXPERT),
            P(EXPERT),
            P(EXPERT),
            P(EXPERT, TENSOR),
            P(EXPERT, TENSOR),
            P(TENSOR, EXPERT),
            P(EXPERT, None, TENSOR),
            P(EXPERT, None, TENSOR),
            P(EXPERT, TENSOR, None),
            P(EXPERT, TENSOR),
            P(EXPERT, TENSOR),
        ),
        check_vma=False,
    )
```

```python
import functools
import math

import jax
import jax.numpy as jnp
from jax import lax
from jax.experimental import pallas as pl
from jax.experimental.pallas import tpu as pltpu
from jax.sharding import Mesh
from jax.sharding import PartitionSpec as P

D = 2048
HALF = D // 2
NOPE = 128
ROPE = 64
VDIM = 128
KVRANK = 512
TOPK = 6
PROMPT = 1024
CONT = 2
EXPERTS = 64
CAP = 48
SPAN = 4
RING = 4
OWN = 48
EPSILON = 1e-06

BF = jnp.bfloat16
F32 = jnp.float32
EXPERT = ("z", "y")
TENSOR = ("x", "c")


def dot(left, right, contract=((1,), (0,))):
    return lax.dot_general(left, right, (contract, ((), ())), preferred_element_type=F32)


def swap(block):
    return lax.ppermute(block, "c", [(0, 1), (1, 0)])


def shift(block, axis, step):
    return lax.ppermute(block, axis, [(i, (i + step) % RING) for i in range(RING)])


def spread(block):
    return lax.all_to_all(block, EXPERT, split_axis=0, concat_axis=0, tiled=True)


def pick_index(blocks, index, axis=0):
    return lax.dynamic_index_in_dim(blocks, index, axis, keepdims=False)


def sum_ring(blocks, axis, index):
    return sum_sent(*ring_parts(blocks, index), axis)


def ring_parts(blocks, index):
    own = pick_index(blocks, index)
    return own, [pick_index(blocks, (index + step) % RING).astype(BF) for step in (1, 2, 3)]


def sum_sent(own, parts, axis):
    for step in (1, 2, 3):
        own = own + shift(parts[step - 1], axis, step).astype(F32)
    return own


def gather_ring(block, axis, index):
    blocks = jnp.zeros((RING,) + block.shape, block.dtype)
    blocks = lax.dynamic_update_index_in_dim(blocks, block, index, 0)
    for step in (1, 2, 3):
        blocks = lax.dynamic_update_index_in_dim(
            blocks, shift(block, axis, step), (index - step) % RING, 0
        )
    return blocks


def gather_pair(block, core):
    blocks = jnp.zeros((2,) + block.shape, block.dtype)
    blocks = lax.dynamic_update_index_in_dim(blocks, block, core, 0)
    return lax.dynamic_update_index_in_dim(blocks, swap(block), 1 - core, 0)


def gather_rows(block):
    return lax.all_gather(block, TENSOR, axis=0, tiled=True)


def after(value, *others):
    return lax.optimization_barrier((value, *others))[0]


PIECE = 176
HIDDEN = RING * PIECE
SLOTS = 16 * CAP
TILE = 256
EXTRA = 128
NT = ((1,), (1,))
TN = ((0,), (0,))
VMEM_LIMIT = 56 << 20
HINT = 64


def whole(*shape):
    return pl.BlockSpec(shape, lambda *_: (0,) * len(shape))


def anywhere():
    return pl.BlockSpec(memory_space=pl.ANY)


def copy_all(pairs, sems):
    copies = [pltpu.make_async_copy(a, b, sems.at[i]) for i, (a, b) in enumerate(pairs)]
    for one in copies:
        one.start()
    for one in copies:
        one.wait()


def cost(flops, bytes_accessed, exps=0):
    return pl.CostEstimate(
        flops=int(flops) // HINT, bytes_accessed=int(bytes_accessed) // HINT, transcendentals=0
    )


OUTWARD = (208, 320)
HOMEWARD = (112, 112, 304)


def spans(parts):
    found, start = [], 0
    for part, size in enumerate(parts):
        at = start
        while at < start + size:
            weight, inside = divmod(at, PIECE)
            length = min(PIECE - inside, start + size - at)
            found.append((part, at - start, weight, inside, length))
            at += length
        start += size
    return found


def pack_kernel(x_ref, *refs):
    for step in range(3):
        for part, at, weight, inside, length in spans(OUTWARD):
            out = refs[9 + step * len(OUTWARD) + part]
            out[at : at + length, :] = refs[3 * step + weight][0, inside : inside + length, :]


def pack(x, gate, up, down):
    block = 512

    def source(step):
        return pl.BlockSpec((1, PIECE, block), lambda i, x: (lax.rem(x[0] + step, RING), 0, i))

    outs = pl.pallas_call(
        pack_kernel,
        grid_spec=pltpu.PrefetchScalarGridSpec(
            num_scalar_prefetch=1,
            grid=(D // block,),
            in_specs=[source(step) for step in (1, 2, 3) for _ in range(3)],
            out_specs=[pl.BlockSpec((size, block), lambda i, _: (0, i)) for size in OUTWARD] * 3,
        ),
        out_shape=[jax.ShapeDtypeStruct((size, D), BF) for size in OUTWARD] * 3,
        compiler_params=pltpu.CompilerParams(vmem_limit_bytes=VMEM_LIMIT),
        cost_estimate=cost(0, 13 << 20),
        name="pack_weights",
    )(x.reshape(1), *((gate, up, down) * 3))
    return [outs[part :: len(OUTWARD)] for part in range(len(OUTWARD))]


def unpack_kernel(x_ref, *refs):
    outs = refs[len(HOMEWARD) * RING :]
    for step in range(RING):
        index = lax.rem(x_ref[0] + step, RING)
        for part, at, weight, inside, length in spans(HOMEWARD):
            piece = refs[part * RING + step]
            outs[weight][index, inside : inside + length, :] = piece[at : at + length, :].astype(F32)


def unpack(x, parts):
    block = 512
    return pl.pallas_call(
        unpack_kernel,
        grid_spec=pltpu.PrefetchScalarGridSpec(
            num_scalar_prefetch=1,
            grid=(D // block,),
            in_specs=[
                pl.BlockSpec((size, block), lambda i, _: (0, i))
                for size in HOMEWARD
                for _ in range(RING)
            ],
            out_specs=[pl.BlockSpec((RING, PIECE, block), lambda i, _: (0, 0, i))] * 3,
        ),
        out_shape=[jax.ShapeDtypeStruct((RING, PIECE, D), F32)] * 3,
        compiler_params=pltpu.CompilerParams(vmem_limit_bytes=VMEM_LIMIT),
        cost_estimate=cost(0, 26 << 20),
        name="unpack_gradients",
    )(x.reshape(1), *[piece for part in parts for piece in part])


def load_weight(which, index, own_ref, parts, weight):
    pairs = [(own_ref.at[index], weight.at[pl.ds(0, PIECE)])]
    for part, at, kind, inside, length in spans(OUTWARD):
        if kind == which:
            for step, piece in enumerate(parts[part]):
                start = (step + 1) * PIECE + inside
                pairs.append((piece.at[pl.ds(at, length)], weight.at[pl.ds(start, length)]))
    return pairs


def halves_of(place_ref):
    core = place_ref[1]
    return (
        pl.ds(pl.multiple_of(core * HALF, HALF), HALF),
        pl.ds(pl.multiple_of((1 - core) * HALF, HALF), HALF),
    )


def expert_kernel(
    place_ref,
    mine_ref,
    other_ref,
    grad_mine_ref,
    grad_other_ref,
    gate_ref,
    own_gate,
    own_up,
    own_down,
    p1,
    p2,
    p3,
    q1,
    q2,
    q3,
    act_ref,
    scaled_ref,
    gate_grad_ref,
    up_grad_ref,
    keep_ref,
    give_ref,
    columns_ref,
    gate_w,
    up_w,
    down_w,
    sems,
):
    @pl.when(pl.program_id(0) == 0)
    def _():
        index = place_ref[0]
        parts = {0: (p1, p2, p3), 1: (q1, q2, q3)}
        copy_all(
            load_weight(0, index, own_gate, parts, gate_w)
            + load_weight(1, index, own_up, parts, up_w)
            + load_weight(2, index, own_down, parts, down_w),
            sems,
        )

    first, second = halves_of(place_ref)
    mine, other = mine_ref[...], other_ref[...]
    extra = gate_ref[...].astype(F32)
    gate = extra[:, 0:1] + extra[:, 1:2]
    gate_lin = dot(mine, gate_w[:, first], NT) + dot(other, gate_w[:, second], NT)
    up_lin = dot(mine, up_w[:, first], NT) + dot(other, up_w[:, second], NT)
    raw = dot(grad_mine_ref[...], down_w[:, first], NT)
    raw = raw + dot(grad_other_ref[...], down_w[:, second], NT)
    sigmoid = jax.nn.sigmoid(gate_lin)
    silu = gate_lin * sigmoid
    act = (silu * up_lin).astype(BF)
    act_ref[...] = act
    act = act.astype(F32)
    scaled_ref[...] = (act * gate).astype(BF)
    act_grad = raw * gate
    gate_grad = (act_grad * up_lin * (sigmoid * (1.0 + gate_lin * (1.0 - sigmoid)))).astype(BF)
    up_grad = (act_grad * silu).astype(BF)
    gate_grad_ref[...] = gate_grad
    up_grad_ref[...] = up_grad
    keep_ref[...] = dot(gate_grad, gate_w[:, first]) + dot(up_grad, up_w[:, first])
    give_ref[...] = (dot(gate_grad, gate_w[:, second]) + dot(up_grad, up_w[:, second])).astype(BF)
    slot_grad = jnp.sum(act * raw, axis=1, keepdims=True)
    high = slot_grad.astype(BF).astype(F32)
    lane = lax.broadcasted_iota(jnp.int32, (TILE, EXTRA), 1)
    expert_id = place_ref[2]
    columns_ref[...] = jnp.where(
        lane == expert_id, high, jnp.where(lane == EXPERTS + expert_id, slot_grad - high, 0.0)
    ).astype(BF)


def expert_pass(place, mine, other, gate, up, down, packed):
    rows = lambda width, at=0: pl.BlockSpec((TILE, width), lambda i, _: (i, at))
    shape = lambda width, dtype: jax.ShapeDtypeStruct((SLOTS, width), dtype)
    return pl.pallas_call(
        expert_kernel,
        grid_spec=pltpu.PrefetchScalarGridSpec(
            num_scalar_prefetch=1,
            grid=(SLOTS // TILE,),
            in_specs=[rows(HALF)] * 2 + [rows(HALF, 1)] * 2 + [rows(EXTRA, D // EXTRA)]
            + [anywhere()] * 9,
            out_specs=[rows(HIDDEN)] * 4 + [rows(HALF)] * 2 + [rows(EXTRA)],
            scratch_shapes=[pltpu.VMEM((HIDDEN, D), BF)] * 3 + [pltpu.SemaphoreType.DMA((15,))],
        ),
        out_shape=[shape(HIDDEN, BF)] * 4
        + [shape(HALF, F32), shape(HALF, BF), shape(EXTRA, BF)],
        compiler_params=pltpu.CompilerParams(vmem_limit_bytes=VMEM_LIMIT),
        cost_estimate=cost(10 * SLOTS * D * HIDDEN, 24 << 20, SLOTS * HIDDEN),
        name="expert_pass",
    )(place, mine, other, mine, other, mine, gate, up, down, *[p for part in packed for p in part])


def produce_kernel(place_ref, act_ref, mine_ref, own_down, p1, p2, p3, keep_ref, give_ref, down, sems):
    @pl.when(pl.program_id(0) == 0)
    def _():
        copy_all(load_weight(2, place_ref[0], own_down, {1: (p1, p2, p3)}, down), sems)

    first, second = halves_of(place_ref)
    extra = mine_ref[...].astype(F32)
    gate = extra[:, 0:1] + extra[:, 1:2]
    keep_ref[...] = dot(act_ref[...], down[:, first]) * gate
    give_ref[...] = (dot(act_ref[...], down[:, second]) * gate).astype(BF)


def produce(place, act, mine, down, packed):
    rows = lambda width: pl.BlockSpec((TILE, width), lambda i, _: (i, 0))
    return pl.pallas_call(
        produce_kernel,
        grid_spec=pltpu.PrefetchScalarGridSpec(
            num_scalar_prefetch=1,
            grid=(SLOTS // TILE,),
            in_specs=[
                rows(HIDDEN),
                pl.BlockSpec((TILE, EXTRA), lambda i, _: (i, D // EXTRA)),
            ]
            + [anywhere()] * 4,
            out_specs=[rows(HALF)] * 2,
            scratch_shapes=[pltpu.VMEM((HIDDEN, D), BF), pltpu.SemaphoreType.DMA((4,))],
        ),
        out_shape=[
            jax.ShapeDtypeStruct((SLOTS, HALF), F32),
            jax.ShapeDtypeStruct((SLOTS, HALF), BF),
        ],
        compiler_params=pltpu.CompilerParams(vmem_limit_bytes=VMEM_LIMIT),
        cost_estimate=cost(2 * SLOTS * D * HIDDEN, 9 << 20),
        name="produce",
    )(place, act, mine, down, *packed[1])


def weight_grad_kernel(place_ref, *refs, weights, parts):
    lefts = refs[: len(weights)]
    rights, outs = refs[len(weights) : -len(parts) * RING], refs[-len(parts) * RING :]
    own = pl.program_id(0) < 2
    rights = [jnp.where(own, rights[i][...], rights[i + 1][...]) for i in range(0, len(rights), 2)]
    for left, weight in zip(lefts, weights):
        right = rights[1] if weight == 2 and len(rights) > 1 else rights[0]
        product = dot(left[...], right, TN).astype(BF)
        for step in range(RING):
            for part, at, kind, inside, length in spans(HOMEWARD):
                if kind == weight:
                    start = step * PIECE + inside
                    out = outs[parts.index(part) * RING + step]
                    out[at : at + length, :] = product[start : start + length, :]


def weight_grads(place, weights, parts, lefts, rows):
    block = HALF // 2
    mine = [pl.BlockSpec((SLOTS, block), lambda i, _, at=at: (0, at + jnp.minimum(i, 1))) for at in (0, 2)]
    other = [
        pl.BlockSpec((SLOTS, block), lambda i, _, at=at: (0, at + jnp.maximum(i - 2, 0)))
        for at in (0, 2)
    ]
    sizes = [HOMEWARD[part] for part in parts for _ in range(RING)]
    outs = pl.pallas_call(
        functools.partial(weight_grad_kernel, weights=weights, parts=parts),
        grid_spec=pltpu.PrefetchScalarGridSpec(
            num_scalar_prefetch=1,
            grid=(4,),
            in_specs=[whole(SLOTS, HIDDEN)] * len(lefts)
            + [mine[0], other[0], mine[1], other[1]],
            out_specs=[
                pl.BlockSpec((size, block), lambda i, place: (0, lax.rem(2 * place[1] + i, 4)))
                for size in sizes
            ],
        ),
        out_shape=[jax.ShapeDtypeStruct((size, D), BF) for size in sizes],
        compiler_params=pltpu.CompilerParams(vmem_limit_bytes=VMEM_LIMIT),
        cost_estimate=cost(2 * len(lefts) * SLOTS * D * HIDDEN, 18 << 20),
        name="weight_grads",
    )(place, *lefts, *rows, *rows)
    return [outs[i * RING : (i + 1) * RING] for i in range(len(parts))]


SHARED = 352
WIDE = 384
ATT = 2 * VDIM


def shared_kernel(mixed, out_grad, gate_w, up_w, down_w, part, mixed_grad, grads):
    gate_lin = dot(mixed[...], gate_w[...], NT)
    up_lin = dot(mixed[...], up_w[...], NT)
    sigmoid = jax.nn.sigmoid(gate_lin)
    silu = gate_lin * sigmoid
    act = (silu * up_lin).astype(BF)
    act_grad = dot(out_grad[...], down_w[...], NT)
    gate_grad = (act_grad * up_lin * (sigmoid * (1.0 + gate_lin * (1.0 - sigmoid)))).astype(BF)
    up_grad = (act_grad * silu).astype(BF)
    for start in range(0, D, 512):
        at = slice(start, start + 512)
        part[:, at] = dot(act, down_w[:, at])
        mixed_grad[:, at] = dot(gate_grad, gate_w[:, at]) + dot(up_grad, up_w[:, at])
        zeros = jnp.zeros((512, WIDE - SHARED), BF)
        for i, (left, right) in enumerate(((mixed, gate_grad), (mixed, up_grad), (out_grad, act))):
            start = i * WIDE
            grads[at, start : start + SHARED] = dot(left[:, at], right, TN).astype(BF)
            grads[at, start + SHARED : start + WIDE] = zeros


def shared_experts(mixed, out_grad, gate_w, up_w, down_w):
    args = (mixed, out_grad, gate_w, up_w, down_w)
    rows = mixed.shape[0]
    outs = [
        jax.ShapeDtypeStruct((rows, D), F32),
        jax.ShapeDtypeStruct((rows, D), F32),
        jax.ShapeDtypeStruct((D, 3 * WIDE), BF),
    ]
    return pl.pallas_call(
        shared_kernel,
        grid=(1,),
        in_specs=[whole(*arg.shape) for arg in args],
        out_specs=[whole(*out.shape) for out in outs],
        out_shape=outs,
        compiler_params=pltpu.CompilerParams(vmem_limit_bytes=VMEM_LIMIT),
        cost_estimate=cost(18 * rows * D * SHARED, 18 << 20, rows * SHARED),
        name="shared_experts",
    )(*args)


GROUP = 1536
ROWS = 384
LATENT = KVRANK + ROPE
HEADS = 2
HEAD = NOPE + ROPE
SCALE = 1.0 / math.sqrt(HEAD)


def turn(block, cosine, sine):
    half = ROPE // 2
    return block * cosine + jnp.concatenate([block[:, half:], block[:, :half]], axis=1) * sine


def mask_bias(seg_keys, seg_rows, row_start):
    key = lax.broadcasted_iota(jnp.int32, (GROUP, ROWS), 0)
    row = lax.broadcasted_iota(jnp.int32, (GROUP, ROWS), 1) + row_start
    same = (seg_keys == seg_rows) & (key <= row)
    return jnp.where(same | ((seg_keys == 0) & (seg_rows > 0)), 0.0, -1e30)


def wide_tables(cos, sin):
    return jnp.concatenate([cos, cos], axis=1), jnp.concatenate([-sin, sin], axis=1)


def row_tables(cos_ref, sin_ref, row_start):
    at = pl.ds(pl.multiple_of(row_start, ROWS), ROWS)
    return wide_tables(cos_ref[at, :], sin_ref[at, :])


def head_queries(query, row_cos, row_sin, head):
    start = head * HEAD
    plain = query[:, start : start + NOPE].astype(BF)
    return plain, turn(query[:, start + NOPE : start + HEAD], row_cos, row_sin).astype(BF)


def attention_kernel(
    place_ref,
    mine_ref,
    other_ref,
    query_ref,
    gain_ref,
    kv_up_ref,
    out_weight_ref,
    cos_ref,
    sin_ref,
    seg_keys_ref,
    seg_rows_ref,
    give_ref,
    keep_ref,
    attended_ref,
    compressed_ref,
    kv_ref,
    key_rot_ref,
    log_total_ref,
    peak_ref,
    latent,
    attended,
):
    core = place_ref[1]
    half = ROWS // 2
    for block in range(SPAN):
        start = pl.multiple_of(block * ROWS + core * half, half)
        latent[pl.ds(start, half), :] = mine_ref[block]
        start = pl.multiple_of(block * ROWS + (1 - core) * half, half)
        latent[pl.ds(start, half), :] = other_ref[block]
    inputs = latent[:, :KVRANK].astype(F32)
    inverse = lax.rsqrt(jnp.mean(inputs * inputs, axis=1, keepdims=True) + EPSILON)
    compressed_ref[...] = (inputs * inverse * gain_ref[...]).astype(BF)
    kv_ref[...] = dot(compressed_ref[...], kv_up_ref[...]).astype(BF)
    cosine, sine = wide_tables(cos_ref[...], sin_ref[...])
    key_rot_ref[...] = turn(latent[:, KVRANK:].astype(F32), cosine, sine).astype(BF)
    seg_rows = seg_rows_ref[:, pl.ds(pl.multiple_of(place_ref[3], ROWS), ROWS)]
    bias = mask_bias(seg_keys_ref[...], seg_rows, place_ref[3])
    row_cos, row_sin = row_tables(cos_ref, sin_ref, place_ref[3])
    for head in range(HEADS):
        plain, turned = head_queries(query_ref, row_cos, row_sin, head)
        start = head * (NOPE + VDIM)
        scores = dot(kv_ref[:, start : start + NOPE], plain, NT)
        scores = (scores + dot(key_rot_ref[...], turned, NT)) * SCALE + bias
        peak = jnp.max(scores, axis=0, keepdims=True)
        powers = jnp.exp(scores - peak)
        total = jnp.sum(powers, axis=0, keepdims=True)
        log_total_ref[head : head + 1, :] = peak + jnp.log(total)
        peak_ref[head : head + 1, :] = peak
        weights = (powers * (1.0 / total)).astype(BF)
        values = kv_ref[:, start + NOPE : start + NOPE + VDIM]
        attended[:, head * VDIM : (head + 1) * VDIM] = dot(values, weights, TN).T
    attended_ref[...] = attended[...].astype(BF)
    for block in range(RING):
        for out, which in ((give_ref, 1 - core), (keep_ref, core)):
            start = pl.multiple_of(block * 2 * OWN + which * OWN, OWN)
            out[block] = dot(
                attended[pl.ds(start, OWN), :].astype(BF), out_weight_ref[...]
            ).astype(out.dtype)


def attention(place, mine, other, query, gain, kv_up, out_weight, tables, segs):
    shape = jax.ShapeDtypeStruct
    args = (mine, other, query, gain.reshape(1, KVRANK), kv_up, out_weight, *tables, *segs)
    outs = [
        shape((RING, OWN, D), BF),
        shape((RING, OWN, D), F32),
        shape((ROWS, HEADS * VDIM), BF),
        shape((GROUP, KVRANK), BF),
        shape((GROUP, HEADS * (NOPE + VDIM)), BF),
        shape((GROUP, ROPE), BF),
        shape((HEADS, ROWS), F32),
        shape((HEADS, ROWS), F32),
    ]
    return pl.pallas_call(
        attention_kernel,
        grid_spec=pltpu.PrefetchScalarGridSpec(
            num_scalar_prefetch=1,
            grid=(1,),
            in_specs=[whole(*arg.shape) for arg in args],
            out_specs=[whole(*out.shape) for out in outs],
            scratch_shapes=[
                pltpu.VMEM((GROUP, LATENT), BF),
                pltpu.VMEM((ROWS, HEADS * VDIM), F32),
            ],
        ),
        out_shape=outs,
        compiler_params=pltpu.CompilerParams(vmem_limit_bytes=VMEM_LIMIT),
        cost_estimate=cost(3e9, 14 << 20, 2 * GROUP * ROWS),
        name="attention_forward",
    )(place, *args)


def attention_back_kernel(
    place_ref,
    mine_ref,
    other_ref,
    query_ref,
    compressed_ref,
    kv_ref,
    key_rot_ref,
    log_total_ref,
    kv_up_ref,
    out_weight_ref,
    cos_ref,
    sin_ref,
    seg_keys_ref,
    seg_rows_ref,
    give_ref,
    keep_ref,
    kv_grad_ref,
    query_grad_ref,
    branch_ref,
    comp_grad,
    rot_grad,
):
    core = place_ref[1]
    interleave(core, mine_ref, other_ref, branch_ref, D + EXTRA)
    attended_grad = dot(branch_ref[:, :D], out_weight_ref[...], NT).astype(BF)
    seg_rows = seg_rows_ref[:, pl.ds(pl.multiple_of(place_ref[3], ROWS), ROWS)]
    bias = mask_bias(seg_keys_ref[...], seg_rows, place_ref[3])
    row_cos, row_sin = row_tables(cos_ref, sin_ref, place_ref[3])
    turned_sum = 0.0
    query_grads = []
    for head in range(HEADS):
        plain, turned = head_queries(query_ref, row_cos, row_sin, head)
        start = head * (NOPE + VDIM)
        keys = kv_ref[:, start : start + NOPE]
        values = kv_ref[:, start + NOPE : start + NOPE + VDIM]
        key_rot = key_rot_ref[...]
        scores = (dot(keys, plain, NT) + dot(key_rot, turned, NT)) * SCALE + bias
        probs = jnp.exp(scores - log_total_ref[head : head + 1, :])
        grad = attended_grad[:, head * VDIM : (head + 1) * VDIM]
        value_grad = dot(probs.astype(BF), grad)
        prob_grad = dot(values, grad, NT)
        inner = jnp.sum(probs * prob_grad, axis=0, keepdims=True)
        score_grad = (probs * (prob_grad - inner)).astype(BF)
        kv_grad_ref[:, start : start + NOPE] = (dot(score_grad, plain) * SCALE).astype(BF)
        kv_grad_ref[:, start + NOPE : start + NOPE + VDIM] = value_grad.astype(BF)
        turned_sum = turned_sum + dot(score_grad, turned) * SCALE
        query_grads.append((dot(keys, score_grad, TN) * SCALE).T)
        turned_grad = (dot(key_rot, score_grad, TN) * SCALE).T
        query_grads.append(turn(turned_grad, row_cos, -row_sin))
    comp_grad[...] = dot(kv_grad_ref[...], kv_up_ref[...], NT)
    cosine, sine = wide_tables(cos_ref[...], sin_ref[...])
    rot_grad[...] = turn(turned_sum, cosine, -sine)
    for block in range(SPAN):
        for inner in range(RING):
            for out, which in ((give_ref, 1 - core), (keep_ref, core)):
                start = pl.multiple_of(block * ROWS + inner * 2 * OWN + which * OWN, OWN)
                out[block, inner, :, :KVRANK] = comp_grad[pl.ds(start, OWN), :].astype(out.dtype)
                out[block, inner, :, KVRANK:] = rot_grad[pl.ds(start, OWN), :].astype(out.dtype)
    query_grad_ref[...] = jnp.concatenate(query_grads, axis=1).astype(BF)


def attention_back(
    place, mine, other, query, compressed, kv, key_rot, log_total, kv_up, out_weight, tables, segs
):
    shape = jax.ShapeDtypeStruct
    args = (
        mine, other, query, compressed, kv, key_rot, log_total, kv_up, out_weight, *tables, *segs
    )
    outs = [
        shape((SPAN, RING, OWN, LATENT), BF),
        shape((SPAN, RING, OWN, LATENT), F32),
        shape((GROUP, HEADS * (NOPE + VDIM)), BF),
        shape((ROWS, HEADS * HEAD), BF),
        shape((ROWS, D + EXTRA), BF),
    ]
    return pl.pallas_call(
        attention_back_kernel,
        grid_spec=pltpu.PrefetchScalarGridSpec(
            num_scalar_prefetch=1,
            grid=(1,),
            in_specs=[whole(*arg.shape) for arg in args],
            out_specs=[whole(*out.shape) for out in outs],
            scratch_shapes=[pltpu.VMEM((GROUP, KVRANK), F32), pltpu.VMEM((GROUP, ROPE), F32)],
        ),
        out_shape=outs,
        compiler_params=pltpu.CompilerParams(vmem_limit_bytes=VMEM_LIMIT),
        cost_estimate=cost(4e9, 16 << 20, 2 * GROUP * ROWS),
        name="attention_backward",
    )(place, *args)


def normed_kernel(place_ref, query_grad_ref, q_weight_ref, give_ref, keep_ref):
    core = place_ref[1]
    for block in range(RING):
        for out, which in ((give_ref, 1 - core), (keep_ref, core)):
            start = pl.multiple_of(block * 2 * OWN + which * OWN, OWN)
            part = query_grad_ref[pl.ds(start, OWN), :]
            out[block] = dot(part, q_weight_ref[...], NT).astype(out.dtype)


def normed_grad_part(place, query_grad, q_weight):
    args = (query_grad, q_weight)
    outs = [
        jax.ShapeDtypeStruct((RING, OWN, D), BF),
        jax.ShapeDtypeStruct((RING, OWN, D), F32),
    ]
    return pl.pallas_call(
        normed_kernel,
        grid_spec=pltpu.PrefetchScalarGridSpec(
            num_scalar_prefetch=1,
            grid=(1,),
            in_specs=[whole(*arg.shape) for arg in args],
            out_specs=[whole(*out.shape) for out in outs],
        ),
        out_shape=outs,
        compiler_params=pltpu.CompilerParams(vmem_limit_bytes=VMEM_LIMIT),
        cost_estimate=cost(6e8, 5 << 20),
        name="normed_grad_part",
    )(place, *args)


UP_ROWS = KVRANK // 16
BIG = HEADS * HEAD + ATT + 128


def projection_grad_kernel(
    normed, branch, compressed, query_grad, attended, kv_grad, out
):
    width = HEADS * HEAD
    out[:, :width] = dot(normed[...], query_grad[...], TN).astype(BF)
    out[:, width : width + ATT] = dot(branch[...], attended[...], TN).astype(BF)
    up = dot(compressed[...], kv_grad[...], TN)
    for index in range(4):
        for part in range(4):
            start = index * 128 + part * UP_ROWS
            out[start : start + UP_ROWS, width + ATT :] = up[
                index * UP_ROWS : (index + 1) * UP_ROWS, part * 128 : (part + 1) * 128
            ].astype(BF)


def projection_grads(normed, branch, compressed, query_grad, attended, kv_grad):
    block = 512
    return pl.pallas_call(
        projection_grad_kernel,
        grid=(D // block,),
        in_specs=[
            pl.BlockSpec((ROWS, block), lambda i: (0, i)),
            pl.BlockSpec((ROWS, block), lambda i: (0, i)),
            pl.BlockSpec((GROUP, 128), lambda i: (0, i)),
            whole(ROWS, HEADS * HEAD),
            whole(ROWS, ATT),
            whole(GROUP, HEADS * (NOPE + VDIM)),
        ],
        out_specs=pl.BlockSpec((block, BIG), lambda i: (i, 0)),
        out_shape=jax.ShapeDtypeStruct((D, BIG), BF),
        compiler_params=pltpu.CompilerParams(vmem_limit_bytes=VMEM_LIMIT),
        cost_estimate=cost(2e9, 10 << 20),
        name="projection_grads",
    )(normed, branch, compressed, query_grad, attended, kv_grad)


def combine_kernel(place_ref, pick_ref, returned_ref, shared_ref, give_ref, keep_ref, total):
    core = place_ref[1]
    rows = dot(pick_ref[...], returned_ref[...], TN)
    total[:, :D] = shared_ref[...]
    mine = pl.ds(pl.multiple_of(core * HALF, HALF), HALF)
    total[:, mine] = total[:, mine] + rows[:, :HALF]
    if returned_ref.shape[1] > HALF:
        total[:, D:] = rows[:, HALF:]
    for block in range(RING):
        for out, which in ((give_ref, 1 - core), (keep_ref, core)):
            start = pl.multiple_of(block * 2 * OWN + which * OWN, OWN)
            out[block] = total[pl.ds(start, OWN), :].astype(out.dtype)


def combine_rows(place, pick, returned, shared):
    width = D + returned.shape[1] - HALF
    args = (pick, returned, shared)
    outs = [
        jax.ShapeDtypeStruct((RING, OWN, width), BF),
        jax.ShapeDtypeStruct((RING, OWN, width), F32),
    ]
    return pl.pallas_call(
        combine_kernel,
        grid_spec=pltpu.PrefetchScalarGridSpec(
            num_scalar_prefetch=1,
            grid=(1,),
            in_specs=[whole(*arg.shape) for arg in args],
            out_specs=[whole(*out.shape) for out in outs],
            scratch_shapes=[pltpu.VMEM((ROWS, width), F32)],
        ),
        out_shape=outs,
        compiler_params=pltpu.CompilerParams(vmem_limit_bytes=VMEM_LIMIT),
        cost_estimate=cost(7e8, 8 << 20),
        name="combine_rows",
    )(place, *args)


def order_kernel(x_ref, *refs):
    for step in range(RING):
        refs[RING][lax.rem(x_ref[0] + RING - step, RING)] = refs[step][...]


def order_ring(x, blocks):
    rows, width = blocks[0].shape
    return pl.pallas_call(
        order_kernel,
        grid_spec=pltpu.PrefetchScalarGridSpec(
            num_scalar_prefetch=1,
            grid=(1,),
            in_specs=[whole(rows, width)] * RING,
            out_specs=whole(RING, rows, width),
        ),
        out_shape=jax.ShapeDtypeStruct((RING, rows, width), blocks[0].dtype),
        cost_estimate=cost(0, 2 << 20),
        name="order_ring",
    )(x.reshape(1), *blocks)


def interleave(core, mine_ref, other_ref, out, width):
    for block in range(RING):
        for ref, which in ((mine_ref, core), (other_ref, 1 - core)):
            start = pl.multiple_of(block * 2 * OWN + which * OWN, OWN)
            out[pl.ds(start, OWN), :] = ref[block, :, :width]


def gating_kernel(
    place_ref, mine_ref, other_ref, router_ref, pick_ref, grad_ref, mixed_ref, probs_ref, sent_ref
):
    core = place_ref[1]
    interleave(core, mine_ref, other_ref, mixed_ref, D)
    logits = dot(mixed_ref[...], router_ref[...])
    powers = jnp.exp(logits - jnp.max(logits, axis=1, keepdims=True))
    probs = powers / jnp.sum(powers, axis=1, keepdims=True)
    probs_ref[...] = probs
    pick = pick_ref[...]
    high = probs.astype(BF)
    rest = probs - high.astype(F32)
    middle = rest.astype(BF)
    low = (rest - middle.astype(F32)).astype(BF)
    gates = dot(pick, high) + dot(pick, middle) + dot(pick, low)
    slot = lax.broadcasted_iota(jnp.int32, (SLOTS, EXPERTS), 0)
    lane = lax.broadcasted_iota(jnp.int32, (SLOTS, EXPERTS), 1)
    first = (lane - place_ref[0]) * (CAP // 4)
    inside = (slot >= first) & (slot < first + CAP) & (lax.rem(lane, 4) == place_ref[0])
    gate = jnp.sum(jnp.where(inside, gates, 0.0), axis=1, keepdims=True)
    high = gate.astype(BF).astype(F32)
    lane = lax.broadcasted_iota(jnp.int32, (SLOTS, EXTRA), 1)
    sent_ref[:, D:] = jnp.where(
        lane == 0, high, jnp.where(lane == 1, gate - high, 0.0)
    ).astype(BF)
    mine = pl.ds(pl.multiple_of(core * HALF, HALF), HALF)
    sent_ref[:, :HALF] = dot(pick, mixed_ref[:, mine]).astype(BF)
    sent_ref[:, HALF:D] = dot(pick, grad_ref[:, mine]).astype(BF)


def gating(place, mine, other, router, pick, out_grad):
    args = (mine, other, router, pick, out_grad)
    outs = [
        jax.ShapeDtypeStruct((ROWS, D), BF),
        jax.ShapeDtypeStruct((ROWS, EXPERTS), F32),
        jax.ShapeDtypeStruct((SLOTS, D + EXTRA), BF),
    ]
    return pl.pallas_call(
        gating_kernel,
        grid_spec=pltpu.PrefetchScalarGridSpec(
            num_scalar_prefetch=1,
            grid=(1,),
            in_specs=[whole(*arg.shape) for arg in args],
            out_specs=[whole(*out.shape) for out in outs],
        ),
        out_shape=outs,
        compiler_params=pltpu.CompilerParams(vmem_limit_bytes=VMEM_LIMIT),
        cost_estimate=cost(8e8, 6 << 20),
        name="gating",
    )(place, *args)


KD_COLUMNS = LATENT // 8
ROUTER_COLUMNS = EXPERTS // 8
SHARE = KD_COLUMNS + ROUTER_COLUMNS
SMALL = SHARE + 16


def small_kernel(latent, logit, normed, mixed, norm_gain, mix_gain, kv_gain, peak_ref, out):
    kv_down = dot(latent[...], normed[...], TN)
    router = dot(logit[...], mixed[...], TN)
    lane = lax.broadcasted_iota(jnp.int32, (1, 128), 1)
    peak = 0.0
    for head in range(HEADS):
        highest = jnp.max(peak_ref[head : head + 1, :], axis=1, keepdims=True)
        peak = jnp.where(lane == head, highest, peak)

    def parts(row, number):
        found = []
        for _ in range(number):
            found.append(row.astype(BF).astype(F32))
            row = row - found[-1]
        return found

    peaks = parts(peak, 3)
    zeros = jnp.zeros((7, 128), F32)
    for index in range(16):
        at = slice(index * 128, (index + 1) * 128)
        gain = kv_gain[:, index * UP_ROWS : (index + 1) * UP_ROWS]
        gain = jnp.concatenate([gain, jnp.zeros((1, 128 - UP_ROWS), F32)], axis=1)
        rows = parts(norm_gain[:, at], 2) + parts(mix_gain[:, at], 2) + parts(gain, 2)
        rows = [kv_down[:, at], router[:, at]] + rows + peaks + [zeros]
        out[index] = jnp.concatenate(rows, axis=0).astype(BF)


def small_grads(latent, logit, normed, mixed, norm_gain, mix_gain, kv_gain, peak):
    args = (
        latent,
        logit,
        normed,
        mixed,
        norm_gain.reshape(1, D),
        mix_gain.reshape(1, D),
        kv_gain.reshape(1, KVRANK),
        peak,
    )
    return pl.pallas_call(
        small_kernel,
        grid=(1,),
        in_specs=[whole(*arg.shape) for arg in args],
        out_specs=whole(16, SMALL, 128),
        out_shape=jax.ShapeDtypeStruct((16, SMALL, 128), BF),
        compiler_params=pltpu.CompilerParams(vmem_limit_bytes=VMEM_LIMIT),
        cost_estimate=cost(2e8, 4 << 20),
        name="small_grads",
    )(*args)


def split_two(value):
    high = lax.reduce_precision(value, 8, 7)
    return high.astype(BF), (value - high).astype(BF)


def norm_rows(inputs, gain_vec):
    inverse = lax.rsqrt(jnp.mean(inputs * inputs, axis=-1, keepdims=True) + EPSILON)
    return (inputs * inverse * gain_vec, inverse)


def norm_back(inputs, inverse, gain_vec, gradient):
    weighted = gradient * gain_vec
    inner = jnp.mean(weighted * inputs, axis=-1, keepdims=True)
    d_inputs = inverse * weighted - inputs * (inverse * inverse * inverse) * inner
    return (d_inputs, jnp.sum(gradient * inputs * inverse, axis=0))


def rotate(inputs, cosine, sine):
    half_size = inputs.shape[-1] // 2
    first_half = inputs[..., :half_size]
    second_half = inputs[..., half_size:]
    return jnp.concatenate(
        [first_half * cosine - second_half * sine, second_half * cosine + first_half * sine],
        axis=-1,
    )


def unrotate(gradient, cosine, sine):
    return rotate(gradient, cosine, -sine)


def shards(
    tokens,
    out_grad,
    routes,
    segment,
    norm_gain,
    q_weight,
    kv_down,
    kv_gain,
    kv_up,
    out_weight,
    mix_gain,
    router,
    shared_gate,
    shared_up,
    shared_down,
    expert_gate,
    expert_up,
    expert_down,
    step_size,
    threshold,
):
    rows = tokens.shape[0]
    x = lax.axis_index("x")
    c = lax.axis_index("c")
    y = lax.axis_index("y")
    z = lax.axis_index("z")
    j = z * RING + y
    t = x * 2 + c
    heads = q_weight.shape[1] // (NOPE + ROPE)
    group_len = rows * SPAN
    count = expert_down.shape[0] * 4
    score_scale = 1.0 / math.sqrt(NOPE + ROPE)
    own_start = t * OWN

    def own_rows(array):
        return lax.dynamic_slice_in_dim(array, own_start, OWN, 0)

    routes_t = routes.T
    chosen = 4 * jnp.arange(count, dtype=jnp.int32) + x
    hot = jnp.any(routes_t[None, :, :] == chosen[:, None, None], axis=1)
    number = jnp.arange(rows, dtype=jnp.int32)
    earlier = (number[:, None] < number[None, :]).astype(BF)
    slot = dot(hot.astype(BF), earlier)
    pick = hot[:, None, :] & (slot[:, None, :] == jnp.arange(CAP, dtype=F32)[None, :, None])
    pick_b = pick.astype(BF).reshape(count * CAP, rows)

    place = jnp.stack([x, c, 4 * j + x, y * rows]).astype(jnp.int32)

    def send_rows(sent):
        width = sent.shape[1]
        return spread(sent.reshape(count, CAP, width)).reshape(count * CAP, width)

    gate_t = jnp.swapaxes(expert_gate, 1, 2)
    up_t = jnp.swapaxes(expert_up, 1, 2)
    first_part, last_part = pack(x, gate_t, up_t, expert_down)
    first_part = [shift(first_part[step - 1], "x", step) for step in (1, 2, 3)]

    group_ids = lax.dynamic_slice_in_dim(segment, z * group_len, group_len)
    key_number = jnp.arange(group_len, dtype=jnp.int32)
    first_length = jnp.sum((group_ids == 1).astype(jnp.int32))
    key_place = jnp.where(
        group_ids == 0,
        key_number - (group_len - PROMPT),
        key_number + PROMPT - jnp.where(group_ids == 1, 0, first_length),
    )
    frequency = jnp.power(10000.0, -2.0 * jnp.arange(ROPE // 2, dtype=F32) / ROPE)
    key_angle = key_place.astype(F32)[:, None] * frequency[None, :]
    tables = (jnp.cos(key_angle), jnp.sin(key_angle))
    segs = (group_ids.reshape(group_len, 1), group_ids.reshape(1, group_len))

    x_input = after(tokens, last_part[0]).astype(F32)
    normed_f, _ = norm_rows(x_input, norm_gain)
    normed = normed_f.astype(BF)
    latent = dot(normed, kv_down).astype(BF)
    half_latent = lax.dynamic_slice_in_dim(latent, c * (rows // 2), rows // 2, 0)
    gathered = gather_ring(half_latent, "y", y)
    query_lin = dot(normed, q_weight)
    attn_give, attn_keep, attended_b, compressed, kv_rows, key_rot, log_total, row_peak = attention(
        place, gathered, swap(gathered), query_lin, kv_gain, kv_up, out_weight, tables, segs
    )

    attn_got = swap(after(attn_give, *first_part))
    attn_own, attn_sent = ring_parts(attn_keep + attn_got.astype(F32), x)
    residual = own_rows(tokens).astype(F32) + sum_sent(attn_own, attn_sent, "x")
    mixed_f, inverse_two = norm_rows(residual, mix_gain)
    mixed_own = mixed_f.astype(BF)
    mixed_ring = [mixed_own] + [shift(mixed_own, "x", step) for step in (1, 2, 3)]
    mixed_mine = order_ring(x, mixed_ring)
    last_part = [after(piece, mixed_mine) for piece in last_part]
    last_part = [shift(last_part[step - 1], "x", step) for step in (1, 2, 3)]
    packed = (first_part, last_part)
    mixed_other = swap(mixed_mine)

    mixed_in, gate_probs, mixed_sent = gating(
        place, mixed_mine, mixed_other, router, pick_b, out_grad
    )
    mixed_rows = send_rows(mixed_sent)
    shared_part, shared_mixed_grad, shared_grads = shared_experts(
        after(mixed_in, mixed_sent), out_grad, shared_gate.T, shared_up.T, shared_down
    )
    mixed_rows = after(mixed_rows, shared_part, *last_part)
    mixed_rows = (mixed_rows, swap(mixed_rows))
    expert_act, scaled_act, gate_lin_grad, up_lin_grad, grad_keep, grad_give, slot_cols = (
        expert_pass(place, *mixed_rows, gate_t, up_t, expert_down, packed)
    )

    grad_half = (grad_keep + swap(grad_give).astype(F32)).astype(BF)
    sent_grad = jnp.concatenate([grad_half, slot_cols], axis=1)
    returned_grad = send_rows(sent_grad)
    parts = weight_grads(
        place,
        (0, 1, 2),
        (0, 1, 2),
        (gate_lin_grad, up_lin_grad, after(scaled_act, sent_grad)),
        mixed_rows,
    )

    def send_home(part):
        return [part[0]] + [shift(part[step], "x", RING - step) for step in (1, 2, 3)]

    home = [send_home(parts[0])]
    produced_keep, produced_give = produce(
        place, after(expert_act, parts[0][0]), mixed_rows[0], expert_down, packed
    )
    mixed_give, mixed_keep = combine_rows(
        place, pick_b, after(returned_grad, parts[0][0], produced_give), shared_mixed_grad
    )
    mixed_half = mixed_keep + swap(after(mixed_give, *home[0])).astype(F32)
    mixed_half, mixed_sent = ring_parts(mixed_half, x)
    shared_grads = lax.psum_scatter(
        after(shared_grads, mixed_rows[0]), EXPERT, scatter_dimension=0, tiled=True
    )
    produced_half = (produced_keep + swap(produced_give).astype(F32)).astype(BF)
    produced = send_rows(after(produced_half, *mixed_sent))
    mixed_total = sum_sent(mixed_half, mixed_sent, "x")
    prob_grad = mixed_total[:, D : D + EXPERTS] + mixed_total[:, D + EXPERTS :]
    own_probs = own_rows(gate_probs)
    logit_grad = (
        own_probs * (prob_grad - jnp.sum(own_probs * prob_grad, axis=-1, keepdims=True))
    ).astype(BF)
    mixed_grad = mixed_total[:, :D] + dot(logit_grad, router, ((1,), (1,)))
    mid_norm_grad, mix_gain_grad = norm_back(residual, inverse_two, mix_gain, mixed_grad)
    mid_grad = own_rows(out_grad).astype(F32) + mid_norm_grad
    branch_own = jnp.concatenate(
        [mid_grad.astype(BF), logit_grad, jnp.zeros((OWN, 128 - EXPERTS), BF)], axis=1
    )
    branch_ring = [branch_own] + [shift(branch_own, "x", step) for step in (1, 2, 3)]
    branch_mine = order_ring(x, branch_ring)
    home.append(send_home([after(piece, branch_mine) for piece in parts[1]]))
    branch_mine = after(branch_mine, produced)
    latent_give, latent_keep, kv_grad, query_lin_grad, branch_all = attention_back(
        place, branch_mine, swap(branch_mine), query_lin, compressed, kv_rows, key_rot, log_total, kv_up, out_weight,
        tables, segs,
    )
    latent_give = after(latent_give, *home[1])
    latent_sent = (latent_keep + swap(latent_give).astype(F32)).astype(BF)
    latent_parts = lax.all_to_all(
        latent_sent.reshape(SPAN * RING, OWN, LATENT), ("y", "x"), split_axis=0, concat_axis=0,
        tiled=True,
    )
    big = projection_grads(
        normed, branch_all, compressed, query_lin_grad, attended_b, after(kv_grad, latent_sent)
    )
    normed_give, normed_keep = normed_grad_part(
        place, after(query_lin_grad, latent_sent, big), q_weight
    )
    latent_total = jnp.sum(after(latent_parts, normed_give).astype(F32), axis=0)
    normed_half = normed_keep + swap(normed_give).astype(F32)
    normed_own, normed_sent = ring_parts(normed_half, x)
    normed_total = sum_sent(normed_own, normed_sent, "x")

    logit_grad_all = branch_all[:, D : D + EXPERTS]
    own_comp = own_rows(latent)[:, :KVRANK].astype(F32)
    _, own_inverse = norm_rows(own_comp, kv_gain)
    comp_own_grad, kv_gain_grad = norm_back(
        own_comp, own_inverse, kv_gain, latent_total[:, :KVRANK]
    )
    latent_grad = jnp.concatenate([comp_own_grad, latent_total[:, KVRANK:]], axis=-1).astype(BF)
    latent_columns = jnp.swapaxes(latent_grad.reshape(OWN, 8, KD_COLUMNS), 0, 1)
    latent_columns = lax.all_to_all(
        latent_columns, TENSOR, split_axis=0, concat_axis=0, tiled=True
    )
    normed_grad = normed_total + dot(latent_grad, kv_down, ((1,), (1,)))
    own_input = own_rows(tokens).astype(F32)
    _, inverse_one = norm_rows(own_input, norm_gain)
    input_norm_grad, norm_gain_grad = norm_back(own_input, inverse_one, norm_gain, normed_grad)


    up_rows = UP_ROWS
    kd_width = KD_COLUMNS
    rt_width = ROUTER_COLUMNS
    small = small_grads(
        latent_columns.reshape(rows, kd_width),
        lax.dynamic_slice_in_dim(logit_grad_all, t * rt_width, rt_width, 1),
        normed,
        mixed_in,
        norm_gain_grad,
        mix_gain_grad,
        kv_gain_grad,
        row_peak,
    )
    small = jnp.swapaxes(small.reshape(count, 6, 16, 128), 1, 2).reshape(count, 16, BIG)
    packed_grads = jnp.concatenate([big.reshape(count, 128, BIG), small], axis=1)
    packed_sent = packed_grads
    packed_grads = spread(packed_grads)
    small = jnp.swapaxes(packed_grads[:, 128:].reshape(count, 16, 6, 128), 1, 2)
    small = small.reshape(count, SMALL, 128)
    layer_give, layer_keep = combine_rows(
        place, pick_b, after(produced, packed_sent), shared_part
    )
    layer_half = layer_keep + swap(layer_give).astype(F32)
    layer_total = residual + sum_ring(layer_half, "x", x)
    layer_out = gather_rows(layer_total.astype(BF))
    home.append(send_home([after(piece, layer_total) for piece in parts[2]]))
    tokens_grad = gather_rows((mid_grad + input_norm_grad).astype(BF)).astype(F32)
    shared_sum = after(shared_grads, layer_total).astype(F32)
    shared_gate_grad = shared_sum[:, :SHARED]
    shared_up_grad = shared_sum[:, WIDE : WIDE + SHARED]
    shared_down_grad = shared_sum[:, 2 * WIDE : 2 * WIDE + SHARED].T
    big = jnp.sum(packed_grads[:, :128].astype(F32), axis=0)
    q_width = q_weight.shape[1]
    q_weight_grad = big[:, :q_width]
    out_weight_grad = big[:, q_width : q_width + ATT].T
    kv_up_grad = jnp.swapaxes(big[:, q_width + ATT :].reshape(4, up_rows, 128), 0, 1).reshape(
        up_rows, 4 * 128
    )

    small = small.astype(F32)
    wide = kd_width + rt_width
    small_sum = jnp.sum(small[:, : wide + 6], axis=0)
    peaks = small[:, wide + 6 : wide + 9, :heads]
    top_peak = jnp.max(peaks[:, 0] + peaks[:, 1] + peaks[:, 2], axis=0)
    vectors = small_sum[wide : wide + 6].reshape(3, 2, 128).sum(axis=1)
    vector_high, vector_low = split_two(vectors)
    shared_small = jnp.concatenate(
        [small_sum[:wide].astype(BF), vector_high, vector_low, jnp.zeros((10, 128), BF)], axis=0
    )
    all_small = lax.all_to_all(
        jnp.broadcast_to(after(shared_small, *home[2])[None], (8, wide + 16, 128)), TENSOR, split_axis=0,
        concat_axis=0, tiled=True,
    )
    expert_gate_grad, expert_up_grad, expert_down_grad = unpack(
        x, [after(home[0], shared_small), *home[1:]]
    )
    all_small = after(all_small, expert_gate_grad, tokens_grad)
    expert_gate_grad = jnp.swapaxes(expert_gate_grad, 1, 2)
    expert_up_grad = jnp.swapaxes(expert_up_grad, 1, 2)
    kv_down_grad = all_small[:, :kd_width].reshape(8 * kd_width, 128).T.astype(F32)
    router_grad = all_small[:, kd_width:wide].reshape(8 * rt_width, 128).T.astype(F32)
    vectors = jnp.sum(all_small[:, wide : wide + 6].astype(F32), axis=0).reshape(2, 3, 128).sum(axis=0)
    norm_gain_grad = vectors[0]
    mix_gain_grad = vectors[1]
    kv_gain_grad = vectors[2, : KVRANK // count]

    factor = jnp.minimum(1.0, threshold[0] / jnp.maximum(top_peak, 1.0))
    root_factor = jnp.sqrt(factor)
    q_rows = q_weight.shape[0] // count
    own_query = lax.dynamic_slice_in_dim(q_weight, j * q_rows, q_rows, 0).astype(F32)
    query_step = (own_query - step_size[0] * q_weight_grad).reshape(q_rows, heads, NOPE + ROPE)
    q_weight_new = jnp.concatenate(
        [
            query_step[..., :NOPE] * root_factor[None, :, None],
            query_step[..., NOPE:] * factor[None, :, None],
        ],
        axis=-1,
    ).reshape(q_rows, heads * (NOPE + ROPE))
    own_up = lax.dynamic_slice_in_dim(kv_up, j * up_rows, up_rows, 0).astype(F32)
    up_step = (own_up - step_size[0] * kv_up_grad).reshape(up_rows, heads, NOPE + VDIM)
    kv_up_new = jnp.concatenate(
        [up_step[..., :NOPE] * root_factor[None, :, None], up_step[..., NOPE:]], axis=-1
    ).reshape(up_rows, heads * (NOPE + VDIM))
    return (
        layer_out,
        tokens_grad,
        q_weight_grad,
        kv_down_grad,
        kv_up_grad,
        out_weight_grad,
        router_grad,
        norm_gain_grad,
        kv_gain_grad,
        mix_gain_grad,
        shared_gate_grad,
        shared_up_grad,
        shared_down_grad,
        expert_gate_grad,
        expert_up_grad,
        expert_down_grad,
        q_weight_new,
        kv_up_new,
    )


def solution(mesh):
    fine = Mesh(mesh.devices.reshape(4, 4, 4, 2), ("z", "y", "x", "c"))
    return jax.shard_map(
        shards,
        mesh=fine,
        in_specs=(
            P(EXPERT, None),
            P(EXPERT, None),
            P(EXPERT, None),
            P(),
            P(),
            P(None, TENSOR),
            P(),
            P(),
            P(None, TENSOR),
            P(TENSOR, None),
            P(),
            P(),
            P(None, TENSOR),
            P(None, TENSOR),
            P(TENSOR, None),
            P(EXPERT, None, TENSOR),
            P(EXPERT, None, TENSOR),
            P(EXPERT, TENSOR, None),
            P(),
            P(),
        ),
        out_specs=(
            P(EXPERT, None),
            P(EXPERT, None),
            P(EXPERT, TENSOR),
            P(EXPERT, None),
            P(EXPERT, TENSOR),
            P(TENSOR, EXPERT),
            P(EXPERT, None),
            P(EXPERT),
            P(EXPERT),
            P(EXPERT),
            P(EXPERT, TENSOR),
            P(EXPERT, TENSOR),
            P(TENSOR, EXPERT),
            P(EXPERT, None, TENSOR),
            P(EXPERT, None, TENSOR),
            P(EXPERT, TENSOR, None),
            P(EXPERT, TENSOR),
            P(EXPERT, TENSOR),
        ),
        check_vma=False,
    )
```

```python
import functools
import math

import jax
import jax.numpy as jnp
from jax import lax
from jax.experimental import pallas as pl
from jax.experimental.pallas import tpu as pltpu
from jax.sharding import Mesh
from jax.sharding import PartitionSpec as P

D = 2048
HALF = D // 2
NOPE = 128
ROPE = 64
VDIM = 128
KVRANK = 512
TOPK = 6
PROMPT = 1024
CONT = 2
EXPERTS = 64
CAP = 48
SPAN = 4
RING = 4
OWN = 48
EPSILON = 1e-06

BF = jnp.bfloat16
F32 = jnp.float32
EXPERT = ("z", "y")
TENSOR = ("x", "c")


def dot(left, right, contract=((1,), (0,))):
    return lax.dot_general(left, right, (contract, ((), ())), preferred_element_type=F32)


def swap(block):
    return lax.ppermute(block, "c", [(0, 1), (1, 0)])


def shift(block, axis, step):
    return lax.ppermute(block, axis, [(i, (i + step) % RING) for i in range(RING)])


def spread(block):
    return lax.all_to_all(block, EXPERT, split_axis=0, concat_axis=0, tiled=True)


def pick_index(blocks, index, axis=0):
    return lax.dynamic_index_in_dim(blocks, index, axis, keepdims=False)


def sum_ring(blocks, axis, index):
    return sum_sent(*ring_parts(blocks, index), axis)


def ring_parts(blocks, index):
    own = pick_index(blocks, index)
    return own, [pick_index(blocks, (index + step) % RING).astype(BF) for step in (1, 2, 3)]


def sum_sent(own, parts, axis):
    for step in (1, 2, 3):
        own = own + shift(parts[step - 1], axis, step).astype(F32)
    return own


def gather_ring(block, axis, index):
    blocks = jnp.zeros((RING,) + block.shape, block.dtype)
    blocks = lax.dynamic_update_index_in_dim(blocks, block, index, 0)
    for step in (1, 2, 3):
        blocks = lax.dynamic_update_index_in_dim(
            blocks, shift(block, axis, step), (index - step) % RING, 0
        )
    return blocks


def gather_pair(block, core):
    blocks = jnp.zeros((2,) + block.shape, block.dtype)
    blocks = lax.dynamic_update_index_in_dim(blocks, block, core, 0)
    return lax.dynamic_update_index_in_dim(blocks, swap(block), 1 - core, 0)


def gather_rows(block):
    return lax.all_gather(block, TENSOR, axis=0, tiled=True)


def after(value, *others):
    return lax.optimization_barrier((value, *others))[0]


PIECE = 176
HIDDEN = RING * PIECE
SLOTS = 16 * CAP
TILE = 256
EXTRA = 128
NT = ((1,), (1,))
TN = ((0,), (0,))
VMEM_LIMIT = 56 << 20
HINT = 64


def whole(*shape):
    return pl.BlockSpec(shape, lambda *_: (0,) * len(shape))


def anywhere():
    return pl.BlockSpec(memory_space=pl.ANY)


def copy_all(pairs, sems):
    copies = [pltpu.make_async_copy(a, b, sems.at[i]) for i, (a, b) in enumerate(pairs)]
    for one in copies:
        one.start()
    for one in copies:
        one.wait()


def cost(flops, bytes_accessed, exps=0):
    return pl.CostEstimate(
        flops=int(flops) // HINT, bytes_accessed=int(bytes_accessed) // HINT, transcendentals=0
    )


OUTWARD = (208, 320)
HOMEWARD = (96, 112, 80, 240)


def spans(parts):
    found, start = [], 0
    for part, size in enumerate(parts):
        at = start
        while at < start + size:
            weight, inside = divmod(at, PIECE)
            length = min(PIECE - inside, start + size - at)
            found.append((part, at - start, weight, inside, length))
            at += length
        start += size
    return found


def pack_kernel(x_ref, *refs):
    for step in range(3):
        for part, at, weight, inside, length in spans(OUTWARD):
            out = refs[9 + step * len(OUTWARD) + part]
            out[at : at + length, :] = refs[3 * step + weight][0, inside : inside + length, :]


def pack(x, gate, up, down):
    block = 512

    def source(step):
        return pl.BlockSpec((1, PIECE, block), lambda i, x: (lax.rem(x[0] + step, RING), 0, i))

    outs = pl.pallas_call(
        pack_kernel,
        grid_spec=pltpu.PrefetchScalarGridSpec(
            num_scalar_prefetch=1,
            grid=(D // block,),
            in_specs=[source(step) for step in (1, 2, 3) for _ in range(3)],
            out_specs=[pl.BlockSpec((size, block), lambda i, _: (0, i)) for size in OUTWARD] * 3,
        ),
        out_shape=[jax.ShapeDtypeStruct((size, D), BF) for size in OUTWARD] * 3,
        compiler_params=pltpu.CompilerParams(vmem_limit_bytes=VMEM_LIMIT),
        cost_estimate=cost(0, 13 << 20),
        name="pack_weights",
    )(x.reshape(1), *((gate, up, down) * 3))
    return [outs[part :: len(OUTWARD)] for part in range(len(OUTWARD))]


def unpack_kernel(x_ref, *refs):
    outs = refs[len(HOMEWARD) * RING :]
    for step in range(RING):
        index = lax.rem(x_ref[0] + step, RING)
        for part, at, weight, inside, length in spans(HOMEWARD):
            piece = refs[part * RING + step]
            outs[weight][index, inside : inside + length, :] = piece[at : at + length, :].astype(F32)


def unpack(x, parts):
    block = 512
    return pl.pallas_call(
        unpack_kernel,
        grid_spec=pltpu.PrefetchScalarGridSpec(
            num_scalar_prefetch=1,
            grid=(D // block,),
            in_specs=[
                pl.BlockSpec((size, block), lambda i, _: (0, i))
                for size in HOMEWARD
                for _ in range(RING)
            ],
            out_specs=[pl.BlockSpec((RING, PIECE, block), lambda i, _: (0, 0, i))] * 3,
        ),
        out_shape=[jax.ShapeDtypeStruct((RING, PIECE, D), F32)] * 3,
        compiler_params=pltpu.CompilerParams(vmem_limit_bytes=VMEM_LIMIT),
        cost_estimate=cost(0, 26 << 20),
        name="unpack_gradients",
    )(x.reshape(1), *[piece for part in parts for piece in part])


def load_weight(which, index, own_ref, parts, weight):
    pairs = [(own_ref.at[index], weight.at[pl.ds(0, PIECE)])]
    for part, at, kind, inside, length in spans(OUTWARD):
        if kind == which:
            for step, piece in enumerate(parts[part]):
                start = (step + 1) * PIECE + inside
                pairs.append((piece.at[pl.ds(at, length)], weight.at[pl.ds(start, length)]))
    return pairs


def halves_of(place_ref):
    core = place_ref[1]
    return (
        pl.ds(pl.multiple_of(core * HALF, HALF), HALF),
        pl.ds(pl.multiple_of((1 - core) * HALF, HALF), HALF),
    )


def expert_kernel(
    place_ref,
    mine_ref,
    other_ref,
    grad_mine_ref,
    grad_other_ref,
    gate_ref,
    own_gate,
    own_up,
    own_down,
    p1,
    p2,
    p3,
    q1,
    q2,
    q3,
    act_ref,
    scaled_ref,
    gate_grad_ref,
    up_grad_ref,
    keep_ref,
    give_ref,
    columns_ref,
    gate_w,
    up_w,
    down_w,
    sems,
):
    @pl.when(pl.program_id(0) == 0)
    def _():
        index = place_ref[0]
        parts = {0: (p1, p2, p3), 1: (q1, q2, q3)}
        copy_all(
            load_weight(0, index, own_gate, parts, gate_w)
            + load_weight(1, index, own_up, parts, up_w)
            + load_weight(2, index, own_down, parts, down_w),
            sems,
        )

    first, second = halves_of(place_ref)
    mine, other = mine_ref[...], other_ref[...]
    extra = gate_ref[...].astype(F32)
    gate = extra[:, 0:1] + extra[:, 1:2]
    gate_lin = dot(mine, gate_w[:, first], NT) + dot(other, gate_w[:, second], NT)
    up_lin = dot(mine, up_w[:, first], NT) + dot(other, up_w[:, second], NT)
    raw = dot(grad_mine_ref[...], down_w[:, first], NT)
    raw = raw + dot(grad_other_ref[...], down_w[:, second], NT)
    sigmoid = jax.nn.sigmoid(gate_lin)
    silu = gate_lin * sigmoid
    act = (silu * up_lin).astype(BF)
    act_ref[...] = act
    act = act.astype(F32)
    scaled_ref[...] = (act * gate).astype(BF)
    act_grad = raw * gate
    gate_grad = (act_grad * up_lin * (sigmoid * (1.0 + gate_lin * (1.0 - sigmoid)))).astype(BF)
    up_grad = (act_grad * silu).astype(BF)
    gate_grad_ref[...] = gate_grad
    up_grad_ref[...] = up_grad
    keep_ref[...] = dot(gate_grad, gate_w[:, first]) + dot(up_grad, up_w[:, first])
    give_ref[...] = (dot(gate_grad, gate_w[:, second]) + dot(up_grad, up_w[:, second])).astype(BF)
    slot_grad = jnp.sum(act * raw, axis=1, keepdims=True)
    high = slot_grad.astype(BF).astype(F32)
    lane = lax.broadcasted_iota(jnp.int32, (TILE, EXTRA), 1)
    expert_id = place_ref[2]
    columns_ref[...] = jnp.where(
        lane == expert_id, high, jnp.where(lane == EXPERTS + expert_id, slot_grad - high, 0.0)
    ).astype(BF)


def expert_pass(place, mine, other, gate, up, down, packed):
    rows = lambda width, at=0: pl.BlockSpec((TILE, width), lambda i, _: (i, at))
    shape = lambda width, dtype: jax.ShapeDtypeStruct((SLOTS, width), dtype)
    return pl.pallas_call(
        expert_kernel,
        grid_spec=pltpu.PrefetchScalarGridSpec(
            num_scalar_prefetch=1,
            grid=(SLOTS // TILE,),
            in_specs=[rows(HALF)] * 2 + [rows(HALF, 1)] * 2 + [rows(EXTRA, D // EXTRA)]
            + [anywhere()] * 9,
            out_specs=[rows(HIDDEN)] * 4 + [rows(HALF)] * 2 + [rows(EXTRA)],
            scratch_shapes=[pltpu.VMEM((HIDDEN, D), BF)] * 3 + [pltpu.SemaphoreType.DMA((15,))],
        ),
        out_shape=[shape(HIDDEN, BF)] * 4
        + [shape(HALF, F32), shape(HALF, BF), shape(EXTRA, BF)],
        compiler_params=pltpu.CompilerParams(vmem_limit_bytes=VMEM_LIMIT),
        cost_estimate=cost(10 * SLOTS * D * HIDDEN, 24 << 20, SLOTS * HIDDEN),
        name="expert_pass",
    )(place, mine, other, mine, other, mine, gate, up, down, *[p for part in packed for p in part])


def produce_kernel(place_ref, act_ref, mine_ref, own_down, p1, p2, p3, keep_ref, give_ref, down, sems):
    @pl.when(pl.program_id(0) == 0)
    def _():
        copy_all(load_weight(2, place_ref[0], own_down, {1: (p1, p2, p3)}, down), sems)

    first, second = halves_of(place_ref)
    extra = mine_ref[...].astype(F32)
    gate = extra[:, 0:1] + extra[:, 1:2]
    keep_ref[...] = dot(act_ref[...], down[:, first]) * gate
    give_ref[...] = (dot(act_ref[...], down[:, second]) * gate).astype(BF)


def produce(place, act, mine, down, packed):
    rows = lambda width: pl.BlockSpec((TILE, width), lambda i, _: (i, 0))
    return pl.pallas_call(
        produce_kernel,
        grid_spec=pltpu.PrefetchScalarGridSpec(
            num_scalar_prefetch=1,
            grid=(SLOTS // TILE,),
            in_specs=[
                rows(HIDDEN),
                pl.BlockSpec((TILE, EXTRA), lambda i, _: (i, D // EXTRA)),
            ]
            + [anywhere()] * 4,
            out_specs=[rows(HALF)] * 2,
            scratch_shapes=[pltpu.VMEM((HIDDEN, D), BF), pltpu.SemaphoreType.DMA((4,))],
        ),
        out_shape=[
            jax.ShapeDtypeStruct((SLOTS, HALF), F32),
            jax.ShapeDtypeStruct((SLOTS, HALF), BF),
        ],
        compiler_params=pltpu.CompilerParams(vmem_limit_bytes=VMEM_LIMIT),
        cost_estimate=cost(2 * SLOTS * D * HIDDEN, 9 << 20),
        name="produce",
    )(place, act, mine, down, *packed[1])


def weight_grad_kernel(place_ref, *refs, weights, parts):
    lefts = refs[: len(weights)]
    rights, outs = refs[len(weights) : -len(parts) * RING], refs[-len(parts) * RING :]
    own = pl.program_id(0) < 2
    rights = [jnp.where(own, rights[i][...], rights[i + 1][...]) for i in range(0, len(rights), 2)]
    for left, weight in zip(lefts, weights):
        right = rights[1] if weight == 2 and len(rights) > 1 else rights[0]
        product = dot(left[...], right, TN).astype(BF)
        for step in range(RING):
            for part, at, kind, inside, length in spans(HOMEWARD):
                if kind == weight:
                    start = step * PIECE + inside
                    out = outs[parts.index(part) * RING + step]
                    out[at : at + length, :] = product[start : start + length, :]


def weight_grads(place, weights, parts, lefts, rows):
    block = HALF // 2
    mine = [pl.BlockSpec((SLOTS, block), lambda i, _, at=at: (0, at + jnp.minimum(i, 1))) for at in (0, 2)]
    other = [
        pl.BlockSpec((SLOTS, block), lambda i, _, at=at: (0, at + jnp.maximum(i - 2, 0)))
        for at in (0, 2)
    ]
    sizes = [HOMEWARD[part] for part in parts for _ in range(RING)]
    outs = pl.pallas_call(
        functools.partial(weight_grad_kernel, weights=weights, parts=parts),
        grid_spec=pltpu.PrefetchScalarGridSpec(
            num_scalar_prefetch=1,
            grid=(4,),
            in_specs=[whole(SLOTS, HIDDEN)] * len(lefts)
            + [mine[0], other[0], mine[1], other[1]],
            out_specs=[
                pl.BlockSpec((size, block), lambda i, place: (0, lax.rem(2 * place[1] + i, 4)))
                for size in sizes
            ],
        ),
        out_shape=[jax.ShapeDtypeStruct((size, D), BF) for size in sizes],
        compiler_params=pltpu.CompilerParams(vmem_limit_bytes=VMEM_LIMIT),
        cost_estimate=cost(2 * len(lefts) * SLOTS * D * HIDDEN, 18 << 20),
        name="weight_grads",
    )(place, *lefts, *rows, *rows)
    return [outs[i * RING : (i + 1) * RING] for i in range(len(parts))]


SHARED = 352
WIDE = 384
ATT = 2 * VDIM


def shared_kernel(mixed, out_grad, gate_w, up_w, down_w, part, mixed_grad, grads):
    gate_lin = dot(mixed[...], gate_w[...], NT)
    up_lin = dot(mixed[...], up_w[...], NT)
    sigmoid = jax.nn.sigmoid(gate_lin)
    silu = gate_lin * sigmoid
    act = (silu * up_lin).astype(BF)
    act_grad = dot(out_grad[...], down_w[...], NT)
    gate_grad = (act_grad * up_lin * (sigmoid * (1.0 + gate_lin * (1.0 - sigmoid)))).astype(BF)
    up_grad = (act_grad * silu).astype(BF)
    for start in range(0, D, 512):
        at = slice(start, start + 512)
        part[:, at] = dot(act, down_w[:, at])
        mixed_grad[:, at] = dot(gate_grad, gate_w[:, at]) + dot(up_grad, up_w[:, at])
        zeros = jnp.zeros((512, WIDE - SHARED), BF)
        for i, (left, right) in enumerate(((mixed, gate_grad), (mixed, up_grad), (out_grad, act))):
            start = i * WIDE
            grads[at, start : start + SHARED] = dot(left[:, at], right, TN).astype(BF)
            grads[at, start + SHARED : start + WIDE] = zeros


def shared_experts(mixed, out_grad, gate_w, up_w, down_w):
    args = (mixed, out_grad, gate_w, up_w, down_w)
    rows = mixed.shape[0]
    outs = [
        jax.ShapeDtypeStruct((rows, D), F32),
        jax.ShapeDtypeStruct((rows, D), F32),
        jax.ShapeDtypeStruct((D, 3 * WIDE), BF),
    ]
    return pl.pallas_call(
        shared_kernel,
        grid=(1,),
        in_specs=[whole(*arg.shape) for arg in args],
        out_specs=[whole(*out.shape) for out in outs],
        out_shape=outs,
        compiler_params=pltpu.CompilerParams(vmem_limit_bytes=VMEM_LIMIT),
        cost_estimate=cost(18 * rows * D * SHARED, 18 << 20, rows * SHARED),
        name="shared_experts",
    )(*args)


GROUP = 1536
ROWS = 384
LATENT = KVRANK + ROPE
HEADS = 2
HEAD = NOPE + ROPE
SCALE = 1.0 / math.sqrt(HEAD)


def turn(block, cosine, sine):
    half = ROPE // 2
    return block * cosine + jnp.concatenate([block[:, half:], block[:, :half]], axis=1) * sine


def mask_bias(seg_keys, seg_rows, row_start):
    key = lax.broadcasted_iota(jnp.int32, (GROUP, ROWS), 0)
    row = lax.broadcasted_iota(jnp.int32, (GROUP, ROWS), 1) + row_start
    same = (seg_keys == seg_rows) & (key <= row)
    return jnp.where(same | ((seg_keys == 0) & (seg_rows > 0)), 0.0, -1e30)


def wide_tables(cos, sin):
    return jnp.concatenate([cos, cos], axis=1), jnp.concatenate([-sin, sin], axis=1)


def row_tables(cos_ref, sin_ref, row_start):
    at = pl.ds(pl.multiple_of(row_start, ROWS), ROWS)
    return wide_tables(cos_ref[at, :], sin_ref[at, :])


def head_queries(query, row_cos, row_sin, head):
    start = head * HEAD
    plain = query[:, start : start + NOPE].astype(BF)
    return plain, turn(query[:, start + NOPE : start + HEAD], row_cos, row_sin).astype(BF)


def attention_kernel(
    place_ref,
    mine_ref,
    other_ref,
    query_ref,
    gain_ref,
    kv_up_ref,
    out_weight_ref,
    cos_ref,
    sin_ref,
    seg_keys_ref,
    seg_rows_ref,
    give_ref,
    keep_ref,
    attended_ref,
    compressed_ref,
    kv_ref,
    key_rot_ref,
    log_total_ref,
    peak_ref,
    latent,
    attended,
):
    core = place_ref[1]
    half = ROWS // 2
    for block in range(SPAN):
        start = pl.multiple_of(block * ROWS + core * half, half)
        latent[pl.ds(start, half), :] = mine_ref[block]
        start = pl.multiple_of(block * ROWS + (1 - core) * half, half)
        latent[pl.ds(start, half), :] = other_ref[block]
    inputs = latent[:, :KVRANK].astype(F32)
    inverse = lax.rsqrt(jnp.mean(inputs * inputs, axis=1, keepdims=True) + EPSILON)
    compressed_ref[...] = (inputs * inverse * gain_ref[...]).astype(BF)
    kv_ref[...] = dot(compressed_ref[...], kv_up_ref[...]).astype(BF)
    cosine, sine = wide_tables(cos_ref[...], sin_ref[...])
    key_rot_ref[...] = turn(latent[:, KVRANK:].astype(F32), cosine, sine).astype(BF)
    seg_rows = seg_rows_ref[:, pl.ds(pl.multiple_of(place_ref[3], ROWS), ROWS)]
    bias = mask_bias(seg_keys_ref[...], seg_rows, place_ref[3])
    row_cos, row_sin = row_tables(cos_ref, sin_ref, place_ref[3])
    for head in range(HEADS):
        plain, turned = head_queries(query_ref, row_cos, row_sin, head)
        start = head * (NOPE + VDIM)
        scores = dot(kv_ref[:, start : start + NOPE], plain, NT)
        scores = (scores + dot(key_rot_ref[...], turned, NT)) * SCALE + bias
        peak = jnp.max(scores, axis=0, keepdims=True)
        powers = jnp.exp(scores - peak)
        total = jnp.sum(powers, axis=0, keepdims=True)
        log_total_ref[head : head + 1, :] = peak + jnp.log(total)
        peak_ref[head : head + 1, :] = peak
        weights = (powers * (1.0 / total)).astype(BF)
        values = kv_ref[:, start + NOPE : start + NOPE + VDIM]
        attended[:, head * VDIM : (head + 1) * VDIM] = dot(values, weights, TN).T
    attended_ref[...] = attended[...].astype(BF)
    for block in range(RING):
        for out, which in ((give_ref, 1 - core), (keep_ref, core)):
            start = pl.multiple_of(block * 2 * OWN + which * OWN, OWN)
            out[block] = dot(
                attended[pl.ds(start, OWN), :].astype(BF), out_weight_ref[...]
            ).astype(out.dtype)


def attention(place, mine, other, query, gain, kv_up, out_weight, tables, segs):
    shape = jax.ShapeDtypeStruct
    args = (mine, other, query, gain.reshape(1, KVRANK), kv_up, out_weight, *tables, *segs)
    outs = [
        shape((RING, OWN, D), BF),
        shape((RING, OWN, D), F32),
        shape((ROWS, HEADS * VDIM), BF),
        shape((GROUP, KVRANK), BF),
        shape((GROUP, HEADS * (NOPE + VDIM)), BF),
        shape((GROUP, ROPE), BF),
        shape((HEADS, ROWS), F32),
        shape((HEADS, ROWS), F32),
    ]
    return pl.pallas_call(
        attention_kernel,
        grid_spec=pltpu.PrefetchScalarGridSpec(
            num_scalar_prefetch=1,
            grid=(1,),
            in_specs=[whole(*arg.shape) for arg in args],
            out_specs=[whole(*out.shape) for out in outs],
            scratch_shapes=[
                pltpu.VMEM((GROUP, LATENT), BF),
                pltpu.VMEM((ROWS, HEADS * VDIM), F32),
            ],
        ),
        out_shape=outs,
        compiler_params=pltpu.CompilerParams(vmem_limit_bytes=VMEM_LIMIT),
        cost_estimate=cost(3e9, 14 << 20, 2 * GROUP * ROWS),
        name="attention_forward",
    )(place, *args)


def attention_back_kernel(
    place_ref,
    mine_ref,
    other_ref,
    query_ref,
    compressed_ref,
    kv_ref,
    key_rot_ref,
    log_total_ref,
    kv_up_ref,
    out_weight_ref,
    cos_ref,
    sin_ref,
    seg_keys_ref,
    seg_rows_ref,
    q_weight_ref,
    give_ref,
    keep_ref,
    kv_grad_ref,
    query_grad_ref,
    branch_ref,
    normed_give_ref,
    normed_keep_ref,
    comp_grad,
    rot_grad,
):
    core = place_ref[1]
    interleave(core, mine_ref, other_ref, branch_ref, D + EXTRA)
    attended_grad = dot(branch_ref[:, :D], out_weight_ref[...], NT).astype(BF)
    seg_rows = seg_rows_ref[:, pl.ds(pl.multiple_of(place_ref[3], ROWS), ROWS)]
    bias = mask_bias(seg_keys_ref[...], seg_rows, place_ref[3])
    row_cos, row_sin = row_tables(cos_ref, sin_ref, place_ref[3])
    turned_sum = 0.0
    query_grads = []
    for head in range(HEADS):
        plain, turned = head_queries(query_ref, row_cos, row_sin, head)
        start = head * (NOPE + VDIM)
        keys = kv_ref[:, start : start + NOPE]
        values = kv_ref[:, start + NOPE : start + NOPE + VDIM]
        key_rot = key_rot_ref[...]
        scores = (dot(keys, plain, NT) + dot(key_rot, turned, NT)) * SCALE + bias
        probs = jnp.exp(scores - log_total_ref[head : head + 1, :])
        grad = attended_grad[:, head * VDIM : (head + 1) * VDIM]
        value_grad = dot(probs.astype(BF), grad)
        prob_grad = dot(values, grad, NT)
        inner = jnp.sum(probs * prob_grad, axis=0, keepdims=True)
        score_grad = (probs * (prob_grad - inner)).astype(BF)
        kv_grad_ref[:, start : start + NOPE] = (dot(score_grad, plain) * SCALE).astype(BF)
        kv_grad_ref[:, start + NOPE : start + NOPE + VDIM] = value_grad.astype(BF)
        turned_sum = turned_sum + dot(score_grad, turned) * SCALE
        query_grads.append((dot(keys, score_grad, TN) * SCALE).T)
        turned_grad = (dot(key_rot, score_grad, TN) * SCALE).T
        query_grads.append(turn(turned_grad, row_cos, -row_sin))
    comp_grad[...] = dot(kv_grad_ref[...], kv_up_ref[...], NT)
    cosine, sine = wide_tables(cos_ref[...], sin_ref[...])
    rot_grad[...] = turn(turned_sum, cosine, -sine)
    for block in range(SPAN):
        for inner in range(RING):
            for out, which in ((give_ref, 1 - core), (keep_ref, core)):
                start = pl.multiple_of(block * ROWS + inner * 2 * OWN + which * OWN, OWN)
                out[block, inner, :, :KVRANK] = comp_grad[pl.ds(start, OWN), :].astype(out.dtype)
                out[block, inner, :, KVRANK:] = rot_grad[pl.ds(start, OWN), :].astype(out.dtype)
    query_grad_ref[...] = jnp.concatenate(query_grads, axis=1).astype(BF)
    for block in range(RING):
        for out, which in ((normed_give_ref, 1 - core), (normed_keep_ref, core)):
            start = pl.multiple_of(block * 2 * OWN + which * OWN, OWN)
            part = query_grad_ref[pl.ds(start, OWN), :]
            out[block] = dot(part, q_weight_ref[...], NT).astype(out.dtype)


def attention_back(
    place, mine, other, query, compressed, kv, key_rot, log_total, kv_up, out_weight, tables, segs,
    q_weight,
):
    shape = jax.ShapeDtypeStruct
    args = (
        mine, other, query, compressed, kv, key_rot, log_total, kv_up, out_weight, *tables, *segs,
        q_weight,
    )
    outs = [
        shape((SPAN, RING, OWN, LATENT), BF),
        shape((SPAN, RING, OWN, LATENT), F32),
        shape((GROUP, HEADS * (NOPE + VDIM)), BF),
        shape((ROWS, HEADS * HEAD), BF),
        shape((ROWS, D + EXTRA), BF),
        shape((RING, OWN, D), BF),
        shape((RING, OWN, D), F32),
    ]
    return pl.pallas_call(
        attention_back_kernel,
        grid_spec=pltpu.PrefetchScalarGridSpec(
            num_scalar_prefetch=1,
            grid=(1,),
            in_specs=[whole(*arg.shape) for arg in args],
            out_specs=[whole(*out.shape) for out in outs],
            scratch_shapes=[pltpu.VMEM((GROUP, KVRANK), F32), pltpu.VMEM((GROUP, ROPE), F32)],
        ),
        out_shape=outs,
        compiler_params=pltpu.CompilerParams(vmem_limit_bytes=VMEM_LIMIT),
        cost_estimate=cost(4e9, 16 << 20, 2 * GROUP * ROWS),
        name="attention_backward",
    )(place, *args)


UP_ROWS = KVRANK // 16
BIG = HEADS * HEAD + ATT + 128


def projection_grad_kernel(
    normed, branch, compressed, query_grad, attended, kv_grad, out
):
    width = HEADS * HEAD
    out[:, :width] = dot(normed[...], query_grad[...], TN).astype(BF)
    out[:, width : width + ATT] = dot(branch[...], attended[...], TN).astype(BF)
    up = dot(compressed[...], kv_grad[...], TN)
    for index in range(4):
        for part in range(4):
            start = index * 128 + part * UP_ROWS
            out[start : start + UP_ROWS, width + ATT :] = up[
                index * UP_ROWS : (index + 1) * UP_ROWS, part * 128 : (part + 1) * 128
            ].astype(BF)


def projection_grads(normed, branch, compressed, query_grad, attended, kv_grad):
    block = 512
    return pl.pallas_call(
        projection_grad_kernel,
        grid=(D // block,),
        in_specs=[
            pl.BlockSpec((ROWS, block), lambda i: (0, i)),
            pl.BlockSpec((ROWS, block), lambda i: (0, i)),
            pl.BlockSpec((GROUP, 128), lambda i: (0, i)),
            whole(ROWS, HEADS * HEAD),
            whole(ROWS, ATT),
            whole(GROUP, HEADS * (NOPE + VDIM)),
        ],
        out_specs=pl.BlockSpec((block, BIG), lambda i: (i, 0)),
        out_shape=jax.ShapeDtypeStruct((D, BIG), BF),
        compiler_params=pltpu.CompilerParams(vmem_limit_bytes=VMEM_LIMIT),
        cost_estimate=cost(2e9, 10 << 20),
        name="projection_grads",
    )(normed, branch, compressed, query_grad, attended, kv_grad)


def combine_kernel(place_ref, pick_ref, returned_ref, shared_ref, give_ref, keep_ref, total):
    core = place_ref[1]
    rows = dot(pick_ref[...], returned_ref[...], TN)
    total[:, :D] = shared_ref[...]
    mine = pl.ds(pl.multiple_of(core * HALF, HALF), HALF)
    total[:, mine] = total[:, mine] + rows[:, :HALF]
    if returned_ref.shape[1] > HALF:
        total[:, D:] = rows[:, HALF:]
    for block in range(RING):
        for out, which in ((give_ref, 1 - core), (keep_ref, core)):
            start = pl.multiple_of(block * 2 * OWN + which * OWN, OWN)
            out[block] = total[pl.ds(start, OWN), :].astype(out.dtype)


def combine_rows(place, pick, returned, shared):
    width = D + returned.shape[1] - HALF
    args = (pick, returned, shared)
    outs = [
        jax.ShapeDtypeStruct((RING, OWN, width), BF),
        jax.ShapeDtypeStruct((RING, OWN, width), F32),
    ]
    return pl.pallas_call(
        combine_kernel,
        grid_spec=pltpu.PrefetchScalarGridSpec(
            num_scalar_prefetch=1,
            grid=(1,),
            in_specs=[whole(*arg.shape) for arg in args],
            out_specs=[whole(*out.shape) for out in outs],
            scratch_shapes=[pltpu.VMEM((ROWS, width), F32)],
        ),
        out_shape=outs,
        compiler_params=pltpu.CompilerParams(vmem_limit_bytes=VMEM_LIMIT),
        cost_estimate=cost(7e8, 8 << 20),
        name="combine_rows",
    )(place, *args)


def order_kernel(x_ref, *refs):
    for step in range(RING):
        refs[RING][lax.rem(x_ref[0] + RING - step, RING)] = refs[step][...]


def order_ring(x, blocks):
    rows, width = blocks[0].shape
    return pl.pallas_call(
        order_kernel,
        grid_spec=pltpu.PrefetchScalarGridSpec(
            num_scalar_prefetch=1,
            grid=(1,),
            in_specs=[whole(rows, width)] * RING,
            out_specs=whole(RING, rows, width),
        ),
        out_shape=jax.ShapeDtypeStruct((RING, rows, width), blocks[0].dtype),
        cost_estimate=cost(0, 2 << 20),
        name="order_ring",
    )(x.reshape(1), *blocks)


def interleave(core, mine_ref, other_ref, out, width):
    for block in range(RING):
        for ref, which in ((mine_ref, core), (other_ref, 1 - core)):
            start = pl.multiple_of(block * 2 * OWN + which * OWN, OWN)
            out[pl.ds(start, OWN), :] = ref[block, :, :width]


def gating_kernel(
    place_ref, mine_ref, other_ref, router_ref, pick_ref, grad_ref, mixed_ref, probs_ref, sent_ref
):
    core = place_ref[1]
    interleave(core, mine_ref, other_ref, mixed_ref, D)
    logits = dot(mixed_ref[...], router_ref[...])
    powers = jnp.exp(logits - jnp.max(logits, axis=1, keepdims=True))
    probs = powers / jnp.sum(powers, axis=1, keepdims=True)
    probs_ref[...] = probs
    pick = pick_ref[...]
    high = probs.astype(BF)
    rest = probs - high.astype(F32)
    middle = rest.astype(BF)
    low = (rest - middle.astype(F32)).astype(BF)
    gates = dot(pick, high) + dot(pick, middle) + dot(pick, low)
    slot = lax.broadcasted_iota(jnp.int32, (SLOTS, EXPERTS), 0)
    lane = lax.broadcasted_iota(jnp.int32, (SLOTS, EXPERTS), 1)
    first = (lane - place_ref[0]) * (CAP // 4)
    inside = (slot >= first) & (slot < first + CAP) & (lax.rem(lane, 4) == place_ref[0])
    gate = jnp.sum(jnp.where(inside, gates, 0.0), axis=1, keepdims=True)
    high = gate.astype(BF).astype(F32)
    lane = lax.broadcasted_iota(jnp.int32, (SLOTS, EXTRA), 1)
    sent_ref[:, D:] = jnp.where(
        lane == 0, high, jnp.where(lane == 1, gate - high, 0.0)
    ).astype(BF)
    mine = pl.ds(pl.multiple_of(core * HALF, HALF), HALF)
    sent_ref[:, :HALF] = dot(pick, mixed_ref[:, mine]).astype(BF)
    sent_ref[:, HALF:D] = dot(pick, grad_ref[:, mine]).astype(BF)


def gating(place, mine, other, router, pick, out_grad):
    args = (mine, other, router, pick, out_grad)
    outs = [
        jax.ShapeDtypeStruct((ROWS, D), BF),
        jax.ShapeDtypeStruct((ROWS, EXPERTS), F32),
        jax.ShapeDtypeStruct((SLOTS, D + EXTRA), BF),
    ]
    return pl.pallas_call(
        gating_kernel,
        grid_spec=pltpu.PrefetchScalarGridSpec(
            num_scalar_prefetch=1,
            grid=(1,),
            in_specs=[whole(*arg.shape) for arg in args],
            out_specs=[whole(*out.shape) for out in outs],
        ),
        out_shape=outs,
        compiler_params=pltpu.CompilerParams(vmem_limit_bytes=VMEM_LIMIT),
        cost_estimate=cost(8e8, 6 << 20),
        name="gating",
    )(place, *args)


KD_COLUMNS = LATENT // 8
ROUTER_COLUMNS = EXPERTS // 8
SHARE = KD_COLUMNS + ROUTER_COLUMNS
SMALL = SHARE + 16


def small_kernel(latent, logit, normed, mixed, norm_gain, mix_gain, kv_gain, peak_ref, out):
    kv_down = dot(latent[...], normed[...], TN)
    router = dot(logit[...], mixed[...], TN)
    lane = lax.broadcasted_iota(jnp.int32, (1, 128), 1)
    peak = 0.0
    for head in range(HEADS):
        highest = jnp.max(peak_ref[head : head + 1, :], axis=1, keepdims=True)
        peak = jnp.where(lane == head, highest, peak)

    def parts(row, number):
        found = []
        for _ in range(number):
            found.append(row.astype(BF).astype(F32))
            row = row - found[-1]
        return found

    peaks = parts(peak, 3)
    zeros = jnp.zeros((7, 128), F32)
    for index in range(16):
        at = slice(index * 128, (index + 1) * 128)
        gain = kv_gain[:, index * UP_ROWS : (index + 1) * UP_ROWS]
        gain = jnp.concatenate([gain, jnp.zeros((1, 128 - UP_ROWS), F32)], axis=1)
        rows = parts(norm_gain[:, at], 2) + parts(mix_gain[:, at], 2) + parts(gain, 2)
        rows = [kv_down[:, at], router[:, at]] + rows + peaks + [zeros]
        out[index] = jnp.concatenate(rows, axis=0).astype(BF)


def small_grads(latent, logit, normed, mixed, norm_gain, mix_gain, kv_gain, peak):
    args = (
        latent,
        logit,
        normed,
        mixed,
        norm_gain.reshape(1, D),
        mix_gain.reshape(1, D),
        kv_gain.reshape(1, KVRANK),
        peak,
    )
    return pl.pallas_call(
        small_kernel,
        grid=(1,),
        in_specs=[whole(*arg.shape) for arg in args],
        out_specs=whole(16, SMALL, 128),
        out_shape=jax.ShapeDtypeStruct((16, SMALL, 128), BF),
        compiler_params=pltpu.CompilerParams(vmem_limit_bytes=VMEM_LIMIT),
        cost_estimate=cost(2e8, 4 << 20),
        name="small_grads",
    )(*args)


def split_two(value):
    high = lax.reduce_precision(value, 8, 7)
    return high.astype(BF), (value - high).astype(BF)


def norm_rows(inputs, gain_vec):
    inverse = lax.rsqrt(jnp.mean(inputs * inputs, axis=-1, keepdims=True) + EPSILON)
    return (inputs * inverse * gain_vec, inverse)


def norm_back(inputs, inverse, gain_vec, gradient):
    weighted = gradient * gain_vec
    inner = jnp.mean(weighted * inputs, axis=-1, keepdims=True)
    d_inputs = inverse * weighted - inputs * (inverse * inverse * inverse) * inner
    return (d_inputs, jnp.sum(gradient * inputs * inverse, axis=0))


def rotate(inputs, cosine, sine):
    half_size = inputs.shape[-1] // 2
    first_half = inputs[..., :half_size]
    second_half = inputs[..., half_size:]
    return jnp.concatenate(
        [first_half * cosine - second_half * sine, second_half * cosine + first_half * sine],
        axis=-1,
    )


def unrotate(gradient, cosine, sine):
    return rotate(gradient, cosine, -sine)


def shards(
    tokens,
    out_grad,
    routes,
    segment,
    norm_gain,
    q_weight,
    kv_down,
    kv_gain,
    kv_up,
    out_weight,
    mix_gain,
    router,
    shared_gate,
    shared_up,
    shared_down,
    expert_gate,
    expert_up,
    expert_down,
    step_size,
    threshold,
):
    rows = tokens.shape[0]
    x = lax.axis_index("x")
    c = lax.axis_index("c")
    y = lax.axis_index("y")
    z = lax.axis_index("z")
    j = z * RING + y
    t = x * 2 + c
    heads = q_weight.shape[1] // (NOPE + ROPE)
    group_len = rows * SPAN
    count = expert_down.shape[0] * 4
    score_scale = 1.0 / math.sqrt(NOPE + ROPE)
    own_start = t * OWN

    def own_rows(array):
        return lax.dynamic_slice_in_dim(array, own_start, OWN, 0)

    routes_t = routes.T
    chosen = 4 * jnp.arange(count, dtype=jnp.int32) + x
    hot = jnp.any(routes_t[None, :, :] == chosen[:, None, None], axis=1)
    number = jnp.arange(rows, dtype=jnp.int32)
    earlier = (number[:, None] < number[None, :]).astype(BF)
    slot = dot(hot.astype(BF), earlier)
    pick = hot[:, None, :] & (slot[:, None, :] == jnp.arange(CAP, dtype=F32)[None, :, None])
    pick_b = pick.astype(BF).reshape(count * CAP, rows)

    place = jnp.stack([x, c, 4 * j + x, y * rows]).astype(jnp.int32)

    def send_rows(sent):
        width = sent.shape[1]
        return spread(sent.reshape(count, CAP, width)).reshape(count * CAP, width)

    gate_t = jnp.swapaxes(expert_gate, 1, 2)
    up_t = jnp.swapaxes(expert_up, 1, 2)
    first_part, last_part = pack(x, gate_t, up_t, expert_down)
    first_part = [shift(first_part[step - 1], "x", step) for step in (1, 2, 3)]

    group_ids = lax.dynamic_slice_in_dim(segment, z * group_len, group_len)
    key_number = jnp.arange(group_len, dtype=jnp.int32)
    first_length = jnp.sum((group_ids == 1).astype(jnp.int32))
    key_place = jnp.where(
        group_ids == 0,
        key_number - (group_len - PROMPT),
        key_number + PROMPT - jnp.where(group_ids == 1, 0, first_length),
    )
    frequency = jnp.power(10000.0, -2.0 * jnp.arange(ROPE // 2, dtype=F32) / ROPE)
    key_angle = key_place.astype(F32)[:, None] * frequency[None, :]
    tables = (jnp.cos(key_angle), jnp.sin(key_angle))
    segs = (group_ids.reshape(group_len, 1), group_ids.reshape(1, group_len))

    x_input = after(tokens, last_part[0]).astype(F32)
    normed_f, _ = norm_rows(x_input, norm_gain)
    normed = normed_f.astype(BF)
    latent = dot(normed, kv_down).astype(BF)
    half_latent = lax.dynamic_slice_in_dim(latent, c * (rows // 2), rows // 2, 0)
    gathered = gather_ring(half_latent, "y", y)
    query_lin = dot(normed, q_weight)
    attn_give, attn_keep, attended_b, compressed, kv_rows, key_rot, log_total, row_peak = attention(
        place, gathered, swap(gathered), query_lin, kv_gain, kv_up, out_weight, tables, segs
    )

    attn_got = swap(after(attn_give, *first_part))
    attn_own, attn_sent = ring_parts(attn_keep + attn_got.astype(F32), x)
    residual = own_rows(tokens).astype(F32) + sum_sent(attn_own, attn_sent, "x")
    mixed_f, inverse_two = norm_rows(residual, mix_gain)
    mixed_own = mixed_f.astype(BF)
    mixed_ring = [mixed_own] + [shift(mixed_own, "x", step) for step in (1, 2, 3)]
    mixed_mine = order_ring(x, mixed_ring)
    last_part = [after(piece, mixed_mine) for piece in last_part]
    last_part = [shift(last_part[step - 1], "x", step) for step in (1, 2, 3)]
    packed = (first_part, last_part)
    mixed_other = swap(mixed_mine)

    mixed_in, gate_probs, mixed_sent = gating(
        place, mixed_mine, mixed_other, router, pick_b, out_grad
    )
    mixed_rows = send_rows(mixed_sent)
    shared_part, shared_mixed_grad, shared_grads = shared_experts(
        after(mixed_in, mixed_sent), out_grad, shared_gate.T, shared_up.T, shared_down
    )
    mixed_rows = after(mixed_rows, shared_part, *last_part)
    mixed_rows = (mixed_rows, swap(mixed_rows))
    expert_act, scaled_act, gate_lin_grad, up_lin_grad, grad_keep, grad_give, slot_cols = (
        expert_pass(place, *mixed_rows, gate_t, up_t, expert_down, packed)
    )

    grad_half = (grad_keep + swap(grad_give).astype(F32)).astype(BF)
    sent_grad = jnp.concatenate([grad_half, slot_cols], axis=1)
    returned_grad = send_rows(sent_grad)
    parts = weight_grads(
        place,
        (0, 1, 2),
        (0, 1, 2, 3),
        (gate_lin_grad, up_lin_grad, after(scaled_act, sent_grad)),
        mixed_rows,
    )

    def send_home(part):
        return [part[0]] + [shift(part[step], "x", RING - step) for step in (1, 2, 3)]

    home = [send_home(parts[0])]
    produced_keep, produced_give = produce(
        place, after(expert_act, parts[0][0]), mixed_rows[0], expert_down, packed
    )
    mixed_give, mixed_keep = combine_rows(
        place, pick_b, after(returned_grad, parts[0][0], produced_give), shared_mixed_grad
    )
    mixed_half = mixed_keep + swap(after(mixed_give, *home[0])).astype(F32)
    mixed_half, mixed_sent = ring_parts(mixed_half, x)
    shared_grads = lax.psum_scatter(
        after(shared_grads, mixed_rows[0]), EXPERT, scatter_dimension=0, tiled=True
    )
    produced_half = (produced_keep + swap(produced_give).astype(F32)).astype(BF)
    produced = send_rows(after(produced_half, *mixed_sent))
    mixed_total = sum_sent(mixed_half, mixed_sent, "x")
    prob_grad = mixed_total[:, D : D + EXPERTS] + mixed_total[:, D + EXPERTS :]
    own_probs = own_rows(gate_probs)
    logit_grad = (
        own_probs * (prob_grad - jnp.sum(own_probs * prob_grad, axis=-1, keepdims=True))
    ).astype(BF)
    mixed_grad = mixed_total[:, :D] + dot(logit_grad, router, ((1,), (1,)))
    mid_norm_grad, mix_gain_grad = norm_back(residual, inverse_two, mix_gain, mixed_grad)
    mid_grad = own_rows(out_grad).astype(F32) + mid_norm_grad
    branch_own = jnp.concatenate(
        [mid_grad.astype(BF), logit_grad, jnp.zeros((OWN, 128 - EXPERTS), BF)], axis=1
    )
    branch_ring = [branch_own] + [shift(branch_own, "x", step) for step in (1, 2, 3)]
    branch_mine = order_ring(x, branch_ring)
    home.append(send_home([after(piece, branch_mine) for piece in parts[1]]))
    (
        latent_give, latent_keep, kv_grad, query_lin_grad, branch_all, normed_give, normed_keep,
    ) = attention_back(
        place, branch_mine, swap(branch_mine), query_lin, compressed, kv_rows, key_rot, log_total, kv_up, out_weight,
        tables, segs, q_weight,
    )
    latent_give = after(latent_give, produced, *home[1])
    latent_sent = (latent_keep + swap(latent_give).astype(F32)).astype(BF)
    latent_parts = lax.all_to_all(
        latent_sent.reshape(SPAN * RING, OWN, LATENT), ("y", "x"), split_axis=0, concat_axis=0,
        tiled=True,
    )
    latent_total = jnp.sum(latent_parts.astype(F32), axis=0)
    normed_half = normed_keep + swap(after(normed_give, latent_sent)).astype(F32)
    normed_own, normed_sent = ring_parts(normed_half, x)
    normed_total = sum_sent(normed_own, normed_sent, "x")

    logit_grad_all = branch_all[:, D : D + EXPERTS]
    own_comp = own_rows(latent)[:, :KVRANK].astype(F32)
    _, own_inverse = norm_rows(own_comp, kv_gain)
    comp_own_grad, kv_gain_grad = norm_back(
        own_comp, own_inverse, kv_gain, latent_total[:, :KVRANK]
    )
    latent_grad = jnp.concatenate([comp_own_grad, latent_total[:, KVRANK:]], axis=-1).astype(BF)
    latent_columns = jnp.swapaxes(latent_grad.reshape(OWN, 8, KD_COLUMNS), 0, 1)
    big = projection_grads(
        normed, branch_all, compressed, query_lin_grad, attended_b, after(kv_grad, latent_columns)
    )
    latent_columns = lax.all_to_all(
        latent_columns, TENSOR, split_axis=0, concat_axis=0, tiled=True
    )
    normed_grad = normed_total + dot(latent_grad, kv_down, ((1,), (1,)))
    own_input = own_rows(tokens).astype(F32)
    _, inverse_one = norm_rows(own_input, norm_gain)
    input_norm_grad, norm_gain_grad = norm_back(own_input, inverse_one, norm_gain, normed_grad)


    up_rows = UP_ROWS
    kd_width = KD_COLUMNS
    rt_width = ROUTER_COLUMNS
    small = small_grads(
        latent_columns.reshape(rows, kd_width),
        lax.dynamic_slice_in_dim(logit_grad_all, t * rt_width, rt_width, 1),
        normed,
        mixed_in,
        norm_gain_grad,
        mix_gain_grad,
        kv_gain_grad,
        row_peak,
    )
    small = jnp.swapaxes(small.reshape(count, 6, 16, 128), 1, 2).reshape(count, 16, BIG)
    packed_grads = jnp.concatenate([big.reshape(count, 128, BIG), small], axis=1)
    home.append(send_home([after(piece, *normed_sent) for piece in parts[2]]))
    packed_grads = after(packed_grads, *home[2])
    packed_sent = packed_grads
    packed_grads = spread(packed_grads)
    small = jnp.swapaxes(packed_grads[:, 128:].reshape(count, 16, 6, 128), 1, 2)
    small = small.reshape(count, SMALL, 128)
    layer_give, layer_keep = combine_rows(
        place, pick_b, after(produced, packed_sent), shared_part
    )
    layer_half = layer_keep + swap(layer_give).astype(F32)
    home.append(send_home([after(piece, packed_sent) for piece in parts[3]]))
    layer_total = residual + sum_ring(after(layer_half, *home[3]), "x", x)
    layer_out = gather_rows(layer_total.astype(BF))
    tokens_grad = gather_rows((mid_grad + input_norm_grad).astype(BF)).astype(F32)
    shared_sum = after(shared_grads, layer_total).astype(F32)
    shared_gate_grad = shared_sum[:, :SHARED]
    shared_up_grad = shared_sum[:, WIDE : WIDE + SHARED]
    shared_down_grad = shared_sum[:, 2 * WIDE : 2 * WIDE + SHARED].T
    big = jnp.sum(packed_grads[:, :128].astype(F32), axis=0)
    q_width = q_weight.shape[1]
    q_weight_grad = big[:, :q_width]
    out_weight_grad = big[:, q_width : q_width + ATT].T
    kv_up_grad = jnp.swapaxes(big[:, q_width + ATT :].reshape(4, up_rows, 128), 0, 1).reshape(
        up_rows, 4 * 128
    )

    small = small.astype(F32)
    wide = kd_width + rt_width
    small_sum = jnp.sum(small[:, : wide + 6], axis=0)
    peaks = small[:, wide + 6 : wide + 9, :heads]
    top_peak = jnp.max(peaks[:, 0] + peaks[:, 1] + peaks[:, 2], axis=0)
    vectors = small_sum[wide : wide + 6].reshape(3, 2, 128).sum(axis=1)
    vector_high, vector_low = split_two(vectors)
    shared_small = jnp.concatenate(
        [small_sum[:wide].astype(BF), vector_high, vector_low, jnp.zeros((10, 128), BF)], axis=0
    )
    all_small = lax.all_to_all(
        jnp.broadcast_to(shared_small[None], (8, wide + 16, 128)), TENSOR, split_axis=0,
        concat_axis=0, tiled=True,
    )
    expert_gate_grad, expert_up_grad, expert_down_grad = unpack(
        x, [after(home[0], shared_small), *home[1:]]
    )
    all_small = after(all_small, expert_gate_grad, tokens_grad)
    expert_gate_grad = jnp.swapaxes(expert_gate_grad, 1, 2)
    expert_up_grad = jnp.swapaxes(expert_up_grad, 1, 2)
    kv_down_grad = all_small[:, :kd_width].reshape(8 * kd_width, 128).T.astype(F32)
    router_grad = all_small[:, kd_width:wide].reshape(8 * rt_width, 128).T.astype(F32)
    vectors = jnp.sum(all_small[:, wide : wide + 6].astype(F32), axis=0).reshape(2, 3, 128).sum(axis=0)
    norm_gain_grad = vectors[0]
    mix_gain_grad = vectors[1]
    kv_gain_grad = vectors[2, : KVRANK // count]

    factor = jnp.minimum(1.0, threshold[0] / jnp.maximum(top_peak, 1.0))
    root_factor = jnp.sqrt(factor)
    q_rows = q_weight.shape[0] // count
    own_query = lax.dynamic_slice_in_dim(q_weight, j * q_rows, q_rows, 0).astype(F32)
    query_step = (own_query - step_size[0] * q_weight_grad).reshape(q_rows, heads, NOPE + ROPE)
    q_weight_new = jnp.concatenate(
        [
            query_step[..., :NOPE] * root_factor[None, :, None],
            query_step[..., NOPE:] * factor[None, :, None],
        ],
        axis=-1,
    ).reshape(q_rows, heads * (NOPE + ROPE))
    own_up = lax.dynamic_slice_in_dim(kv_up, j * up_rows, up_rows, 0).astype(F32)
    up_step = (own_up - step_size[0] * kv_up_grad).reshape(up_rows, heads, NOPE + VDIM)
    kv_up_new = jnp.concatenate(
        [up_step[..., :NOPE] * root_factor[None, :, None], up_step[..., NOPE:]], axis=-1
    ).reshape(up_rows, heads * (NOPE + VDIM))
    return (
        layer_out,
        tokens_grad,
        q_weight_grad,
        kv_down_grad,
        kv_up_grad,
        out_weight_grad,
        router_grad,
        norm_gain_grad,
        kv_gain_grad,
        mix_gain_grad,
        shared_gate_grad,
        shared_up_grad,
        shared_down_grad,
        expert_gate_grad,
        expert_up_grad,
        expert_down_grad,
        q_weight_new,
        kv_up_new,
    )


def solution(mesh):
    fine = Mesh(mesh.devices.reshape(4, 4, 4, 2), ("z", "y", "x", "c"))
    return jax.shard_map(
        shards,
        mesh=fine,
        in_specs=(
            P(EXPERT, None),
            P(EXPERT, None),
            P(EXPERT, None),
            P(),
            P(),
            P(None, TENSOR),
            P(),
            P(),
            P(None, TENSOR),
            P(TENSOR, None),
            P(),
            P(),
            P(None, TENSOR),
            P(None, TENSOR),
            P(TENSOR, None),
            P(EXPERT, None, TENSOR),
            P(EXPERT, None, TENSOR),
            P(EXPERT, TENSOR, None),
            P(),
            P(),
        ),
        out_specs=(
            P(EXPERT, None),
            P(EXPERT, None),
            P(EXPERT, TENSOR),
            P(EXPERT, None),
            P(EXPERT, TENSOR),
            P(TENSOR, EXPERT),
            P(EXPERT, None),
            P(EXPERT),
            P(EXPERT),
            P(EXPERT),
            P(EXPERT, TENSOR),
            P(EXPERT, TENSOR),
            P(TENSOR, EXPERT),
            P(EXPERT, None, TENSOR),
            P(EXPERT, None, TENSOR),
            P(EXPERT, TENSOR, None),
            P(EXPERT, TENSOR),
            P(EXPERT, TENSOR),
        ),
        check_vma=False,
    )
```

```python
import functools
import math

import jax
import jax.numpy as jnp
from jax import lax
from jax.experimental import pallas as pl
from jax.experimental.pallas import tpu as pltpu
from jax.sharding import Mesh
from jax.sharding import PartitionSpec as P

D = 2048
HALF = D // 2
NOPE = 128
ROPE = 64
VDIM = 128
KVRANK = 512
TOPK = 6
PROMPT = 1024
CONT = 2
EXPERTS = 64
CAP = 48
SPAN = 4
RING = 4
OWN = 48
EPSILON = 1e-06

BF = jnp.bfloat16
F32 = jnp.float32
EXPERT = ("z", "y")
TENSOR = ("x", "c")


def dot(left, right, contract=((1,), (0,))):
    return lax.dot_general(left, right, (contract, ((), ())), preferred_element_type=F32)


def swap(block):
    return lax.ppermute(block, "c", [(0, 1), (1, 0)])


def shift(block, axis, step):
    return lax.ppermute(block, axis, [(i, (i + step) % RING) for i in range(RING)])


def spread(block):
    return lax.all_to_all(block, EXPERT, split_axis=0, concat_axis=0, tiled=True)


def pick_index(blocks, index, axis=0):
    return lax.dynamic_index_in_dim(blocks, index, axis, keepdims=False)


def sum_ring(blocks, axis, index):
    return sum_sent(*ring_parts(blocks, index), axis)


def ring_parts(blocks, index):
    own = pick_index(blocks, index)
    return own, [pick_index(blocks, (index + step) % RING).astype(BF) for step in (1, 2, 3)]


def sum_sent(own, parts, axis):
    for step in (1, 2, 3):
        own = own + shift(parts[step - 1], axis, step).astype(F32)
    return own


def gather_ring(block, axis, index):
    blocks = jnp.zeros((RING,) + block.shape, block.dtype)
    blocks = lax.dynamic_update_index_in_dim(blocks, block, index, 0)
    for step in (1, 2, 3):
        blocks = lax.dynamic_update_index_in_dim(
            blocks, shift(block, axis, step), (index - step) % RING, 0
        )
    return blocks


def gather_pair(block, core):
    blocks = jnp.zeros((2,) + block.shape, block.dtype)
    blocks = lax.dynamic_update_index_in_dim(blocks, block, core, 0)
    return lax.dynamic_update_index_in_dim(blocks, swap(block), 1 - core, 0)


def gather_rows(block):
    return lax.all_gather(block, TENSOR, axis=0, tiled=True)


def after(value, *others):
    return lax.optimization_barrier((value, *others))[0]


PIECE = 176
HIDDEN = RING * PIECE
SLOTS = 16 * CAP
TILE = 256
EXTRA = 128
NT = ((1,), (1,))
TN = ((0,), (0,))
VMEM_LIMIT = 56 << 20
HINT = 64


def whole(*shape):
    return pl.BlockSpec(shape, lambda *_: (0,) * len(shape))


def anywhere():
    return pl.BlockSpec(memory_space=pl.ANY)


def copy_all(pairs, sems):
    copies = [pltpu.make_async_copy(a, b, sems.at[i]) for i, (a, b) in enumerate(pairs)]
    for one in copies:
        one.start()
    for one in copies:
        one.wait()


def cost(flops, bytes_accessed, exps=0):
    return pl.CostEstimate(
        flops=int(flops) // HINT, bytes_accessed=int(bytes_accessed) // HINT, transcendentals=0
    )


OUTWARD = (208, 320)
HOMEWARD = (96, 112, 80, 240)


def spans(parts):
    found, start = [], 0
    for part, size in enumerate(parts):
        at = start
        while at < start + size:
            weight, inside = divmod(at, PIECE)
            length = min(PIECE - inside, start + size - at)
            found.append((part, at - start, weight, inside, length))
            at += length
        start += size
    return found


def pack_kernel(x_ref, *refs):
    for step in range(3):
        for part, at, weight, inside, length in spans(OUTWARD):
            out = refs[9 + step * len(OUTWARD) + part]
            out[at : at + length, :] = refs[3 * step + weight][0, inside : inside + length, :]


def pack(x, gate, up, down):
    block = 512

    def source(step):
        return pl.BlockSpec((1, PIECE, block), lambda i, x: (lax.rem(x[0] + step, RING), 0, i))

    outs = pl.pallas_call(
        pack_kernel,
        grid_spec=pltpu.PrefetchScalarGridSpec(
            num_scalar_prefetch=1,
            grid=(D // block,),
            in_specs=[source(step) for step in (1, 2, 3) for _ in range(3)],
            out_specs=[pl.BlockSpec((size, block), lambda i, _: (0, i)) for size in OUTWARD] * 3,
        ),
        out_shape=[jax.ShapeDtypeStruct((size, D), BF) for size in OUTWARD] * 3,
        compiler_params=pltpu.CompilerParams(vmem_limit_bytes=VMEM_LIMIT),
        cost_estimate=cost(0, 13 << 20),
        name="pack_weights",
    )(x.reshape(1), *((gate, up, down) * 3))
    return [outs[part :: len(OUTWARD)] for part in range(len(OUTWARD))]


def unpack_kernel(x_ref, *refs):
    outs = refs[len(HOMEWARD) * RING :]
    for step in range(RING):
        index = lax.rem(x_ref[0] + step, RING)
        for part, at, weight, inside, length in spans(HOMEWARD):
            piece = refs[part * RING + step]
            outs[weight][index, inside : inside + length, :] = piece[at : at + length, :].astype(F32)


def unpack(x, parts):
    block = 512
    return pl.pallas_call(
        unpack_kernel,
        grid_spec=pltpu.PrefetchScalarGridSpec(
            num_scalar_prefetch=1,
            grid=(D // block,),
            in_specs=[
                pl.BlockSpec((size, block), lambda i, _: (0, i))
                for size in HOMEWARD
                for _ in range(RING)
            ],
            out_specs=[pl.BlockSpec((RING, PIECE, block), lambda i, _: (0, 0, i))] * 3,
        ),
        out_shape=[jax.ShapeDtypeStruct((RING, PIECE, D), F32)] * 3,
        compiler_params=pltpu.CompilerParams(vmem_limit_bytes=VMEM_LIMIT),
        cost_estimate=cost(0, 26 << 20),
        name="unpack_gradients",
    )(x.reshape(1), *[piece for part in parts for piece in part])


def load_weight(which, index, own_ref, parts, weight):
    pairs = [(own_ref.at[index], weight.at[pl.ds(0, PIECE)])]
    for part, at, kind, inside, length in spans(OUTWARD):
        if kind == which:
            for step, piece in enumerate(parts[part]):
                start = (step + 1) * PIECE + inside
                pairs.append((piece.at[pl.ds(at, length)], weight.at[pl.ds(start, length)]))
    return pairs


def halves_of(place_ref):
    core = place_ref[1]
    return (
        pl.ds(pl.multiple_of(core * HALF, HALF), HALF),
        pl.ds(pl.multiple_of((1 - core) * HALF, HALF), HALF),
    )


def expert_kernel(
    place_ref,
    mine_ref,
    other_ref,
    grad_mine_ref,
    grad_other_ref,
    gate_ref,
    own_gate,
    own_up,
    own_down,
    p1,
    p2,
    p3,
    q1,
    q2,
    q3,
    act_ref,
    scaled_ref,
    gate_grad_ref,
    up_grad_ref,
    keep_ref,
    give_ref,
    columns_ref,
    gate_w,
    up_w,
    down_w,
    sems,
):
    @pl.when(pl.program_id(0) == 0)
    def _():
        index = place_ref[0]
        parts = {0: (p1, p2, p3), 1: (q1, q2, q3)}
        copy_all(
            load_weight(0, index, own_gate, parts, gate_w)
            + load_weight(1, index, own_up, parts, up_w)
            + load_weight(2, index, own_down, parts, down_w),
            sems,
        )

    first, second = halves_of(place_ref)
    mine, other = mine_ref[...], other_ref[...]
    extra = gate_ref[...].astype(F32)
    gate = extra[:, 0:1] + extra[:, 1:2]
    gate_lin = dot(mine, gate_w[:, first], NT) + dot(other, gate_w[:, second], NT)
    up_lin = dot(mine, up_w[:, first], NT) + dot(other, up_w[:, second], NT)
    raw = dot(grad_mine_ref[...], down_w[:, first], NT)
    raw = raw + dot(grad_other_ref[...], down_w[:, second], NT)
    sigmoid = jax.nn.sigmoid(gate_lin)
    silu = gate_lin * sigmoid
    act = (silu * up_lin).astype(BF)
    act_ref[...] = act
    act = act.astype(F32)
    scaled_ref[...] = (act * gate).astype(BF)
    act_grad = raw * gate
    gate_grad = (act_grad * up_lin * (sigmoid * (1.0 + gate_lin * (1.0 - sigmoid)))).astype(BF)
    up_grad = (act_grad * silu).astype(BF)
    gate_grad_ref[...] = gate_grad
    up_grad_ref[...] = up_grad
    keep_ref[...] = dot(gate_grad, gate_w[:, first]) + dot(up_grad, up_w[:, first])
    give_ref[...] = (dot(gate_grad, gate_w[:, second]) + dot(up_grad, up_w[:, second])).astype(BF)
    slot_grad = jnp.sum(act * raw, axis=1, keepdims=True)
    high = slot_grad.astype(BF).astype(F32)
    lane = lax.broadcasted_iota(jnp.int32, (TILE, EXTRA), 1)
    expert_id = place_ref[2]
    columns_ref[...] = jnp.where(
        lane == expert_id, high, jnp.where(lane == EXPERTS + expert_id, slot_grad - high, 0.0)
    ).astype(BF)


def expert_pass(place, mine, other, gate, up, down, packed):
    rows = lambda width, at=0: pl.BlockSpec((TILE, width), lambda i, _: (i, at))
    shape = lambda width, dtype: jax.ShapeDtypeStruct((SLOTS, width), dtype)
    return pl.pallas_call(
        expert_kernel,
        grid_spec=pltpu.PrefetchScalarGridSpec(
            num_scalar_prefetch=1,
            grid=(SLOTS // TILE,),
            in_specs=[rows(HALF)] * 2 + [rows(HALF, 1)] * 2 + [rows(EXTRA, D // EXTRA)]
            + [anywhere()] * 9,
            out_specs=[rows(HIDDEN)] * 4 + [rows(HALF)] * 2 + [rows(EXTRA)],
            scratch_shapes=[pltpu.VMEM((HIDDEN, D), BF)] * 3 + [pltpu.SemaphoreType.DMA((15,))],
        ),
        out_shape=[shape(HIDDEN, BF)] * 4
        + [shape(HALF, F32), shape(HALF, BF), shape(EXTRA, BF)],
        compiler_params=pltpu.CompilerParams(vmem_limit_bytes=VMEM_LIMIT),
        cost_estimate=cost(10 * SLOTS * D * HIDDEN, 24 << 20, SLOTS * HIDDEN),
        name="expert_pass",
    )(place, mine, other, mine, other, mine, gate, up, down, *[p for part in packed for p in part])


def produce_kernel(place_ref, act_ref, mine_ref, own_down, p1, p2, p3, keep_ref, give_ref, down, sems):
    @pl.when(pl.program_id(0) == 0)
    def _():
        copy_all(load_weight(2, place_ref[0], own_down, {1: (p1, p2, p3)}, down), sems)

    first, second = halves_of(place_ref)
    extra = mine_ref[...].astype(F32)
    gate = extra[:, 0:1] + extra[:, 1:2]
    keep_ref[...] = dot(act_ref[...], down[:, first]) * gate
    give_ref[...] = (dot(act_ref[...], down[:, second]) * gate).astype(BF)


def produce(place, act, mine, down, packed):
    rows = lambda width: pl.BlockSpec((TILE, width), lambda i, _: (i, 0))
    return pl.pallas_call(
        produce_kernel,
        grid_spec=pltpu.PrefetchScalarGridSpec(
            num_scalar_prefetch=1,
            grid=(SLOTS // TILE,),
            in_specs=[
                rows(HIDDEN),
                pl.BlockSpec((TILE, EXTRA), lambda i, _: (i, D // EXTRA)),
            ]
            + [anywhere()] * 4,
            out_specs=[rows(HALF)] * 2,
            scratch_shapes=[pltpu.VMEM((HIDDEN, D), BF), pltpu.SemaphoreType.DMA((4,))],
        ),
        out_shape=[
            jax.ShapeDtypeStruct((SLOTS, HALF), F32),
            jax.ShapeDtypeStruct((SLOTS, HALF), BF),
        ],
        compiler_params=pltpu.CompilerParams(vmem_limit_bytes=VMEM_LIMIT),
        cost_estimate=cost(2 * SLOTS * D * HIDDEN, 9 << 20),
        name="produce",
    )(place, act, mine, down, *packed[1])


def weight_grad_kernel(place_ref, *refs, weights, parts):
    lefts = refs[: len(weights)]
    rights, outs = refs[len(weights) : -len(parts) * RING], refs[-len(parts) * RING :]
    own = pl.program_id(0) < 2
    rights = [jnp.where(own, rights[i][...], rights[i + 1][...]) for i in range(0, len(rights), 2)]
    for left, weight in zip(lefts, weights):
        right = rights[1] if weight == 2 and len(rights) > 1 else rights[0]
        product = dot(left[...], right, TN).astype(BF)
        for step in range(RING):
            for part, at, kind, inside, length in spans(HOMEWARD):
                if kind == weight:
                    start = step * PIECE + inside
                    out = outs[parts.index(part) * RING + step]
                    out[at : at + length, :] = product[start : start + length, :]


def weight_grads(place, weights, parts, lefts, rows):
    block = HALF // 2
    mine = [pl.BlockSpec((SLOTS, block), lambda i, _, at=at: (0, at + jnp.minimum(i, 1))) for at in (0, 2)]
    other = [
        pl.BlockSpec((SLOTS, block), lambda i, _, at=at: (0, at + jnp.maximum(i - 2, 0)))
        for at in (0, 2)
    ]
    sizes = [HOMEWARD[part] for part in parts for _ in range(RING)]
    outs = pl.pallas_call(
        functools.partial(weight_grad_kernel, weights=weights, parts=parts),
        grid_spec=pltpu.PrefetchScalarGridSpec(
            num_scalar_prefetch=1,
            grid=(4,),
            in_specs=[whole(SLOTS, HIDDEN)] * len(lefts)
            + [mine[0], other[0], mine[1], other[1]],
            out_specs=[
                pl.BlockSpec((size, block), lambda i, place: (0, lax.rem(2 * place[1] + i, 4)))
                for size in sizes
            ],
        ),
        out_shape=[jax.ShapeDtypeStruct((size, D), BF) for size in sizes],
        compiler_params=pltpu.CompilerParams(vmem_limit_bytes=VMEM_LIMIT),
        cost_estimate=cost(2 * len(lefts) * SLOTS * D * HIDDEN, 18 << 20),
        name="weight_grads",
    )(place, *lefts, *rows, *rows)
    return [outs[i * RING : (i + 1) * RING] for i in range(len(parts))]


SHARED = 352
WIDE = 384
ATT = 2 * VDIM


def shared_kernel(mixed, out_grad, gate_w, up_w, down_w, part, mixed_grad, grads):
    gate_lin = dot(mixed[...], gate_w[...], NT)
    up_lin = dot(mixed[...], up_w[...], NT)
    sigmoid = jax.nn.sigmoid(gate_lin)
    silu = gate_lin * sigmoid
    act = (silu * up_lin).astype(BF)
    act_grad = dot(out_grad[...], down_w[...], NT)
    gate_grad = (act_grad * up_lin * (sigmoid * (1.0 + gate_lin * (1.0 - sigmoid)))).astype(BF)
    up_grad = (act_grad * silu).astype(BF)
    for start in range(0, D, 512):
        at = slice(start, start + 512)
        part[:, at] = dot(act, down_w[:, at])
        mixed_grad[:, at] = dot(gate_grad, gate_w[:, at]) + dot(up_grad, up_w[:, at])
        zeros = jnp.zeros((512, WIDE - SHARED), BF)
        for i, (left, right) in enumerate(((mixed, gate_grad), (mixed, up_grad), (out_grad, act))):
            start = i * WIDE
            grads[at, start : start + SHARED] = dot(left[:, at], right, TN).astype(BF)
            grads[at, start + SHARED : start + WIDE] = zeros


def shared_experts(mixed, out_grad, gate_w, up_w, down_w):
    args = (mixed, out_grad, gate_w, up_w, down_w)
    rows = mixed.shape[0]
    outs = [
        jax.ShapeDtypeStruct((rows, D), F32),
        jax.ShapeDtypeStruct((rows, D), F32),
        jax.ShapeDtypeStruct((D, 3 * WIDE), BF),
    ]
    return pl.pallas_call(
        shared_kernel,
        grid=(1,),
        in_specs=[whole(*arg.shape) for arg in args],
        out_specs=[whole(*out.shape) for out in outs],
        out_shape=outs,
        compiler_params=pltpu.CompilerParams(vmem_limit_bytes=VMEM_LIMIT),
        cost_estimate=cost(18 * rows * D * SHARED, 18 << 20, rows * SHARED),
        name="shared_experts",
    )(*args)


GROUP = 1536
ROWS = 384
LATENT = KVRANK + ROPE
HEADS = 2
HEAD = NOPE + ROPE
SCALE = 1.0 / math.sqrt(HEAD)


def turn(block, cosine, sine):
    half = ROPE // 2
    return block * cosine + jnp.concatenate([block[:, half:], block[:, :half]], axis=1) * sine


def mask_bias(seg_keys, seg_rows, row_start):
    key = lax.broadcasted_iota(jnp.int32, (GROUP, ROWS), 0)
    row = lax.broadcasted_iota(jnp.int32, (GROUP, ROWS), 1) + row_start
    same = (seg_keys == seg_rows) & (key <= row)
    return jnp.where(same | ((seg_keys == 0) & (seg_rows > 0)), 0.0, -1e30)


def wide_tables(cos, sin):
    return jnp.concatenate([cos, cos], axis=1), jnp.concatenate([-sin, sin], axis=1)


def row_tables(cos_ref, sin_ref, row_start):
    at = pl.ds(pl.multiple_of(row_start, ROWS), ROWS)
    return wide_tables(cos_ref[at, :], sin_ref[at, :])


def head_queries(query, row_cos, row_sin, head):
    start = head * HEAD
    plain = query[:, start : start + NOPE].astype(BF)
    return plain, turn(query[:, start + NOPE : start + HEAD], row_cos, row_sin).astype(BF)


def attention_kernel(
    place_ref,
    mine_ref,
    other_ref,
    query_ref,
    gain_ref,
    kv_up_ref,
    out_weight_ref,
    cos_ref,
    sin_ref,
    seg_keys_ref,
    seg_rows_ref,
    give_ref,
    keep_ref,
    attended_ref,
    compressed_ref,
    kv_ref,
    key_rot_ref,
    log_total_ref,
    peak_ref,
    latent,
    attended,
):
    core = place_ref[1]
    half = ROWS // 2
    for block in range(SPAN):
        start = pl.multiple_of(block * ROWS + core * half, half)
        latent[pl.ds(start, half), :] = mine_ref[block]
        start = pl.multiple_of(block * ROWS + (1 - core) * half, half)
        latent[pl.ds(start, half), :] = other_ref[block]
    inputs = latent[:, :KVRANK].astype(F32)
    inverse = lax.rsqrt(jnp.mean(inputs * inputs, axis=1, keepdims=True) + EPSILON)
    compressed_ref[...] = (inputs * inverse * gain_ref[...]).astype(BF)
    kv_ref[...] = dot(compressed_ref[...], kv_up_ref[...]).astype(BF)
    cosine, sine = wide_tables(cos_ref[...], sin_ref[...])
    key_rot_ref[...] = turn(latent[:, KVRANK:].astype(F32), cosine, sine).astype(BF)
    seg_rows = seg_rows_ref[:, pl.ds(pl.multiple_of(place_ref[3], ROWS), ROWS)]
    bias = mask_bias(seg_keys_ref[...], seg_rows, place_ref[3])
    row_cos, row_sin = row_tables(cos_ref, sin_ref, place_ref[3])
    for head in range(HEADS):
        plain, turned = head_queries(query_ref, row_cos, row_sin, head)
        start = head * (NOPE + VDIM)
        scores = dot(kv_ref[:, start : start + NOPE], plain, NT)
        scores = (scores + dot(key_rot_ref[...], turned, NT)) * SCALE + bias
        peak = jnp.max(scores, axis=0, keepdims=True)
        powers = jnp.exp(scores - peak)
        total = jnp.sum(powers, axis=0, keepdims=True)
        log_total_ref[head : head + 1, :] = peak + jnp.log(total)
        peak_ref[head : head + 1, :] = peak
        weights = (powers * (1.0 / total)).astype(BF)
        values = kv_ref[:, start + NOPE : start + NOPE + VDIM]
        attended[:, head * VDIM : (head + 1) * VDIM] = dot(values, weights, TN).T
    attended_ref[...] = attended[...].astype(BF)
    for block in range(RING):
        for out, which in ((give_ref, 1 - core), (keep_ref, core)):
            start = pl.multiple_of(block * 2 * OWN + which * OWN, OWN)
            out[block] = dot(
                attended[pl.ds(start, OWN), :].astype(BF), out_weight_ref[...]
            ).astype(out.dtype)


def attention(place, mine, other, query, gain, kv_up, out_weight, tables, segs):
    shape = jax.ShapeDtypeStruct
    args = (mine, other, query, gain.reshape(1, KVRANK), kv_up, out_weight, *tables, *segs)
    outs = [
        shape((RING, OWN, D), BF),
        shape((RING, OWN, D), F32),
        shape((ROWS, HEADS * VDIM), BF),
        shape((GROUP, KVRANK), BF),
        shape((GROUP, HEADS * (NOPE + VDIM)), BF),
        shape((GROUP, ROPE), BF),
        shape((HEADS, ROWS), F32),
        shape((HEADS, ROWS), F32),
    ]
    return pl.pallas_call(
        attention_kernel,
        grid_spec=pltpu.PrefetchScalarGridSpec(
            num_scalar_prefetch=1,
            grid=(1,),
            in_specs=[whole(*arg.shape) for arg in args],
            out_specs=[whole(*out.shape) for out in outs],
            scratch_shapes=[
                pltpu.VMEM((GROUP, LATENT), BF),
                pltpu.VMEM((ROWS, HEADS * VDIM), F32),
            ],
        ),
        out_shape=outs,
        compiler_params=pltpu.CompilerParams(vmem_limit_bytes=VMEM_LIMIT),
        cost_estimate=cost(3e9, 14 << 20, 2 * GROUP * ROWS),
        name="attention_forward",
    )(place, *args)


def attention_back_kernel(
    place_ref,
    mine_ref,
    other_ref,
    query_ref,
    compressed_ref,
    kv_ref,
    key_rot_ref,
    log_total_ref,
    kv_up_ref,
    out_weight_ref,
    cos_ref,
    sin_ref,
    seg_keys_ref,
    seg_rows_ref,
    q_weight_ref,
    give_ref,
    keep_ref,
    kv_grad_ref,
    query_grad_ref,
    branch_ref,
    normed_give_ref,
    normed_keep_ref,
    comp_grad,
    rot_grad,
):
    core = place_ref[1]
    interleave(core, mine_ref, other_ref, branch_ref, D + EXTRA)
    attended_grad = dot(branch_ref[:, :D], out_weight_ref[...], NT).astype(BF)
    seg_rows = seg_rows_ref[:, pl.ds(pl.multiple_of(place_ref[3], ROWS), ROWS)]
    bias = mask_bias(seg_keys_ref[...], seg_rows, place_ref[3])
    row_cos, row_sin = row_tables(cos_ref, sin_ref, place_ref[3])
    turned_sum = 0.0
    query_grads = []
    for head in range(HEADS):
        plain, turned = head_queries(query_ref, row_cos, row_sin, head)
        start = head * (NOPE + VDIM)
        keys = kv_ref[:, start : start + NOPE]
        values = kv_ref[:, start + NOPE : start + NOPE + VDIM]
        key_rot = key_rot_ref[...]
        scores = (dot(keys, plain, NT) + dot(key_rot, turned, NT)) * SCALE + bias
        probs = jnp.exp(scores - log_total_ref[head : head + 1, :])
        grad = attended_grad[:, head * VDIM : (head + 1) * VDIM]
        value_grad = dot(probs.astype(BF), grad)
        prob_grad = dot(values, grad, NT)
        inner = jnp.sum(probs * prob_grad, axis=0, keepdims=True)
        score_grad = (probs * (prob_grad - inner)).astype(BF)
        kv_grad_ref[:, start : start + NOPE] = (dot(score_grad, plain) * SCALE).astype(BF)
        kv_grad_ref[:, start + NOPE : start + NOPE + VDIM] = value_grad.astype(BF)
        turned_sum = turned_sum + dot(score_grad, turned) * SCALE
        query_grads.append((dot(keys, score_grad, TN) * SCALE).T)
        turned_grad = (dot(key_rot, score_grad, TN) * SCALE).T
        query_grads.append(turn(turned_grad, row_cos, -row_sin))
    comp_grad[...] = dot(kv_grad_ref[...], kv_up_ref[...], NT)
    cosine, sine = wide_tables(cos_ref[...], sin_ref[...])
    rot_grad[...] = turn(turned_sum, cosine, -sine)
    for block in range(SPAN):
        for inner in range(RING):
            for out, which in ((give_ref, 1 - core), (keep_ref, core)):
                start = pl.multiple_of(block * ROWS + inner * 2 * OWN + which * OWN, OWN)
                out[block, inner, :, :KVRANK] = comp_grad[pl.ds(start, OWN), :].astype(out.dtype)
                out[block, inner, :, KVRANK:] = rot_grad[pl.ds(start, OWN), :].astype(out.dtype)
    query_grad_ref[...] = jnp.concatenate(query_grads, axis=1).astype(BF)
    for block in range(RING):
        for out, which in ((normed_give_ref, 1 - core), (normed_keep_ref, core)):
            start = pl.multiple_of(block * 2 * OWN + which * OWN, OWN)
            part = query_grad_ref[pl.ds(start, OWN), :]
            out[block] = dot(part, q_weight_ref[...], NT).astype(out.dtype)


def attention_back(
    place, mine, other, query, compressed, kv, key_rot, log_total, kv_up, out_weight, tables, segs,
    q_weight,
):
    shape = jax.ShapeDtypeStruct
    args = (
        mine, other, query, compressed, kv, key_rot, log_total, kv_up, out_weight, *tables, *segs,
        q_weight,
    )
    outs = [
        shape((SPAN, RING, OWN, LATENT), BF),
        shape((SPAN, RING, OWN, LATENT), F32),
        shape((GROUP, HEADS * (NOPE + VDIM)), BF),
        shape((ROWS, HEADS * HEAD), BF),
        shape((ROWS, D + EXTRA), BF),
        shape((RING, OWN, D), BF),
        shape((RING, OWN, D), F32),
    ]
    return pl.pallas_call(
        attention_back_kernel,
        grid_spec=pltpu.PrefetchScalarGridSpec(
            num_scalar_prefetch=1,
            grid=(1,),
            in_specs=[whole(*arg.shape) for arg in args],
            out_specs=[whole(*out.shape) for out in outs],
            scratch_shapes=[pltpu.VMEM((GROUP, KVRANK), F32), pltpu.VMEM((GROUP, ROPE), F32)],
        ),
        out_shape=outs,
        compiler_params=pltpu.CompilerParams(vmem_limit_bytes=VMEM_LIMIT),
        cost_estimate=cost(4e9, 16 << 20, 2 * GROUP * ROWS),
        name="attention_backward",
    )(place, *args)


UP_ROWS = KVRANK // 16
BIG = HEADS * HEAD + ATT + 128


def projection_grad_kernel(
    normed, branch, compressed, query_grad, attended, kv_grad, out
):
    width = HEADS * HEAD
    out[:, :width] = dot(normed[...], query_grad[...], TN).astype(BF)
    out[:, width : width + ATT] = dot(branch[...], attended[...], TN).astype(BF)
    up = dot(compressed[...], kv_grad[...], TN)
    for index in range(4):
        for part in range(4):
            start = index * 128 + part * UP_ROWS
            out[start : start + UP_ROWS, width + ATT :] = up[
                index * UP_ROWS : (index + 1) * UP_ROWS, part * 128 : (part + 1) * 128
            ].astype(BF)


def projection_grads(normed, branch, compressed, query_grad, attended, kv_grad):
    block = 512
    return pl.pallas_call(
        projection_grad_kernel,
        grid=(D // block,),
        in_specs=[
            pl.BlockSpec((ROWS, block), lambda i: (0, i)),
            pl.BlockSpec((ROWS, block), lambda i: (0, i)),
            pl.BlockSpec((GROUP, 128), lambda i: (0, i)),
            whole(ROWS, HEADS * HEAD),
            whole(ROWS, ATT),
            whole(GROUP, HEADS * (NOPE + VDIM)),
        ],
        out_specs=pl.BlockSpec((block, BIG), lambda i: (i, 0)),
        out_shape=jax.ShapeDtypeStruct((D, BIG), BF),
        compiler_params=pltpu.CompilerParams(vmem_limit_bytes=VMEM_LIMIT),
        cost_estimate=cost(2e9, 10 << 20),
        name="projection_grads",
    )(normed, branch, compressed, query_grad, attended, kv_grad)


def combine_kernel(place_ref, pick_ref, returned_ref, shared_ref, give_ref, keep_ref, total):
    core = place_ref[1]
    rows = dot(pick_ref[...], returned_ref[...], TN)
    total[:, :D] = shared_ref[...]
    mine = pl.ds(pl.multiple_of(core * HALF, HALF), HALF)
    total[:, mine] = total[:, mine] + rows[:, :HALF]
    if returned_ref.shape[1] > HALF:
        total[:, D:] = rows[:, HALF:]
    for block in range(RING):
        for out, which in ((give_ref, 1 - core), (keep_ref, core)):
            start = pl.multiple_of(block * 2 * OWN + which * OWN, OWN)
            out[block] = total[pl.ds(start, OWN), :].astype(out.dtype)


def combine_rows(place, pick, returned, shared):
    width = D + returned.shape[1] - HALF
    args = (pick, returned, shared)
    outs = [
        jax.ShapeDtypeStruct((RING, OWN, width), BF),
        jax.ShapeDtypeStruct((RING, OWN, width), F32),
    ]
    return pl.pallas_call(
        combine_kernel,
        grid_spec=pltpu.PrefetchScalarGridSpec(
            num_scalar_prefetch=1,
            grid=(1,),
            in_specs=[whole(*arg.shape) for arg in args],
            out_specs=[whole(*out.shape) for out in outs],
            scratch_shapes=[pltpu.VMEM((ROWS, width), F32)],
        ),
        out_shape=outs,
        compiler_params=pltpu.CompilerParams(vmem_limit_bytes=VMEM_LIMIT),
        cost_estimate=cost(7e8, 8 << 20),
        name="combine_rows",
    )(place, *args)


def order_kernel(x_ref, *refs):
    for step in range(RING):
        refs[RING][lax.rem(x_ref[0] + RING - step, RING)] = refs[step][...]


def order_ring(x, blocks):
    rows, width = blocks[0].shape
    return pl.pallas_call(
        order_kernel,
        grid_spec=pltpu.PrefetchScalarGridSpec(
            num_scalar_prefetch=1,
            grid=(1,),
            in_specs=[whole(rows, width)] * RING,
            out_specs=whole(RING, rows, width),
        ),
        out_shape=jax.ShapeDtypeStruct((RING, rows, width), blocks[0].dtype),
        cost_estimate=cost(0, 2 << 20),
        name="order_ring",
    )(x.reshape(1), *blocks)


def interleave(core, mine_ref, other_ref, out, width):
    for block in range(RING):
        for ref, which in ((mine_ref, core), (other_ref, 1 - core)):
            start = pl.multiple_of(block * 2 * OWN + which * OWN, OWN)
            out[pl.ds(start, OWN), :] = ref[block, :, :width]


def gating_kernel(
    place_ref, mine_ref, other_ref, router_ref, pick_ref, grad_ref, mixed_ref, probs_ref, sent_ref
):
    core = place_ref[1]
    interleave(core, mine_ref, other_ref, mixed_ref, D)
    logits = dot(mixed_ref[...], router_ref[...])
    powers = jnp.exp(logits - jnp.max(logits, axis=1, keepdims=True))
    probs = powers / jnp.sum(powers, axis=1, keepdims=True)
    probs_ref[...] = probs
    pick = pick_ref[...]
    high = probs.astype(BF)
    rest = probs - high.astype(F32)
    middle = rest.astype(BF)
    low = (rest - middle.astype(F32)).astype(BF)
    gates = dot(pick, high) + dot(pick, middle) + dot(pick, low)
    slot = lax.broadcasted_iota(jnp.int32, (SLOTS, EXPERTS), 0)
    lane = lax.broadcasted_iota(jnp.int32, (SLOTS, EXPERTS), 1)
    first = (lane - place_ref[0]) * (CAP // 4)
    inside = (slot >= first) & (slot < first + CAP) & (lax.rem(lane, 4) == place_ref[0])
    gate = jnp.sum(jnp.where(inside, gates, 0.0), axis=1, keepdims=True)
    high = gate.astype(BF).astype(F32)
    lane = lax.broadcasted_iota(jnp.int32, (SLOTS, EXTRA), 1)
    sent_ref[:, D:] = jnp.where(
        lane == 0, high, jnp.where(lane == 1, gate - high, 0.0)
    ).astype(BF)
    mine = pl.ds(pl.multiple_of(core * HALF, HALF), HALF)
    sent_ref[:, :HALF] = dot(pick, mixed_ref[:, mine]).astype(BF)
    sent_ref[:, HALF:D] = dot(pick, grad_ref[:, mine]).astype(BF)


def gating(place, mine, other, router, pick, out_grad):
    args = (mine, other, router, pick, out_grad)
    outs = [
        jax.ShapeDtypeStruct((ROWS, D), BF),
        jax.ShapeDtypeStruct((ROWS, EXPERTS), F32),
        jax.ShapeDtypeStruct((SLOTS, D + EXTRA), BF),
    ]
    return pl.pallas_call(
        gating_kernel,
        grid_spec=pltpu.PrefetchScalarGridSpec(
            num_scalar_prefetch=1,
            grid=(1,),
            in_specs=[whole(*arg.shape) for arg in args],
            out_specs=[whole(*out.shape) for out in outs],
        ),
        out_shape=outs,
        compiler_params=pltpu.CompilerParams(vmem_limit_bytes=VMEM_LIMIT),
        cost_estimate=cost(8e8, 6 << 20),
        name="gating",
    )(place, *args)


KD_COLUMNS = LATENT // 8
ROUTER_COLUMNS = EXPERTS // 8
SHARE = KD_COLUMNS + ROUTER_COLUMNS
SMALL = SHARE + 16


def small_kernel(latent, logit, normed, mixed, norm_gain, mix_gain, kv_gain, peak_ref, out):
    kv_down = dot(latent[...], normed[...], TN)
    router = dot(logit[...], mixed[...], TN)
    lane = lax.broadcasted_iota(jnp.int32, (1, 128), 1)
    peak = 0.0
    for head in range(HEADS):
        highest = jnp.max(peak_ref[head : head + 1, :], axis=1, keepdims=True)
        peak = jnp.where(lane == head, highest, peak)

    def parts(row, number):
        found = []
        for _ in range(number):
            found.append(row.astype(BF).astype(F32))
            row = row - found[-1]
        return found

    peaks = parts(peak, 3)
    zeros = jnp.zeros((7, 128), F32)
    for index in range(16):
        at = slice(index * 128, (index + 1) * 128)
        gain = kv_gain[:, index * UP_ROWS : (index + 1) * UP_ROWS]
        gain = jnp.concatenate([gain, jnp.zeros((1, 128 - UP_ROWS), F32)], axis=1)
        rows = parts(norm_gain[:, at], 2) + parts(mix_gain[:, at], 2) + parts(gain, 2)
        rows = [kv_down[:, at], router[:, at]] + rows + peaks + [zeros]
        out[index] = jnp.concatenate(rows, axis=0).astype(BF)


def small_grads(latent, logit, normed, mixed, norm_gain, mix_gain, kv_gain, peak):
    args = (
        latent,
        logit,
        normed,
        mixed,
        norm_gain.reshape(1, D),
        mix_gain.reshape(1, D),
        kv_gain.reshape(1, KVRANK),
        peak,
    )
    return pl.pallas_call(
        small_kernel,
        grid=(1,),
        in_specs=[whole(*arg.shape) for arg in args],
        out_specs=whole(16, SMALL, 128),
        out_shape=jax.ShapeDtypeStruct((16, SMALL, 128), BF),
        compiler_params=pltpu.CompilerParams(vmem_limit_bytes=VMEM_LIMIT),
        cost_estimate=cost(2e8, 4 << 20),
        name="small_grads",
    )(*args)


def split_two(value):
    high = lax.reduce_precision(value, 8, 7)
    return high.astype(BF), (value - high).astype(BF)


def norm_rows(inputs, gain_vec):
    inverse = lax.rsqrt(jnp.mean(inputs * inputs, axis=-1, keepdims=True) + EPSILON)
    return (inputs * inverse * gain_vec, inverse)


def norm_back(inputs, inverse, gain_vec, gradient):
    weighted = gradient * gain_vec
    inner = jnp.mean(weighted * inputs, axis=-1, keepdims=True)
    d_inputs = inverse * weighted - inputs * (inverse * inverse * inverse) * inner
    return (d_inputs, jnp.sum(gradient * inputs * inverse, axis=0))


def rotate(inputs, cosine, sine):
    half_size = inputs.shape[-1] // 2
    first_half = inputs[..., :half_size]
    second_half = inputs[..., half_size:]
    return jnp.concatenate(
        [first_half * cosine - second_half * sine, second_half * cosine + first_half * sine],
        axis=-1,
    )


def unrotate(gradient, cosine, sine):
    return rotate(gradient, cosine, -sine)


def shards(
    tokens,
    out_grad,
    routes,
    segment,
    norm_gain,
    q_weight,
    kv_down,
    kv_gain,
    kv_up,
    out_weight,
    mix_gain,
    router,
    shared_gate,
    shared_up,
    shared_down,
    expert_gate,
    expert_up,
    expert_down,
    step_size,
    threshold,
):
    rows = tokens.shape[0]
    x = lax.axis_index("x")
    c = lax.axis_index("c")
    y = lax.axis_index("y")
    z = lax.axis_index("z")
    j = z * RING + y
    t = x * 2 + c
    heads = q_weight.shape[1] // (NOPE + ROPE)
    group_len = rows * SPAN
    count = expert_down.shape[0] * 4
    score_scale = 1.0 / math.sqrt(NOPE + ROPE)
    own_start = t * OWN

    def own_rows(array):
        return lax.dynamic_slice_in_dim(array, own_start, OWN, 0)

    routes_t = routes.T
    chosen = 4 * jnp.arange(count, dtype=jnp.int32) + x
    hot = jnp.any(routes_t[None, :, :] == chosen[:, None, None], axis=1)
    number = jnp.arange(rows, dtype=jnp.int32)
    earlier = (number[:, None] < number[None, :]).astype(BF)
    slot = dot(hot.astype(BF), earlier)
    pick = hot[:, None, :] & (slot[:, None, :] == jnp.arange(CAP, dtype=F32)[None, :, None])
    pick_b = pick.astype(BF).reshape(count * CAP, rows)

    place = jnp.stack([x, c, 4 * j + x, y * rows]).astype(jnp.int32)

    def send_rows(sent):
        width = sent.shape[1]
        return spread(sent.reshape(count, CAP, width)).reshape(count * CAP, width)

    gate_t = jnp.swapaxes(expert_gate, 1, 2)
    up_t = jnp.swapaxes(expert_up, 1, 2)
    first_part, last_part = pack(x, gate_t, up_t, expert_down)
    first_part = [shift(first_part[step - 1], "x", step) for step in (1, 2, 3)]

    group_ids = lax.dynamic_slice_in_dim(segment, z * group_len, group_len)
    key_number = jnp.arange(group_len, dtype=jnp.int32)
    first_length = jnp.sum((group_ids == 1).astype(jnp.int32))
    key_place = jnp.where(
        group_ids == 0,
        key_number - (group_len - PROMPT),
        key_number + PROMPT - jnp.where(group_ids == 1, 0, first_length),
    )
    frequency = jnp.power(10000.0, -2.0 * jnp.arange(ROPE // 2, dtype=F32) / ROPE)
    key_angle = key_place.astype(F32)[:, None] * frequency[None, :]
    tables = (jnp.cos(key_angle), jnp.sin(key_angle))
    segs = (group_ids.reshape(group_len, 1), group_ids.reshape(1, group_len))

    x_input = after(tokens, last_part[0]).astype(F32)
    normed_f, _ = norm_rows(x_input, norm_gain)
    normed = normed_f.astype(BF)
    latent = dot(normed, kv_down).astype(BF)
    half_latent = lax.dynamic_slice_in_dim(latent, c * (rows // 2), rows // 2, 0)
    gathered = gather_ring(half_latent, "y", y)
    query_lin = dot(normed, q_weight)
    attn_give, attn_keep, attended_b, compressed, kv_rows, key_rot, log_total, row_peak = attention(
        place, gathered, swap(gathered), query_lin, kv_gain, kv_up, out_weight, tables, segs
    )

    attn_got = swap(after(attn_give, *first_part))
    attn_own, attn_sent = ring_parts(attn_keep + attn_got.astype(F32), x)
    residual = own_rows(tokens).astype(F32) + sum_sent(attn_own, attn_sent, "x")
    mixed_f, inverse_two = norm_rows(residual, mix_gain)
    mixed_own = mixed_f.astype(BF)
    mixed_ring = [mixed_own] + [shift(mixed_own, "x", step) for step in (1, 2, 3)]
    mixed_mine = order_ring(x, mixed_ring)
    last_part = [after(piece, mixed_mine) for piece in last_part]
    last_part = [shift(last_part[step - 1], "x", step) for step in (1, 2, 3)]
    packed = (first_part, last_part)
    mixed_other = swap(mixed_mine)

    mixed_in, gate_probs, mixed_sent = gating(
        place, mixed_mine, mixed_other, router, pick_b, out_grad
    )
    mixed_rows = send_rows(mixed_sent)
    shared_part, shared_mixed_grad, shared_grads = shared_experts(
        after(mixed_in, mixed_sent), out_grad, shared_gate.T, shared_up.T, shared_down
    )
    mixed_rows = after(mixed_rows, shared_part, *last_part)
    mixed_rows = (mixed_rows, swap(mixed_rows))
    expert_act, scaled_act, gate_lin_grad, up_lin_grad, grad_keep, grad_give, slot_cols = (
        expert_pass(place, *mixed_rows, gate_t, up_t, expert_down, packed)
    )

    grad_half = (grad_keep + swap(grad_give).astype(F32)).astype(BF)
    sent_grad = jnp.concatenate([grad_half, slot_cols], axis=1)
    returned_grad = send_rows(sent_grad)
    parts = weight_grads(
        place,
        (0, 1, 2),
        (0, 1, 2, 3),
        (gate_lin_grad, up_lin_grad, after(scaled_act, sent_grad)),
        mixed_rows,
    )

    def send_home(part):
        return [part[0]] + [shift(part[step], "x", RING - step) for step in (1, 2, 3)]

    home = [send_home(parts[0])]
    produced_keep, produced_give = produce(
        place, after(expert_act, parts[0][0]), mixed_rows[0], expert_down, packed
    )
    mixed_give, mixed_keep = combine_rows(
        place, pick_b, after(returned_grad, parts[0][0], produced_give), shared_mixed_grad
    )
    mixed_half = mixed_keep + swap(after(mixed_give, *home[0])).astype(F32)
    mixed_half, mixed_sent = ring_parts(mixed_half, x)
    shared_grads = lax.psum_scatter(
        after(shared_grads, mixed_rows[0]), EXPERT, scatter_dimension=0, tiled=True
    )
    produced_half = (produced_keep + swap(produced_give).astype(F32)).astype(BF)
    produced = send_rows(after(produced_half, *mixed_sent))
    mixed_total = sum_sent(mixed_half, mixed_sent, "x")
    prob_grad = mixed_total[:, D : D + EXPERTS] + mixed_total[:, D + EXPERTS :]
    own_probs = own_rows(gate_probs)
    logit_grad = (
        own_probs * (prob_grad - jnp.sum(own_probs * prob_grad, axis=-1, keepdims=True))
    ).astype(BF)
    mixed_grad = mixed_total[:, :D] + dot(logit_grad, router, ((1,), (1,)))
    mid_norm_grad, mix_gain_grad = norm_back(residual, inverse_two, mix_gain, mixed_grad)
    mid_grad = own_rows(out_grad).astype(F32) + mid_norm_grad
    branch_own = jnp.concatenate(
        [mid_grad.astype(BF), logit_grad, jnp.zeros((OWN, 128 - EXPERTS), BF)], axis=1
    )
    branch_ring = [branch_own] + [shift(branch_own, "x", step) for step in (1, 2, 3)]
    branch_mine = order_ring(x, branch_ring)
    home.append(send_home([after(piece, branch_mine) for piece in parts[1]]))
    (
        latent_give, latent_keep, kv_grad, query_lin_grad, branch_all, normed_give, normed_keep,
    ) = attention_back(
        place, branch_mine, swap(branch_mine), query_lin, compressed, kv_rows, key_rot, log_total, kv_up, out_weight,
        tables, segs, q_weight,
    )
    latent_give = after(latent_give, produced, *home[1])
    latent_sent = (latent_keep + swap(latent_give).astype(F32)).astype(BF)
    latent_parts = lax.all_to_all(
        latent_sent.reshape(SPAN * RING, OWN, LATENT), ("y", "x"), split_axis=0, concat_axis=0,
        tiled=True,
    )
    latent_total = jnp.sum(latent_parts.astype(F32), axis=0)
    normed_half = normed_keep + swap(after(normed_give, latent_sent)).astype(F32)
    normed_own, normed_sent = ring_parts(normed_half, x)
    normed_total = sum_sent(normed_own, normed_sent, "x")

    logit_grad_all = branch_all[:, D : D + EXPERTS]
    own_comp = own_rows(latent)[:, :KVRANK].astype(F32)
    _, own_inverse = norm_rows(own_comp, kv_gain)
    comp_own_grad, kv_gain_grad = norm_back(
        own_comp, own_inverse, kv_gain, latent_total[:, :KVRANK]
    )
    latent_grad = jnp.concatenate([comp_own_grad, latent_total[:, KVRANK:]], axis=-1).astype(BF)
    latent_columns = jnp.swapaxes(latent_grad.reshape(OWN, 8, KD_COLUMNS), 0, 1)
    big = projection_grads(
        normed, branch_all, compressed, query_lin_grad, attended_b, after(kv_grad, latent_columns)
    )
    latent_columns = lax.all_to_all(
        latent_columns, TENSOR, split_axis=0, concat_axis=0, tiled=True
    )
    normed_grad = normed_total + dot(latent_grad, kv_down, ((1,), (1,)))
    own_input = own_rows(tokens).astype(F32)
    _, inverse_one = norm_rows(own_input, norm_gain)
    input_norm_grad, norm_gain_grad = norm_back(own_input, inverse_one, norm_gain, normed_grad)


    up_rows = UP_ROWS
    kd_width = KD_COLUMNS
    rt_width = ROUTER_COLUMNS
    small = small_grads(
        latent_columns.reshape(rows, kd_width),
        lax.dynamic_slice_in_dim(logit_grad_all, t * rt_width, rt_width, 1),
        normed,
        mixed_in,
        norm_gain_grad,
        mix_gain_grad,
        kv_gain_grad,
        row_peak,
    )
    small = jnp.swapaxes(small.reshape(count, 6, 16, 128), 1, 2).reshape(count, 16, BIG)
    packed_grads = jnp.concatenate([big.reshape(count, 128, BIG), small], axis=1)
    home.append(send_home([after(piece, *normed_sent) for piece in parts[2]]))
    packed_grads = after(packed_grads, *home[2])
    packed_sent = packed_grads
    packed_grads = spread(packed_grads)
    small = jnp.swapaxes(packed_grads[:, 128:].reshape(count, 16, 6, 128), 1, 2)
    small = small.reshape(count, SMALL, 128)
    layer_give, layer_keep = combine_rows(
        place, pick_b, after(produced, packed_sent), shared_part
    )
    layer_half = layer_keep + swap(layer_give).astype(F32)
    layer_half, layer_sent = ring_parts(layer_half, x)
    layer_total = residual + sum_sent(layer_half, layer_sent, "x")
    home.append(send_home([after(piece, layer_total) for piece in parts[3]]))
    layer_out = gather_rows(layer_total.astype(BF))
    tokens_grad = gather_rows((mid_grad + input_norm_grad).astype(BF)).astype(F32)
    shared_sum = after(shared_grads, layer_total).astype(F32)
    shared_gate_grad = shared_sum[:, :SHARED]
    shared_up_grad = shared_sum[:, WIDE : WIDE + SHARED]
    shared_down_grad = shared_sum[:, 2 * WIDE : 2 * WIDE + SHARED].T
    big = jnp.sum(packed_grads[:, :128].astype(F32), axis=0)
    q_width = q_weight.shape[1]
    q_weight_grad = big[:, :q_width]
    out_weight_grad = big[:, q_width : q_width + ATT].T
    kv_up_grad = jnp.swapaxes(big[:, q_width + ATT :].reshape(4, up_rows, 128), 0, 1).reshape(
        up_rows, 4 * 128
    )

    small = small.astype(F32)
    wide = kd_width + rt_width
    small_sum = jnp.sum(small[:, : wide + 6], axis=0)
    peaks = small[:, wide + 6 : wide + 9, :heads]
    top_peak = jnp.max(peaks[:, 0] + peaks[:, 1] + peaks[:, 2], axis=0)
    vectors = small_sum[wide : wide + 6].reshape(3, 2, 128).sum(axis=1)
    vector_high, vector_low = split_two(vectors)
    shared_small = jnp.concatenate(
        [small_sum[:wide].astype(BF), vector_high, vector_low, jnp.zeros((10, 128), BF)], axis=0
    )
    all_small = lax.all_to_all(
        jnp.broadcast_to(after(shared_small, *home[3])[None], (8, wide + 16, 128)), TENSOR, split_axis=0,
        concat_axis=0, tiled=True,
    )
    expert_gate_grad, expert_up_grad, expert_down_grad = unpack(
        x, [after(home[0], shared_small), *home[1:]]
    )
    all_small = after(all_small, expert_gate_grad, tokens_grad)
    expert_gate_grad = jnp.swapaxes(expert_gate_grad, 1, 2)
    expert_up_grad = jnp.swapaxes(expert_up_grad, 1, 2)
    kv_down_grad = all_small[:, :kd_width].reshape(8 * kd_width, 128).T.astype(F32)
    router_grad = all_small[:, kd_width:wide].reshape(8 * rt_width, 128).T.astype(F32)
    vectors = jnp.sum(all_small[:, wide : wide + 6].astype(F32), axis=0).reshape(2, 3, 128).sum(axis=0)
    norm_gain_grad = vectors[0]
    mix_gain_grad = vectors[1]
    kv_gain_grad = vectors[2, : KVRANK // count]

    factor = jnp.minimum(1.0, threshold[0] / jnp.maximum(top_peak, 1.0))
    root_factor = jnp.sqrt(factor)
    q_rows = q_weight.shape[0] // count
    own_query = lax.dynamic_slice_in_dim(q_weight, j * q_rows, q_rows, 0).astype(F32)
    query_step = (own_query - step_size[0] * q_weight_grad).reshape(q_rows, heads, NOPE + ROPE)
    q_weight_new = jnp.concatenate(
        [
            query_step[..., :NOPE] * root_factor[None, :, None],
            query_step[..., NOPE:] * factor[None, :, None],
        ],
        axis=-1,
    ).reshape(q_rows, heads * (NOPE + ROPE))
    own_up = lax.dynamic_slice_in_dim(kv_up, j * up_rows, up_rows, 0).astype(F32)
    up_step = (own_up - step_size[0] * kv_up_grad).reshape(up_rows, heads, NOPE + VDIM)
    kv_up_new = jnp.concatenate(
        [up_step[..., :NOPE] * root_factor[None, :, None], up_step[..., NOPE:]], axis=-1
    ).reshape(up_rows, heads * (NOPE + VDIM))
    return (
        layer_out,
        tokens_grad,
        q_weight_grad,
        kv_down_grad,
        kv_up_grad,
        out_weight_grad,
        router_grad,
        norm_gain_grad,
        kv_gain_grad,
        mix_gain_grad,
        shared_gate_grad,
        shared_up_grad,
        shared_down_grad,
        expert_gate_grad,
        expert_up_grad,
        expert_down_grad,
        q_weight_new,
        kv_up_new,
    )


def solution(mesh):
    fine = Mesh(mesh.devices.reshape(4, 4, 4, 2), ("z", "y", "x", "c"))
    return jax.shard_map(
        shards,
        mesh=fine,
        in_specs=(
            P(EXPERT, None),
            P(EXPERT, None),
            P(EXPERT, None),
            P(),
            P(),
            P(None, TENSOR),
            P(),
            P(),
            P(None, TENSOR),
            P(TENSOR, None),
            P(),
            P(),
            P(None, TENSOR),
            P(None, TENSOR),
            P(TENSOR, None),
            P(EXPERT, None, TENSOR),
            P(EXPERT, None, TENSOR),
            P(EXPERT, TENSOR, None),
            P(),
            P(),
        ),
        out_specs=(
            P(EXPERT, None),
            P(EXPERT, None),
            P(EXPERT, TENSOR),
            P(EXPERT, None),
            P(EXPERT, TENSOR),
            P(TENSOR, EXPERT),
            P(EXPERT, None),
            P(EXPERT),
            P(EXPERT),
            P(EXPERT),
            P(EXPERT, TENSOR),
            P(EXPERT, TENSOR),
            P(TENSOR, EXPERT),
            P(EXPERT, None, TENSOR),
            P(EXPERT, None, TENSOR),
            P(EXPERT, TENSOR, None),
            P(EXPERT, TENSOR),
            P(EXPERT, TENSOR),
        ),
        check_vma=False,
    )
```

```python
import functools
import math

import jax
import jax.numpy as jnp
from jax import lax
from jax.experimental import pallas as pl
from jax.experimental.pallas import tpu as pltpu
from jax.sharding import Mesh
from jax.sharding import PartitionSpec as P

D = 2048
HALF = D // 2
NOPE = 128
ROPE = 64
VDIM = 128
KVRANK = 512
TOPK = 6
PROMPT = 1024
CONT = 2
EXPERTS = 64
CAP = 48
SPAN = 4
RING = 4
OWN = 48
EPSILON = 1e-06

BF = jnp.bfloat16
F32 = jnp.float32
EXPERT = ("z", "y")
TENSOR = ("x", "c")


def dot(left, right, contract=((1,), (0,))):
    return lax.dot_general(left, right, (contract, ((), ())), preferred_element_type=F32)


def swap(block):
    return lax.ppermute(block, "c", [(0, 1), (1, 0)])


def shift(block, axis, step):
    return lax.ppermute(block, axis, [(i, (i + step) % RING) for i in range(RING)])


def spread(block):
    return lax.all_to_all(block, EXPERT, split_axis=0, concat_axis=0, tiled=True)


def pick_index(blocks, index, axis=0):
    return lax.dynamic_index_in_dim(blocks, index, axis, keepdims=False)


def sum_ring(blocks, axis, index):
    return sum_sent(*ring_parts(blocks, index), axis)


def ring_parts(blocks, index):
    own = pick_index(blocks, index)
    return own, [pick_index(blocks, (index + step) % RING).astype(BF) for step in (1, 2, 3)]


def sum_sent(own, parts, axis):
    for step in (1, 2, 3):
        own = own + shift(parts[step - 1], axis, step).astype(F32)
    return own


def gather_ring(block, axis, index):
    blocks = jnp.zeros((RING,) + block.shape, block.dtype)
    blocks = lax.dynamic_update_index_in_dim(blocks, block, index, 0)
    for step in (1, 2, 3):
        blocks = lax.dynamic_update_index_in_dim(
            blocks, shift(block, axis, step), (index - step) % RING, 0
        )
    return blocks


def gather_pair(block, core):
    blocks = jnp.zeros((2,) + block.shape, block.dtype)
    blocks = lax.dynamic_update_index_in_dim(blocks, block, core, 0)
    return lax.dynamic_update_index_in_dim(blocks, swap(block), 1 - core, 0)


def gather_rows(block):
    return lax.all_gather(block, TENSOR, axis=0, tiled=True)


def after(value, *others):
    return lax.optimization_barrier((value, *others))[0]


PIECE = 176
HIDDEN = RING * PIECE
SLOTS = 16 * CAP
TILE = 256
EXTRA = 128
NT = ((1,), (1,))
TN = ((0,), (0,))
VMEM_LIMIT = 56 << 20
HINT = 64


def whole(*shape):
    return pl.BlockSpec(shape, lambda *_: (0,) * len(shape))


def anywhere():
    return pl.BlockSpec(memory_space=pl.ANY)


def copy_all(pairs, sems):
    copies = [pltpu.make_async_copy(a, b, sems.at[i]) for i, (a, b) in enumerate(pairs)]
    for one in copies:
        one.start()
    for one in copies:
        one.wait()


def cost(flops, bytes_accessed, exps=0):
    return pl.CostEstimate(
        flops=int(flops) // HINT, bytes_accessed=int(bytes_accessed) // HINT, transcendentals=0
    )


OUTWARD = (208, 320)
HOMEWARD = (96, 112, 96, 224)


def spans(parts):
    found, start = [], 0
    for part, size in enumerate(parts):
        at = start
        while at < start + size:
            weight, inside = divmod(at, PIECE)
            length = min(PIECE - inside, start + size - at)
            found.append((part, at - start, weight, inside, length))
            at += length
        start += size
    return found


def pack_kernel(x_ref, *refs):
    for step in range(3):
        for part, at, weight, inside, length in spans(OUTWARD):
            out = refs[9 + step * len(OUTWARD) + part]
            out[at : at + length, :] = refs[3 * step + weight][0, inside : inside + length, :]


def pack(x, gate, up, down):
    block = 512

    def source(step):
        return pl.BlockSpec((1, PIECE, block), lambda i, x: (lax.rem(x[0] + step, RING), 0, i))

    outs = pl.pallas_call(
        pack_kernel,
        grid_spec=pltpu.PrefetchScalarGridSpec(
            num_scalar_prefetch=1,
            grid=(D // block,),
            in_specs=[source(step) for step in (1, 2, 3) for _ in range(3)],
            out_specs=[pl.BlockSpec((size, block), lambda i, _: (0, i)) for size in OUTWARD] * 3,
        ),
        out_shape=[jax.ShapeDtypeStruct((size, D), BF) for size in OUTWARD] * 3,
        compiler_params=pltpu.CompilerParams(vmem_limit_bytes=VMEM_LIMIT),
        cost_estimate=cost(0, 13 << 20),
        name="pack_weights",
    )(x.reshape(1), *((gate, up, down) * 3))
    return [outs[part :: len(OUTWARD)] for part in range(len(OUTWARD))]


def unpack_kernel(x_ref, *refs):
    outs = refs[len(HOMEWARD) * RING :]
    for step in range(RING):
        index = lax.rem(x_ref[0] + step, RING)
        for part, at, weight, inside, length in spans(HOMEWARD):
            piece = refs[part * RING + step]
            outs[weight][index, inside : inside + length, :] = piece[at : at + length, :].astype(F32)


def unpack(x, parts):
    block = 512
    return pl.pallas_call(
        unpack_kernel,
        grid_spec=pltpu.PrefetchScalarGridSpec(
            num_scalar_prefetch=1,
            grid=(D // block,),
            in_specs=[
                pl.BlockSpec((size, block), lambda i, _: (0, i))
                for size in HOMEWARD
                for _ in range(RING)
            ],
            out_specs=[pl.BlockSpec((RING, PIECE, block), lambda i, _: (0, 0, i))] * 3,
        ),
        out_shape=[jax.ShapeDtypeStruct((RING, PIECE, D), F32)] * 3,
        compiler_params=pltpu.CompilerParams(vmem_limit_bytes=VMEM_LIMIT),
        cost_estimate=cost(0, 26 << 20),
        name="unpack_gradients",
    )(x.reshape(1), *[piece for part in parts for piece in part])


def load_weight(which, index, own_ref, parts, weight):
    pairs = [(own_ref.at[index], weight.at[pl.ds(0, PIECE)])]
    for part, at, kind, inside, length in spans(OUTWARD):
        if kind == which:
            for step, piece in enumerate(parts[part]):
                start = (step + 1) * PIECE + inside
                pairs.append((piece.at[pl.ds(at, length)], weight.at[pl.ds(start, length)]))
    return pairs


def halves_of(place_ref):
    core = place_ref[1]
    return (
        pl.ds(pl.multiple_of(core * HALF, HALF), HALF),
        pl.ds(pl.multiple_of((1 - core) * HALF, HALF), HALF),
    )


def expert_kernel(
    place_ref,
    mine_ref,
    other_ref,
    grad_mine_ref,
    grad_other_ref,
    gate_ref,
    own_gate,
    own_up,
    own_down,
    p1,
    p2,
    p3,
    q1,
    q2,
    q3,
    act_ref,
    scaled_ref,
    gate_grad_ref,
    up_grad_ref,
    keep_ref,
    give_ref,
    columns_ref,
    gate_w,
    up_w,
    down_w,
    sems,
):
    @pl.when(pl.program_id(0) == 0)
    def _():
        index = place_ref[0]
        parts = {0: (p1, p2, p3), 1: (q1, q2, q3)}
        copy_all(
            load_weight(0, index, own_gate, parts, gate_w)
            + load_weight(1, index, own_up, parts, up_w)
            + load_weight(2, index, own_down, parts, down_w),
            sems,
        )

    first, second = halves_of(place_ref)
    mine, other = mine_ref[...], other_ref[...]
    extra = gate_ref[...].astype(F32)
    gate = extra[:, 0:1] + extra[:, 1:2]
    gate_lin = dot(mine, gate_w[:, first], NT) + dot(other, gate_w[:, second], NT)
    up_lin = dot(mine, up_w[:, first], NT) + dot(other, up_w[:, second], NT)
    raw = dot(grad_mine_ref[...], down_w[:, first], NT)
    raw = raw + dot(grad_other_ref[...], down_w[:, second], NT)
    sigmoid = jax.nn.sigmoid(gate_lin)
    silu = gate_lin * sigmoid
    act = (silu * up_lin).astype(BF)
    act_ref[...] = act
    act = act.astype(F32)
    scaled_ref[...] = (act * gate).astype(BF)
    act_grad = raw * gate
    gate_grad = (act_grad * up_lin * (sigmoid * (1.0 + gate_lin * (1.0 - sigmoid)))).astype(BF)
    up_grad = (act_grad * silu).astype(BF)
    gate_grad_ref[...] = gate_grad
    up_grad_ref[...] = up_grad
    keep_ref[...] = dot(gate_grad, gate_w[:, first]) + dot(up_grad, up_w[:, first])
    give_ref[...] = (dot(gate_grad, gate_w[:, second]) + dot(up_grad, up_w[:, second])).astype(BF)
    slot_grad = jnp.sum(act * raw, axis=1, keepdims=True)
    high = slot_grad.astype(BF).astype(F32)
    lane = lax.broadcasted_iota(jnp.int32, (TILE, EXTRA), 1)
    expert_id = place_ref[2]
    columns_ref[...] = jnp.where(
        lane == expert_id, high, jnp.where(lane == EXPERTS + expert_id, slot_grad - high, 0.0)
    ).astype(BF)


def expert_pass(place, mine, other, gate, up, down, packed):
    rows = lambda width, at=0: pl.BlockSpec((TILE, width), lambda i, _: (i, at))
    shape = lambda width, dtype: jax.ShapeDtypeStruct((SLOTS, width), dtype)
    return pl.pallas_call(
        expert_kernel,
        grid_spec=pltpu.PrefetchScalarGridSpec(
            num_scalar_prefetch=1,
            grid=(SLOTS // TILE,),
            in_specs=[rows(HALF)] * 2 + [rows(HALF, 1)] * 2 + [rows(EXTRA, D // EXTRA)]
            + [anywhere()] * 9,
            out_specs=[rows(HIDDEN)] * 4 + [rows(HALF)] * 2 + [rows(EXTRA)],
            scratch_shapes=[pltpu.VMEM((HIDDEN, D), BF)] * 3 + [pltpu.SemaphoreType.DMA((15,))],
        ),
        out_shape=[shape(HIDDEN, BF)] * 4
        + [shape(HALF, F32), shape(HALF, BF), shape(EXTRA, BF)],
        compiler_params=pltpu.CompilerParams(vmem_limit_bytes=VMEM_LIMIT),
        cost_estimate=cost(10 * SLOTS * D * HIDDEN, 24 << 20, SLOTS * HIDDEN),
        name="expert_pass",
    )(place, mine, other, mine, other, mine, gate, up, down, *[p for part in packed for p in part])


def produce_kernel(place_ref, act_ref, mine_ref, own_down, p1, p2, p3, keep_ref, give_ref, down, sems):
    @pl.when(pl.program_id(0) == 0)
    def _():
        copy_all(load_weight(2, place_ref[0], own_down, {1: (p1, p2, p3)}, down), sems)

    first, second = halves_of(place_ref)
    extra = mine_ref[...].astype(F32)
    gate = extra[:, 0:1] + extra[:, 1:2]
    keep_ref[...] = dot(act_ref[...], down[:, first]) * gate
    give_ref[...] = (dot(act_ref[...], down[:, second]) * gate).astype(BF)


def produce(place, act, mine, down, packed):
    rows = lambda width: pl.BlockSpec((TILE, width), lambda i, _: (i, 0))
    return pl.pallas_call(
        produce_kernel,
        grid_spec=pltpu.PrefetchScalarGridSpec(
            num_scalar_prefetch=1,
            grid=(SLOTS // TILE,),
            in_specs=[
                rows(HIDDEN),
                pl.BlockSpec((TILE, EXTRA), lambda i, _: (i, D // EXTRA)),
            ]
            + [anywhere()] * 4,
            out_specs=[rows(HALF)] * 2,
            scratch_shapes=[pltpu.VMEM((HIDDEN, D), BF), pltpu.SemaphoreType.DMA((4,))],
        ),
        out_shape=[
            jax.ShapeDtypeStruct((SLOTS, HALF), F32),
            jax.ShapeDtypeStruct((SLOTS, HALF), BF),
        ],
        compiler_params=pltpu.CompilerParams(vmem_limit_bytes=VMEM_LIMIT),
        cost_estimate=cost(2 * SLOTS * D * HIDDEN, 9 << 20),
        name="produce",
    )(place, act, mine, down, *packed[1])


def weight_grad_kernel(place_ref, *refs, weights, parts):
    lefts = refs[: len(weights)]
    rights, outs = refs[len(weights) : -len(parts) * RING], refs[-len(parts) * RING :]
    own = pl.program_id(0) < 2
    rights = [jnp.where(own, rights[i][...], rights[i + 1][...]) for i in range(0, len(rights), 2)]
    for left, weight in zip(lefts, weights):
        right = rights[1] if weight == 2 and len(rights) > 1 else rights[0]
        product = dot(left[...], right, TN).astype(BF)
        for step in range(RING):
            for part, at, kind, inside, length in spans(HOMEWARD):
                if kind == weight:
                    start = step * PIECE + inside
                    out = outs[parts.index(part) * RING + step]
                    out[at : at + length, :] = product[start : start + length, :]


def weight_grads(place, weights, parts, lefts, rows):
    block = HALF // 2
    mine = [pl.BlockSpec((SLOTS, block), lambda i, _, at=at: (0, at + jnp.minimum(i, 1))) for at in (0, 2)]
    other = [
        pl.BlockSpec((SLOTS, block), lambda i, _, at=at: (0, at + jnp.maximum(i - 2, 0)))
        for at in (0, 2)
    ]
    sizes = [HOMEWARD[part] for part in parts for _ in range(RING)]
    outs = pl.pallas_call(
        functools.partial(weight_grad_kernel, weights=weights, parts=parts),
        grid_spec=pltpu.PrefetchScalarGridSpec(
            num_scalar_prefetch=1,
            grid=(4,),
            in_specs=[whole(SLOTS, HIDDEN)] * len(lefts)
            + [mine[0], other[0], mine[1], other[1]],
            out_specs=[
                pl.BlockSpec((size, block), lambda i, place: (0, lax.rem(2 * place[1] + i, 4)))
                for size in sizes
            ],
        ),
        out_shape=[jax.ShapeDtypeStruct((size, D), BF) for size in sizes],
        compiler_params=pltpu.CompilerParams(vmem_limit_bytes=VMEM_LIMIT),
        cost_estimate=cost(2 * len(lefts) * SLOTS * D * HIDDEN, 18 << 20),
        name="weight_grads",
    )(place, *lefts, *rows, *rows)
    return [outs[i * RING : (i + 1) * RING] for i in range(len(parts))]


SHARED = 352
WIDE = 384
ATT = 2 * VDIM


def shared_kernel(mixed, out_grad, gate_w, up_w, down_w, part, mixed_grad, grads):
    gate_lin = dot(mixed[...], gate_w[...], NT)
    up_lin = dot(mixed[...], up_w[...], NT)
    sigmoid = jax.nn.sigmoid(gate_lin)
    silu = gate_lin * sigmoid
    act = (silu * up_lin).astype(BF)
    act_grad = dot(out_grad[...], down_w[...], NT)
    gate_grad = (act_grad * up_lin * (sigmoid * (1.0 + gate_lin * (1.0 - sigmoid)))).astype(BF)
    up_grad = (act_grad * silu).astype(BF)
    for start in range(0, D, 512):
        at = slice(start, start + 512)
        part[:, at] = dot(act, down_w[:, at])
        mixed_grad[:, at] = dot(gate_grad, gate_w[:, at]) + dot(up_grad, up_w[:, at])
        zeros = jnp.zeros((512, WIDE - SHARED), BF)
        for i, (left, right) in enumerate(((mixed, gate_grad), (mixed, up_grad), (out_grad, act))):
            start = i * WIDE
            grads[at, start : start + SHARED] = dot(left[:, at], right, TN).astype(BF)
            grads[at, start + SHARED : start + WIDE] = zeros


def shared_experts(mixed, out_grad, gate_w, up_w, down_w):
    args = (mixed, out_grad, gate_w, up_w, down_w)
    rows = mixed.shape[0]
    outs = [
        jax.ShapeDtypeStruct((rows, D), F32),
        jax.ShapeDtypeStruct((rows, D), F32),
        jax.ShapeDtypeStruct((D, 3 * WIDE), BF),
    ]
    return pl.pallas_call(
        shared_kernel,
        grid=(1,),
        in_specs=[whole(*arg.shape) for arg in args],
        out_specs=[whole(*out.shape) for out in outs],
        out_shape=outs,
        compiler_params=pltpu.CompilerParams(vmem_limit_bytes=VMEM_LIMIT),
        cost_estimate=cost(18 * rows * D * SHARED, 18 << 20, rows * SHARED),
        name="shared_experts",
    )(*args)


GROUP = 1536
ROWS = 384
LATENT = KVRANK + ROPE
HEADS = 2
HEAD = NOPE + ROPE
SCALE = 1.0 / math.sqrt(HEAD)


def turn(block, cosine, sine):
    half = ROPE // 2
    return block * cosine + jnp.concatenate([block[:, half:], block[:, :half]], axis=1) * sine


def mask_bias(seg_keys, seg_rows, row_start):
    key = lax.broadcasted_iota(jnp.int32, (GROUP, ROWS), 0)
    row = lax.broadcasted_iota(jnp.int32, (GROUP, ROWS), 1) + row_start
    same = (seg_keys == seg_rows) & (key <= row)
    return jnp.where(same | ((seg_keys == 0) & (seg_rows > 0)), 0.0, -1e30)


def wide_tables(cos, sin):
    return jnp.concatenate([cos, cos], axis=1), jnp.concatenate([-sin, sin], axis=1)


def row_tables(cos_ref, sin_ref, row_start):
    at = pl.ds(pl.multiple_of(row_start, ROWS), ROWS)
    return wide_tables(cos_ref[at, :], sin_ref[at, :])


def head_queries(query, row_cos, row_sin, head):
    start = head * HEAD
    plain = query[:, start : start + NOPE].astype(BF)
    return plain, turn(query[:, start + NOPE : start + HEAD], row_cos, row_sin).astype(BF)


def attention_kernel(
    place_ref,
    mine_ref,
    other_ref,
    query_ref,
    gain_ref,
    kv_up_ref,
    out_weight_ref,
    cos_ref,
    sin_ref,
    seg_keys_ref,
    seg_rows_ref,
    give_ref,
    keep_ref,
    attended_ref,
    compressed_ref,
    kv_ref,
    key_rot_ref,
    log_total_ref,
    peak_ref,
    latent,
    attended,
):
    core = place_ref[1]
    half = ROWS // 2
    for block in range(SPAN):
        start = pl.multiple_of(block * ROWS + core * half, half)
        latent[pl.ds(start, half), :] = mine_ref[block]
        start = pl.multiple_of(block * ROWS + (1 - core) * half, half)
        latent[pl.ds(start, half), :] = other_ref[block]
    inputs = latent[:, :KVRANK].astype(F32)
    inverse = lax.rsqrt(jnp.mean(inputs * inputs, axis=1, keepdims=True) + EPSILON)
    compressed_ref[...] = (inputs * inverse * gain_ref[...]).astype(BF)
    kv_ref[...] = dot(compressed_ref[...], kv_up_ref[...]).astype(BF)
    cosine, sine = wide_tables(cos_ref[...], sin_ref[...])
    key_rot_ref[...] = turn(latent[:, KVRANK:].astype(F32), cosine, sine).astype(BF)
    seg_rows = seg_rows_ref[:, pl.ds(pl.multiple_of(place_ref[3], ROWS), ROWS)]
    bias = mask_bias(seg_keys_ref[...], seg_rows, place_ref[3])
    row_cos, row_sin = row_tables(cos_ref, sin_ref, place_ref[3])
    for head in range(HEADS):
        plain, turned = head_queries(query_ref, row_cos, row_sin, head)
        start = head * (NOPE + VDIM)
        scores = dot(kv_ref[:, start : start + NOPE], plain, NT)
        scores = (scores + dot(key_rot_ref[...], turned, NT)) * SCALE + bias
        peak = jnp.max(scores, axis=0, keepdims=True)
        powers = jnp.exp(scores - peak)
        total = jnp.sum(powers, axis=0, keepdims=True)
        log_total_ref[head : head + 1, :] = peak + jnp.log(total)
        peak_ref[head : head + 1, :] = peak
        weights = (powers * (1.0 / total)).astype(BF)
        values = kv_ref[:, start + NOPE : start + NOPE + VDIM]
        attended[:, head * VDIM : (head + 1) * VDIM] = dot(values, weights, TN).T
    attended_ref[...] = attended[...].astype(BF)
    for block in range(RING):
        for out, which in ((give_ref, 1 - core), (keep_ref, core)):
            start = pl.multiple_of(block * 2 * OWN + which * OWN, OWN)
            out[block] = dot(
                attended[pl.ds(start, OWN), :].astype(BF), out_weight_ref[...]
            ).astype(out.dtype)


def attention(place, mine, other, query, gain, kv_up, out_weight, tables, segs):
    shape = jax.ShapeDtypeStruct
    args = (mine, other, query, gain.reshape(1, KVRANK), kv_up, out_weight, *tables, *segs)
    outs = [
        shape((RING, OWN, D), BF),
        shape((RING, OWN, D), F32),
        shape((ROWS, HEADS * VDIM), BF),
        shape((GROUP, KVRANK), BF),
        shape((GROUP, HEADS * (NOPE + VDIM)), BF),
        shape((GROUP, ROPE), BF),
        shape((HEADS, ROWS), F32),
        shape((HEADS, ROWS), F32),
    ]
    return pl.pallas_call(
        attention_kernel,
        grid_spec=pltpu.PrefetchScalarGridSpec(
            num_scalar_prefetch=1,
            grid=(1,),
            in_specs=[whole(*arg.shape) for arg in args],
            out_specs=[whole(*out.shape) for out in outs],
            scratch_shapes=[
                pltpu.VMEM((GROUP, LATENT), BF),
                pltpu.VMEM((ROWS, HEADS * VDIM), F32),
            ],
        ),
        out_shape=outs,
        compiler_params=pltpu.CompilerParams(vmem_limit_bytes=VMEM_LIMIT),
        cost_estimate=cost(3e9, 14 << 20, 2 * GROUP * ROWS),
        name="attention_forward",
    )(place, *args)


def attention_back_kernel(
    place_ref,
    mine_ref,
    other_ref,
    query_ref,
    compressed_ref,
    kv_ref,
    key_rot_ref,
    log_total_ref,
    kv_up_ref,
    out_weight_ref,
    cos_ref,
    sin_ref,
    seg_keys_ref,
    seg_rows_ref,
    q_weight_ref,
    give_ref,
    keep_ref,
    kv_grad_ref,
    query_grad_ref,
    branch_ref,
    normed_give_ref,
    normed_keep_ref,
    comp_grad,
    rot_grad,
):
    core = place_ref[1]
    interleave(core, mine_ref, other_ref, branch_ref, D + EXTRA)
    attended_grad = dot(branch_ref[:, :D], out_weight_ref[...], NT).astype(BF)
    seg_rows = seg_rows_ref[:, pl.ds(pl.multiple_of(place_ref[3], ROWS), ROWS)]
    bias = mask_bias(seg_keys_ref[...], seg_rows, place_ref[3])
    row_cos, row_sin = row_tables(cos_ref, sin_ref, place_ref[3])
    turned_sum = 0.0
    query_grads = []
    for head in range(HEADS):
        plain, turned = head_queries(query_ref, row_cos, row_sin, head)
        start = head * (NOPE + VDIM)
        keys = kv_ref[:, start : start + NOPE]
        values = kv_ref[:, start + NOPE : start + NOPE + VDIM]
        key_rot = key_rot_ref[...]
        scores = (dot(keys, plain, NT) + dot(key_rot, turned, NT)) * SCALE + bias
        probs = jnp.exp(scores - log_total_ref[head : head + 1, :])
        grad = attended_grad[:, head * VDIM : (head + 1) * VDIM]
        value_grad = dot(probs.astype(BF), grad)
        prob_grad = dot(values, grad, NT)
        inner = jnp.sum(probs * prob_grad, axis=0, keepdims=True)
        score_grad = (probs * (prob_grad - inner)).astype(BF)
        kv_grad_ref[:, start : start + NOPE] = (dot(score_grad, plain) * SCALE).astype(BF)
        kv_grad_ref[:, start + NOPE : start + NOPE + VDIM] = value_grad.astype(BF)
        turned_sum = turned_sum + dot(score_grad, turned) * SCALE
        query_grads.append((dot(keys, score_grad, TN) * SCALE).T)
        turned_grad = (dot(key_rot, score_grad, TN) * SCALE).T
        query_grads.append(turn(turned_grad, row_cos, -row_sin))
    comp_grad[...] = dot(kv_grad_ref[...], kv_up_ref[...], NT)
    cosine, sine = wide_tables(cos_ref[...], sin_ref[...])
    rot_grad[...] = turn(turned_sum, cosine, -sine)
    for block in range(SPAN):
        for inner in range(RING):
            for out, which in ((give_ref, 1 - core), (keep_ref, core)):
                start = pl.multiple_of(block * ROWS + inner * 2 * OWN + which * OWN, OWN)
                out[block, inner, :, :KVRANK] = comp_grad[pl.ds(start, OWN), :].astype(out.dtype)
                out[block, inner, :, KVRANK:] = rot_grad[pl.ds(start, OWN), :].astype(out.dtype)
    query_grad_ref[...] = jnp.concatenate(query_grads, axis=1).astype(BF)
    for block in range(RING):
        for out, which in ((normed_give_ref, 1 - core), (normed_keep_ref, core)):
            start = pl.multiple_of(block * 2 * OWN + which * OWN, OWN)
            part = query_grad_ref[pl.ds(start, OWN), :]
            out[block] = dot(part, q_weight_ref[...], NT).astype(out.dtype)


def attention_back(
    place, mine, other, query, compressed, kv, key_rot, log_total, kv_up, out_weight, tables, segs,
    q_weight,
):
    shape = jax.ShapeDtypeStruct
    args = (
        mine, other, query, compressed, kv, key_rot, log_total, kv_up, out_weight, *tables, *segs,
        q_weight,
    )
    outs = [
        shape((SPAN, RING, OWN, LATENT), BF),
        shape((SPAN, RING, OWN, LATENT), F32),
        shape((GROUP, HEADS * (NOPE + VDIM)), BF),
        shape((ROWS, HEADS * HEAD), BF),
        shape((ROWS, D + EXTRA), BF),
        shape((RING, OWN, D), BF),
        shape((RING, OWN, D), F32),
    ]
    return pl.pallas_call(
        attention_back_kernel,
        grid_spec=pltpu.PrefetchScalarGridSpec(
            num_scalar_prefetch=1,
            grid=(1,),
            in_specs=[whole(*arg.shape) for arg in args],
            out_specs=[whole(*out.shape) for out in outs],
            scratch_shapes=[pltpu.VMEM((GROUP, KVRANK), F32), pltpu.VMEM((GROUP, ROPE), F32)],
        ),
        out_shape=outs,
        compiler_params=pltpu.CompilerParams(vmem_limit_bytes=VMEM_LIMIT),
        cost_estimate=cost(4e9, 16 << 20, 2 * GROUP * ROWS),
        name="attention_backward",
    )(place, *args)


UP_ROWS = KVRANK // 16
BIG = HEADS * HEAD + ATT + 128


def projection_grad_kernel(
    normed, branch, compressed, query_grad, attended, kv_grad, out
):
    width = HEADS * HEAD
    out[:, :width] = dot(normed[...], query_grad[...], TN).astype(BF)
    out[:, width : width + ATT] = dot(branch[...], attended[...], TN).astype(BF)
    up = dot(compressed[...], kv_grad[...], TN)
    for index in range(4):
        for part in range(4):
            start = index * 128 + part * UP_ROWS
            out[start : start + UP_ROWS, width + ATT :] = up[
                index * UP_ROWS : (index + 1) * UP_ROWS, part * 128 : (part + 1) * 128
            ].astype(BF)


def projection_grads(normed, branch, compressed, query_grad, attended, kv_grad):
    block = 512
    return pl.pallas_call(
        projection_grad_kernel,
        grid=(D // block,),
        in_specs=[
            pl.BlockSpec((ROWS, block), lambda i: (0, i)),
            pl.BlockSpec((ROWS, block), lambda i: (0, i)),
            pl.BlockSpec((GROUP, 128), lambda i: (0, i)),
            whole(ROWS, HEADS * HEAD),
            whole(ROWS, ATT),
            whole(GROUP, HEADS * (NOPE + VDIM)),
        ],
        out_specs=pl.BlockSpec((block, BIG), lambda i: (i, 0)),
        out_shape=jax.ShapeDtypeStruct((D, BIG), BF),
        compiler_params=pltpu.CompilerParams(vmem_limit_bytes=VMEM_LIMIT),
        cost_estimate=cost(2e9, 10 << 20),
        name="projection_grads",
    )(normed, branch, compressed, query_grad, attended, kv_grad)


def combine_kernel(place_ref, pick_ref, returned_ref, shared_ref, give_ref, keep_ref, total):
    core = place_ref[1]
    rows = dot(pick_ref[...], returned_ref[...], TN)
    total[:, :D] = shared_ref[...]
    mine = pl.ds(pl.multiple_of(core * HALF, HALF), HALF)
    total[:, mine] = total[:, mine] + rows[:, :HALF]
    if returned_ref.shape[1] > HALF:
        total[:, D:] = rows[:, HALF:]
    for block in range(RING):
        for out, which in ((give_ref, 1 - core), (keep_ref, core)):
            start = pl.multiple_of(block * 2 * OWN + which * OWN, OWN)
            out[block] = total[pl.ds(start, OWN), :].astype(out.dtype)


def combine_rows(place, pick, returned, shared):
    width = D + returned.shape[1] - HALF
    args = (pick, returned, shared)
    outs = [
        jax.ShapeDtypeStruct((RING, OWN, width), BF),
        jax.ShapeDtypeStruct((RING, OWN, width), F32),
    ]
    return pl.pallas_call(
        combine_kernel,
        grid_spec=pltpu.PrefetchScalarGridSpec(
            num_scalar_prefetch=1,
            grid=(1,),
            in_specs=[whole(*arg.shape) for arg in args],
            out_specs=[whole(*out.shape) for out in outs],
            scratch_shapes=[pltpu.VMEM((ROWS, width), F32)],
        ),
        out_shape=outs,
        compiler_params=pltpu.CompilerParams(vmem_limit_bytes=VMEM_LIMIT),
        cost_estimate=cost(7e8, 8 << 20),
        name="combine_rows",
    )(place, *args)


def order_kernel(x_ref, *refs):
    for step in range(RING):
        refs[RING][lax.rem(x_ref[0] + RING - step, RING)] = refs[step][...]


def order_ring(x, blocks):
    rows, width = blocks[0].shape
    return pl.pallas_call(
        order_kernel,
        grid_spec=pltpu.PrefetchScalarGridSpec(
            num_scalar_prefetch=1,
            grid=(1,),
            in_specs=[whole(rows, width)] * RING,
            out_specs=whole(RING, rows, width),
        ),
        out_shape=jax.ShapeDtypeStruct((RING, rows, width), blocks[0].dtype),
        cost_estimate=cost(0, 2 << 20),
        name="order_ring",
    )(x.reshape(1), *blocks)


def interleave(core, mine_ref, other_ref, out, width):
    for block in range(RING):
        for ref, which in ((mine_ref, core), (other_ref, 1 - core)):
            start = pl.multiple_of(block * 2 * OWN + which * OWN, OWN)
            out[pl.ds(start, OWN), :] = ref[block, :, :width]


def gating_kernel(
    place_ref, mine_ref, other_ref, router_ref, pick_ref, grad_ref, mixed_ref, probs_ref, sent_ref
):
    core = place_ref[1]
    interleave(core, mine_ref, other_ref, mixed_ref, D)
    logits = dot(mixed_ref[...], router_ref[...])
    powers = jnp.exp(logits - jnp.max(logits, axis=1, keepdims=True))
    probs = powers / jnp.sum(powers, axis=1, keepdims=True)
    probs_ref[...] = probs
    pick = pick_ref[...]
    high = probs.astype(BF)
    rest = probs - high.astype(F32)
    middle = rest.astype(BF)
    low = (rest - middle.astype(F32)).astype(BF)
    gates = dot(pick, high) + dot(pick, middle) + dot(pick, low)
    slot = lax.broadcasted_iota(jnp.int32, (SLOTS, EXPERTS), 0)
    lane = lax.broadcasted_iota(jnp.int32, (SLOTS, EXPERTS), 1)
    first = (lane - place_ref[0]) * (CAP // 4)
    inside = (slot >= first) & (slot < first + CAP) & (lax.rem(lane, 4) == place_ref[0])
    gate = jnp.sum(jnp.where(inside, gates, 0.0), axis=1, keepdims=True)
    high = gate.astype(BF).astype(F32)
    lane = lax.broadcasted_iota(jnp.int32, (SLOTS, EXTRA), 1)
    sent_ref[:, D:] = jnp.where(
        lane == 0, high, jnp.where(lane == 1, gate - high, 0.0)
    ).astype(BF)
    mine = pl.ds(pl.multiple_of(core * HALF, HALF), HALF)
    sent_ref[:, :HALF] = dot(pick, mixed_ref[:, mine]).astype(BF)
    sent_ref[:, HALF:D] = dot(pick, grad_ref[:, mine]).astype(BF)


def gating(place, mine, other, router, pick, out_grad):
    args = (mine, other, router, pick, out_grad)
    outs = [
        jax.ShapeDtypeStruct((ROWS, D), BF),
        jax.ShapeDtypeStruct((ROWS, EXPERTS), F32),
        jax.ShapeDtypeStruct((SLOTS, D + EXTRA), BF),
    ]
    return pl.pallas_call(
        gating_kernel,
        grid_spec=pltpu.PrefetchScalarGridSpec(
            num_scalar_prefetch=1,
            grid=(1,),
            in_specs=[whole(*arg.shape) for arg in args],
            out_specs=[whole(*out.shape) for out in outs],
        ),
        out_shape=outs,
        compiler_params=pltpu.CompilerParams(vmem_limit_bytes=VMEM_LIMIT),
        cost_estimate=cost(8e8, 6 << 20),
        name="gating",
    )(place, *args)


KD_COLUMNS = LATENT // 8
ROUTER_COLUMNS = EXPERTS // 8
SHARE = KD_COLUMNS + ROUTER_COLUMNS
SMALL = SHARE + 16


def small_kernel(latent, logit, normed, mixed, norm_gain, mix_gain, kv_gain, peak_ref, out):
    kv_down = dot(latent[...], normed[...], TN)
    router = dot(logit[...], mixed[...], TN)
    lane = lax.broadcasted_iota(jnp.int32, (1, 128), 1)
    peak = 0.0
    for head in range(HEADS):
        highest = jnp.max(peak_ref[head : head + 1, :], axis=1, keepdims=True)
        peak = jnp.where(lane == head, highest, peak)

    def parts(row, number):
        found = []
        for _ in range(number):
            found.append(row.astype(BF).astype(F32))
            row = row - found[-1]
        return found

    peaks = parts(peak, 3)
    zeros = jnp.zeros((7, 128), F32)
    for index in range(16):
        at = slice(index * 128, (index + 1) * 128)
        gain = kv_gain[:, index * UP_ROWS : (index + 1) * UP_ROWS]
        gain = jnp.concatenate([gain, jnp.zeros((1, 128 - UP_ROWS), F32)], axis=1)
        rows = parts(norm_gain[:, at], 2) + parts(mix_gain[:, at], 2) + parts(gain, 2)
        rows = [kv_down[:, at], router[:, at]] + rows + peaks + [zeros]
        out[index] = jnp.concatenate(rows, axis=0).astype(BF)


def small_grads(latent, logit, normed, mixed, norm_gain, mix_gain, kv_gain, peak):
    args = (
        latent,
        logit,
        normed,
        mixed,
        norm_gain.reshape(1, D),
        mix_gain.reshape(1, D),
        kv_gain.reshape(1, KVRANK),
        peak,
    )
    return pl.pallas_call(
        small_kernel,
        grid=(1,),
        in_specs=[whole(*arg.shape) for arg in args],
        out_specs=whole(16, SMALL, 128),
        out_shape=jax.ShapeDtypeStruct((16, SMALL, 128), BF),
        compiler_params=pltpu.CompilerParams(vmem_limit_bytes=VMEM_LIMIT),
        cost_estimate=cost(2e8, 4 << 20),
        name="small_grads",
    )(*args)


def split_two(value):
    high = lax.reduce_precision(value, 8, 7)
    return high.astype(BF), (value - high).astype(BF)


def norm_rows(inputs, gain_vec):
    inverse = lax.rsqrt(jnp.mean(inputs * inputs, axis=-1, keepdims=True) + EPSILON)
    return (inputs * inverse * gain_vec, inverse)


def norm_back(inputs, inverse, gain_vec, gradient):
    weighted = gradient * gain_vec
    inner = jnp.mean(weighted * inputs, axis=-1, keepdims=True)
    d_inputs = inverse * weighted - inputs * (inverse * inverse * inverse) * inner
    return (d_inputs, jnp.sum(gradient * inputs * inverse, axis=0))


def rotate(inputs, cosine, sine):
    half_size = inputs.shape[-1] // 2
    first_half = inputs[..., :half_size]
    second_half = inputs[..., half_size:]
    return jnp.concatenate(
        [first_half * cosine - second_half * sine, second_half * cosine + first_half * sine],
        axis=-1,
    )


def unrotate(gradient, cosine, sine):
    return rotate(gradient, cosine, -sine)


def shards(
    tokens,
    out_grad,
    routes,
    segment,
    norm_gain,
    q_weight,
    kv_down,
    kv_gain,
    kv_up,
    out_weight,
    mix_gain,
    router,
    shared_gate,
    shared_up,
    shared_down,
    expert_gate,
    expert_up,
    expert_down,
    step_size,
    threshold,
):
    rows = tokens.shape[0]
    x = lax.axis_index("x")
    c = lax.axis_index("c")
    y = lax.axis_index("y")
    z = lax.axis_index("z")
    j = z * RING + y
    t = x * 2 + c
    heads = q_weight.shape[1] // (NOPE + ROPE)
    group_len = rows * SPAN
    count = expert_down.shape[0] * 4
    score_scale = 1.0 / math.sqrt(NOPE + ROPE)
    own_start = t * OWN

    def own_rows(array):
        return lax.dynamic_slice_in_dim(array, own_start, OWN, 0)

    routes_t = routes.T
    chosen = 4 * jnp.arange(count, dtype=jnp.int32) + x
    hot = jnp.any(routes_t[None, :, :] == chosen[:, None, None], axis=1)
    number = jnp.arange(rows, dtype=jnp.int32)
    earlier = (number[:, None] < number[None, :]).astype(BF)
    slot = dot(hot.astype(BF), earlier)
    pick = hot[:, None, :] & (slot[:, None, :] == jnp.arange(CAP, dtype=F32)[None, :, None])
    pick_b = pick.astype(BF).reshape(count * CAP, rows)

    place = jnp.stack([x, c, 4 * j + x, y * rows]).astype(jnp.int32)

    def send_rows(sent):
        width = sent.shape[1]
        return spread(sent.reshape(count, CAP, width)).reshape(count * CAP, width)

    gate_t = jnp.swapaxes(expert_gate, 1, 2)
    up_t = jnp.swapaxes(expert_up, 1, 2)
    first_part, last_part = pack(x, gate_t, up_t, expert_down)
    first_part = [shift(first_part[step - 1], "x", step) for step in (1, 2, 3)]

    group_ids = lax.dynamic_slice_in_dim(segment, z * group_len, group_len)
    key_number = jnp.arange(group_len, dtype=jnp.int32)
    first_length = jnp.sum((group_ids == 1).astype(jnp.int32))
    key_place = jnp.where(
        group_ids == 0,
        key_number - (group_len - PROMPT),
        key_number + PROMPT - jnp.where(group_ids == 1, 0, first_length),
    )
    frequency = jnp.power(10000.0, -2.0 * jnp.arange(ROPE // 2, dtype=F32) / ROPE)
    key_angle = key_place.astype(F32)[:, None] * frequency[None, :]
    tables = (jnp.cos(key_angle), jnp.sin(key_angle))
    segs = (group_ids.reshape(group_len, 1), group_ids.reshape(1, group_len))

    x_input = after(tokens, last_part[0]).astype(F32)
    normed_f, _ = norm_rows(x_input, norm_gain)
    normed = normed_f.astype(BF)
    latent = dot(normed, kv_down).astype(BF)
    half_latent = lax.dynamic_slice_in_dim(latent, c * (rows // 2), rows // 2, 0)
    gathered = gather_ring(half_latent, "y", y)
    query_lin = dot(normed, q_weight)
    attn_give, attn_keep, attended_b, compressed, kv_rows, key_rot, log_total, row_peak = attention(
        place, gathered, swap(gathered), query_lin, kv_gain, kv_up, out_weight, tables, segs
    )

    attn_got = swap(after(attn_give, *first_part))
    attn_own, attn_sent = ring_parts(attn_keep + attn_got.astype(F32), x)
    residual = own_rows(tokens).astype(F32) + sum_sent(attn_own, attn_sent, "x")
    mixed_f, inverse_two = norm_rows(residual, mix_gain)
    mixed_own = mixed_f.astype(BF)
    mixed_ring = [mixed_own] + [shift(mixed_own, "x", step) for step in (1, 2, 3)]
    mixed_mine = order_ring(x, mixed_ring)
    last_part = [after(piece, mixed_mine) for piece in last_part]
    last_part = [shift(last_part[step - 1], "x", step) for step in (1, 2, 3)]
    packed = (first_part, last_part)
    mixed_other = swap(mixed_mine)

    mixed_in, gate_probs, mixed_sent = gating(
        place, mixed_mine, mixed_other, router, pick_b, out_grad
    )
    mixed_rows = send_rows(mixed_sent)
    shared_part, shared_mixed_grad, shared_grads = shared_experts(
        after(mixed_in, mixed_sent), out_grad, shared_gate.T, shared_up.T, shared_down
    )
    mixed_rows = after(mixed_rows, shared_part, *last_part)
    mixed_rows = (mixed_rows, swap(mixed_rows))
    expert_act, scaled_act, gate_lin_grad, up_lin_grad, grad_keep, grad_give, slot_cols = (
        expert_pass(place, *mixed_rows, gate_t, up_t, expert_down, packed)
    )

    grad_half = (grad_keep + swap(grad_give).astype(F32)).astype(BF)
    sent_grad = jnp.concatenate([grad_half, slot_cols], axis=1)
    returned_grad = send_rows(sent_grad)
    parts = weight_grads(
        place,
        (0, 1, 2),
        (0, 1, 2, 3),
        (gate_lin_grad, up_lin_grad, after(scaled_act, sent_grad)),
        mixed_rows,
    )

    def send_home(part):
        return [part[0]] + [shift(part[step], "x", RING - step) for step in (1, 2, 3)]

    home = [send_home(parts[0])]
    produced_keep, produced_give = produce(
        place, after(expert_act, parts[0][0]), mixed_rows[0], expert_down, packed
    )
    mixed_give, mixed_keep = combine_rows(
        place, pick_b, after(returned_grad, parts[0][0], produced_give), shared_mixed_grad
    )
    mixed_half = mixed_keep + swap(after(mixed_give, *home[0])).astype(F32)
    mixed_half, mixed_sent = ring_parts(mixed_half, x)
    shared_grads = lax.psum_scatter(
        after(shared_grads, mixed_rows[0]), EXPERT, scatter_dimension=0, tiled=True
    )
    produced_half = (produced_keep + swap(produced_give).astype(F32)).astype(BF)
    produced = send_rows(after(produced_half, *mixed_sent))
    mixed_total = sum_sent(mixed_half, mixed_sent, "x")
    prob_grad = mixed_total[:, D : D + EXPERTS] + mixed_total[:, D + EXPERTS :]
    own_probs = own_rows(gate_probs)
    logit_grad = (
        own_probs * (prob_grad - jnp.sum(own_probs * prob_grad, axis=-1, keepdims=True))
    ).astype(BF)
    mixed_grad = mixed_total[:, :D] + dot(logit_grad, router, ((1,), (1,)))
    mid_norm_grad, mix_gain_grad = norm_back(residual, inverse_two, mix_gain, mixed_grad)
    mid_grad = own_rows(out_grad).astype(F32) + mid_norm_grad
    branch_own = jnp.concatenate(
        [mid_grad.astype(BF), logit_grad, jnp.zeros((OWN, 128 - EXPERTS), BF)], axis=1
    )
    branch_ring = [branch_own] + [shift(branch_own, "x", step) for step in (1, 2, 3)]
    branch_mine = order_ring(x, branch_ring)
    home.append(send_home([after(piece, branch_mine) for piece in parts[1]]))
    (
        latent_give, latent_keep, kv_grad, query_lin_grad, branch_all, normed_give, normed_keep,
    ) = attention_back(
        place, branch_mine, swap(branch_mine), query_lin, compressed, kv_rows, key_rot, log_total, kv_up, out_weight,
        tables, segs, q_weight,
    )
    latent_give = after(latent_give, produced, *home[1])
    latent_sent = (latent_keep + swap(latent_give).astype(F32)).astype(BF)
    latent_parts = lax.all_to_all(
        latent_sent.reshape(SPAN * RING, OWN, LATENT), ("y", "x"), split_axis=0, concat_axis=0,
        tiled=True,
    )
    latent_total = jnp.sum(latent_parts.astype(F32), axis=0)
    normed_half = normed_keep + swap(after(normed_give, latent_sent)).astype(F32)
    normed_own, normed_sent = ring_parts(normed_half, x)
    normed_total = sum_sent(normed_own, normed_sent, "x")

    logit_grad_all = branch_all[:, D : D + EXPERTS]
    own_comp = own_rows(latent)[:, :KVRANK].astype(F32)
    _, own_inverse = norm_rows(own_comp, kv_gain)
    comp_own_grad, kv_gain_grad = norm_back(
        own_comp, own_inverse, kv_gain, latent_total[:, :KVRANK]
    )
    latent_grad = jnp.concatenate([comp_own_grad, latent_total[:, KVRANK:]], axis=-1).astype(BF)
    latent_columns = jnp.swapaxes(latent_grad.reshape(OWN, 8, KD_COLUMNS), 0, 1)
    big = projection_grads(
        normed, branch_all, compressed, query_lin_grad, attended_b, after(kv_grad, latent_columns)
    )
    latent_columns = lax.all_to_all(
        latent_columns, TENSOR, split_axis=0, concat_axis=0, tiled=True
    )
    normed_grad = normed_total + dot(latent_grad, kv_down, ((1,), (1,)))
    own_input = own_rows(tokens).astype(F32)
    _, inverse_one = norm_rows(own_input, norm_gain)
    input_norm_grad, norm_gain_grad = norm_back(own_input, inverse_one, norm_gain, normed_grad)


    up_rows = UP_ROWS
    kd_width = KD_COLUMNS
    rt_width = ROUTER_COLUMNS
    small = small_grads(
        latent_columns.reshape(rows, kd_width),
        lax.dynamic_slice_in_dim(logit_grad_all, t * rt_width, rt_width, 1),
        normed,
        mixed_in,
        norm_gain_grad,
        mix_gain_grad,
        kv_gain_grad,
        row_peak,
    )
    small = jnp.swapaxes(small.reshape(count, 6, 16, 128), 1, 2).reshape(count, 16, BIG)
    packed_grads = jnp.concatenate([big.reshape(count, 128, BIG), small], axis=1)
    home.append(send_home([after(piece, *normed_sent) for piece in parts[2]]))
    packed_grads = after(packed_grads, *home[2])
    packed_sent = packed_grads
    packed_grads = spread(packed_grads)
    small = jnp.swapaxes(packed_grads[:, 128:].reshape(count, 16, 6, 128), 1, 2)
    small = small.reshape(count, SMALL, 128)
    layer_give, layer_keep = combine_rows(
        place, pick_b, after(produced, packed_sent), shared_part
    )
    layer_half = layer_keep + swap(layer_give).astype(F32)
    layer_half, layer_sent = ring_parts(layer_half, x)
    layer_total = residual + sum_sent(layer_half, layer_sent, "x")
    home.append(send_home([after(piece, layer_total) for piece in parts[3]]))
    layer_out = gather_rows(layer_total.astype(BF))
    tokens_grad = gather_rows((mid_grad + input_norm_grad).astype(BF)).astype(F32)
    shared_sum = after(shared_grads, layer_total).astype(F32)
    shared_gate_grad = shared_sum[:, :SHARED]
    shared_up_grad = shared_sum[:, WIDE : WIDE + SHARED]
    shared_down_grad = shared_sum[:, 2 * WIDE : 2 * WIDE + SHARED].T
    big = jnp.sum(packed_grads[:, :128].astype(F32), axis=0)
    q_width = q_weight.shape[1]
    q_weight_grad = big[:, :q_width]
    out_weight_grad = big[:, q_width : q_width + ATT].T
    kv_up_grad = jnp.swapaxes(big[:, q_width + ATT :].reshape(4, up_rows, 128), 0, 1).reshape(
        up_rows, 4 * 128
    )

    small = small.astype(F32)
    wide = kd_width + rt_width
    small_sum = jnp.sum(small[:, : wide + 6], axis=0)
    peaks = small[:, wide + 6 : wide + 9, :heads]
    top_peak = jnp.max(peaks[:, 0] + peaks[:, 1] + peaks[:, 2], axis=0)
    vectors = small_sum[wide : wide + 6].reshape(3, 2, 128).sum(axis=1)
    vector_high, vector_low = split_two(vectors)
    shared_small = jnp.concatenate(
        [small_sum[:wide].astype(BF), vector_high, vector_low, jnp.zeros((10, 128), BF)], axis=0
    )
    all_small = lax.all_to_all(
        jnp.broadcast_to(after(shared_small, *home[3])[None], (8, wide + 16, 128)), TENSOR, split_axis=0,
        concat_axis=0, tiled=True,
    )
    expert_gate_grad, expert_up_grad, expert_down_grad = unpack(
        x, [after(home[0], shared_small), *home[1:]]
    )
    all_small = after(all_small, expert_gate_grad, tokens_grad)
    expert_gate_grad = jnp.swapaxes(expert_gate_grad, 1, 2)
    expert_up_grad = jnp.swapaxes(expert_up_grad, 1, 2)
    kv_down_grad = all_small[:, :kd_width].reshape(8 * kd_width, 128).T.astype(F32)
    router_grad = all_small[:, kd_width:wide].reshape(8 * rt_width, 128).T.astype(F32)
    vectors = jnp.sum(all_small[:, wide : wide + 6].astype(F32), axis=0).reshape(2, 3, 128).sum(axis=0)
    norm_gain_grad = vectors[0]
    mix_gain_grad = vectors[1]
    kv_gain_grad = vectors[2, : KVRANK // count]

    factor = jnp.minimum(1.0, threshold[0] / jnp.maximum(top_peak, 1.0))
    root_factor = jnp.sqrt(factor)
    q_rows = q_weight.shape[0] // count
    own_query = lax.dynamic_slice_in_dim(q_weight, j * q_rows, q_rows, 0).astype(F32)
    query_step = (own_query - step_size[0] * q_weight_grad).reshape(q_rows, heads, NOPE + ROPE)
    q_weight_new = jnp.concatenate(
        [
            query_step[..., :NOPE] * root_factor[None, :, None],
            query_step[..., NOPE:] * factor[None, :, None],
        ],
        axis=-1,
    ).reshape(q_rows, heads * (NOPE + ROPE))
    own_up = lax.dynamic_slice_in_dim(kv_up, j * up_rows, up_rows, 0).astype(F32)
    up_step = (own_up - step_size[0] * kv_up_grad).reshape(up_rows, heads, NOPE + VDIM)
    kv_up_new = jnp.concatenate(
        [up_step[..., :NOPE] * root_factor[None, :, None], up_step[..., NOPE:]], axis=-1
    ).reshape(up_rows, heads * (NOPE + VDIM))
    return (
        layer_out,
        tokens_grad,
        q_weight_grad,
        kv_down_grad,
        kv_up_grad,
        out_weight_grad,
        router_grad,
        norm_gain_grad,
        kv_gain_grad,
        mix_gain_grad,
        shared_gate_grad,
        shared_up_grad,
        shared_down_grad,
        expert_gate_grad,
        expert_up_grad,
        expert_down_grad,
        q_weight_new,
        kv_up_new,
    )


def solution(mesh):
    fine = Mesh(mesh.devices.reshape(4, 4, 4, 2), ("z", "y", "x", "c"))
    return jax.shard_map(
        shards,
        mesh=fine,
        in_specs=(
            P(EXPERT, None),
            P(EXPERT, None),
            P(EXPERT, None),
            P(),
            P(),
            P(None, TENSOR),
            P(),
            P(),
            P(None, TENSOR),
            P(TENSOR, None),
            P(),
            P(),
            P(None, TENSOR),
            P(None, TENSOR),
            P(TENSOR, None),
            P(EXPERT, None, TENSOR),
            P(EXPERT, None, TENSOR),
            P(EXPERT, TENSOR, None),
            P(),
            P(),
        ),
        out_specs=(
            P(EXPERT, None),
            P(EXPERT, None),
            P(EXPERT, TENSOR),
            P(EXPERT, None),
            P(EXPERT, TENSOR),
            P(TENSOR, EXPERT),
            P(EXPERT, None),
            P(EXPERT),
            P(EXPERT),
            P(EXPERT),
            P(EXPERT, TENSOR),
            P(EXPERT, TENSOR),
            P(TENSOR, EXPERT),
            P(EXPERT, None, TENSOR),
            P(EXPERT, None, TENSOR),
            P(EXPERT, TENSOR, None),
            P(EXPERT, TENSOR),
            P(EXPERT, TENSOR),
        ),
        check_vma=False,
    )
```
